256 devices in a mesh: slab: 64 (over y, z, core), trans: 4 (over x).
Axes of the slice: x: 4, y: 4, z: 8, core: 2. Of those that a mesh axis runs over, the one named last changes fastest.
Arguments:
- start_block: float32 [32, 3, 128, 32, 128], P(None, None, 'slab', 'trans'), may hold values from -2500 to 2500
- material: int32 [128, 32, 128], P('slab', 'trans'), may hold values from 0 to 3
- pml_mask: int32 [128, 32, 128], P('slab', 'trans'), may hold values 0 or 1
- eps_table: float32 [4], replicated, may hold values from 1.5 to 12
Outputs:
- new_blocks: float32 [2, 32, 3, 128, 32, 128], P(None, None, None, 'slab', 'trans')
- couplings: float32 [2, 2, 32, 32], replicated
The draws below stay inside these ranges and needn't reach their ends.
All inputs are finite; a program needn't handle non-finite values. No bound on the sum of `pml_mask` on one device may be relied on, other than what follows from the above.
Results may differ from the reference program's by a relative error of at most 0.0003.
Values sent between devices are 32-bit elements; how exact they have to be, the bound alone decides.
No kernel may reach another device: no remote copies, remote signals or barrier semaphores. Data moves between devices by JAX's collectives and lax.ppermute only.
A program may use at most 64 MiB of HBM per device.

```python
import math
import jax
import jax.numpy as jnp
from jax import lax

B = 32
CLASSES = 4
STEPS = 2
NY = 128
NZ = 128
NX = 32


def draw_start_block(key, part):
    key = jax.random.fold_in(key, 11)
    key_noise, key_column, key_cell = jax.random.split(key, 3)
    full_shape = (B, 3, NZ, NX, NY)
    position = jnp.arange(NZ, dtype=jnp.float32) / max(NZ - 1, 1)
    profile = (3.0 ** position)[:, None, None]
    column_scale = jnp.exp(jax.random.uniform(key_column, (B, 1, 1, 1, 1), jnp.float32) * math.log(10.0))
    noise = jnp.clip(jax.random.normal(key_noise, full_shape, jnp.float32), -6.0, 6.0)
    cell_scale = jnp.exp(jax.random.uniform(key_cell, (1, 1, NZ, NX, NY), jnp.float32) * math.log(10.0))
    return (noise * cell_scale * column_scale * profile).astype(jnp.float32)


def place_ends(drawn, stream_key, smallest, largest):
    shape = drawn.shape
    place = [jax.random.randint(jax.random.fold_in(stream_key, axis), (), 0, shape[axis]) for axis in range(len(shape))]
    drawn = drawn.at[tuple(place)].set(smallest)
    longest = shape.index(max(shape))
    place[longest] = (place[longest] + 1) % shape[longest]
    return drawn.at[tuple(place)].set(largest)


def setup_inputs(seed: int = 0) -> dict:
    keys = jax.random.split(jax.random.key(seed), 5)
    return {
        "start_block": draw_start_block(jax.random.fold_in(keys[4], 71), 0),
        "material": place_ends(jax.random.randint(keys[1], (NZ, NX, NY), 0, CLASSES), jax.random.fold_in(keys[1], 1), 0, CLASSES - 1).astype(jnp.int32),
        "pml_mask": place_ends((jax.random.randint(keys[2], (NZ, NX, NY), 0, 4) < 1).astype(jnp.int32), jax.random.fold_in(keys[2], 1), 0, 1),
        "eps_table": jnp.clip(jnp.exp(jax.random.uniform(keys[3], (CLASSES,), jnp.float32, math.log(1.5), math.log(12.0))), 1.5, 12.0),
    }


PRECISE = lax.Precision.HIGHEST
SHIFT_SQUARED = 1.0
ABSORB = 4.0

def forward(values, direction):
    first = values.ndim - 3
    length = values.shape[direction]
    difference = lax.slice_in_dim(values, 1, length, axis=direction) - lax.slice_in_dim(values, 0, length - 1, axis=direction)
    for spatial in range(first, first + 3):
        if spatial != direction:
            difference = lax.slice_in_dim(difference, 0, difference.shape[spatial] - 1, axis=spatial)
    return difference

def backward(values, direction):
    first = values.ndim - 3
    length = values.shape[direction]
    difference = lax.slice_in_dim(values, 1, length, axis=direction) - lax.slice_in_dim(values, 0, length - 1, axis=direction)
    for spatial in range(first, first + 3):
        if spatial != direction:
            difference = lax.slice_in_dim(difference, 1, difference.shape[spatial], axis=spatial)
    return difference

def curl_curl(padded):
    first = padded.ndim - 4
    widths = [(0, 0)] * (padded.ndim - 1) + [(1, 1)]
    padded = jnp.pad(padded, widths)
    field_x = lax.index_in_dim(padded, 0, axis=first, keepdims=False)
    field_y = lax.index_in_dim(padded, 1, axis=first, keepdims=False)
    field_z = lax.index_in_dim(padded, 2, axis=first, keepdims=False)
    axis_z, axis_x, axis_y = (first, first + 1, first + 2)
    curl_x = forward(field_z, axis_y) - forward(field_y, axis_z)
    curl_y = forward(field_x, axis_z) - forward(field_z, axis_x)
    curl_z = forward(field_y, axis_x) - forward(field_x, axis_y)
    result_x = backward(curl_z, axis_y) - backward(curl_y, axis_z)
    result_y = backward(curl_x, axis_z) - backward(curl_z, axis_x)
    result_z = backward(curl_y, axis_x) - backward(curl_x, axis_y)
    return jnp.stack([result_x, result_y, result_z], axis=first)

def coefficient(material, pml_mask, eps_table):
    permittivity = jnp.zeros(material.shape, eps_table.dtype)
    for level in range(eps_table.shape[0]):
        permittivity = permittivity + jnp.where(material == level, eps_table[level], 0.0)
    return SHIFT_SQUARED * permittivity + ABSORB * pml_mask.astype(eps_table.dtype)

def apply_single(vector, diagonal):
    padded = jnp.pad(vector, ((0, 0), (1, 1), (1, 1), (0, 0)))
    return curl_curl(padded) + diagonal * vector

def mean_inner(left, right, entries):
    return jnp.einsum('bczxy,dczxy->bd', left, right, precision=PRECISE) / entries

def orthonormal(block, gram_matrix):
    factor_low = jnp.linalg.cholesky(gram_matrix)
    identity = jnp.eye(gram_matrix.shape[0], dtype=gram_matrix.dtype)
    inverse = lax.linalg.triangular_solve(factor_low, identity, left_side=True, lower=True)
    return (jnp.einsum('bd,dczxy->bczxy', inverse, block, precision=PRECISE), factor_low)

def reference(start_block, material, pml_mask, eps_table):
    entries = float(3 * NZ * NX * NY)
    diagonal = coefficient(material, pml_mask, eps_table)
    basis_block, unused = orthonormal(start_block, mean_inner(start_block, start_block, entries))
    blocks = [basis_block]
    couplings = []
    for iteration in range(STEPS):
        applied = lax.map(lambda vector: apply_single(vector, diagonal), blocks[-1])
        projections = [mean_inner(earlier, applied, entries) for earlier in blocks]
        for earlier, weights in zip(blocks, projections):
            applied = applied - jnp.einsum('bd,bczxy->dczxy', weights, earlier, precision=PRECISE)
        basis_block, factor_low = orthonormal(applied, mean_inner(applied, applied, entries))
        couplings.append(jnp.stack([projections[-1], factor_low.T]))
        blocks.append(basis_block)
    return (jnp.stack(blocks[1:]), jnp.stack(couplings))
```

```python
import functools

import jax
import jax.numpy as jnp
from jax import lax
from jax.experimental import pallas as pl
from jax.experimental.pallas import tpu as pltpu
from jax.sharding import PartitionSpec as P

AXES = ("slab", "trans")
ABSORB = 4.0
CURL_CENTRE = 5.0
VMEM_LIMIT = 40 * 1024 * 1024


def call(body, out_shape, operands, smem=(), flops=0):
    specs = [
        pl.BlockSpec(memory_space=pltpu.SMEM if i in smem else pltpu.VMEM)
        for i in range(len(operands))
    ]
    outs = [pl.BlockSpec(memory_space=pltpu.VMEM) for _ in out_shape]
    moved = sum(4 * a.size for a in operands) + sum(
        4 * functools.reduce(lambda p, q: p * q, s.shape) for s in out_shape
    )
    return pl.pallas_call(
        body,
        out_shape=out_shape,
        in_specs=specs,
        out_specs=outs,
        compiler_params=pltpu.CompilerParams(vmem_limit_bytes=VMEM_LIMIT),
        cost_estimate=pl.CostEstimate(flops=flops, bytes_accessed=moved, transcendentals=0),
    )(*operands)


def shape(*dims):
    return jax.ShapeDtypeStruct(dims, jnp.float32)


def edge_shapes(zs, xs, width, ny):
    return [
        shape(3, xs, width, ny),
        shape(2, xs, width, ny),
        shape(zs, 3, width, ny),
        shape(zs, 2, width, ny),
        shape(width, ny),
        shape(width, ny),
    ]


def store_edges(edges, zs, xs, z, c, x, value):
    up_z, down_z, up_x, down_x, corner_up, corner_down = edges
    if z == zs - 1:
        up_z[c, x] = value
    if z == 0 and c < 2:
        down_z[c, x] = value
    if x == xs - 1:
        up_x[z, c] = value
    if x == 0 and c > 0:
        down_x[z, c - 1] = value
    if z == zs - 1 and x == 0 and c == 2:
        corner_up[...] = value
    if z == 0 and x == xs - 1 and c == 0:
        corner_down[...] = value


def split_body(zs, xs, width, start, field, *edges):
    rows = 3 * zs * xs
    for z in range(zs):
        for c in range(3):
            for x in range(xs):
                value = start[pl.ds((c * zs + z) * xs + x, width, stride=rows), :]
                field[z, c, x] = value
                store_edges(edges, zs, xs, z, c, x, value)


def apply_field(zs, xs, field, halo, diagonal, lane, last, put):
    before_z, after_z, before_x, after_x, corner_up, corner_down = halo

    def e(c, z, x):
        if z == -1:
            return corner_up[...] if x == xs else before_z[c, x]
        if z == zs:
            return corner_down[...] if x == -1 else after_z[c, x]
        if x == -1:
            return before_x[z, c]
        if x == xs:
            return after_x[z, c - 1]
        return field[z, c, x]

    def step_y(value):
        return jnp.where(lane == last, 0.0, pltpu.roll(value, last, 1)) - value

    def curl_x(z, x):
        return step_y(e(2, z, x)) - (e(1, z + 1, x) - e(1, z, x))

    def curl_y(z, x):
        return (e(0, z + 1, x) - e(0, z, x)) - (e(2, z, x + 1) - e(2, z, x))

    def curl_z(z, x):
        return (e(1, z, x + 1) - e(1, z, x)) - step_y(e(0, z, x))

    old_y = {z: curl_y(z, -1) for z in range(zs)}
    old_z = {z: curl_z(z, -1) for z in range(zs)}
    for x in range(xs):
        below_x, below_y = curl_x(-1, x), curl_y(-1, x)
        for z in range(zs):
            h_x, h_y, h_z = curl_x(z, x), curl_y(z, x), curl_z(z, x)
            e_x, e_y, e_z = e(0, z, x), e(1, z, x), e(2, z, x)
            d = diagonal(z, x)
            prev_z = jnp.where(lane == 0, -e_x, pltpu.roll(h_z, 1, 1))
            prev_x = jnp.where(lane == 0, e_z, pltpu.roll(h_x, 1, 1))
            put(z, 0, x, (h_z - prev_z) - (h_y - below_y) + d * e_x)
            put(z, 1, x, (h_x - below_x) - (h_z - old_z[z]) + d * e_y)
            put(z, 2, x, (h_y - old_y[z]) - (h_x - prev_x) + d * e_z)
            below_x, below_y = h_x, h_y
            old_y[z], old_z[z] = h_y, h_z


def lanes(width, ny):
    return lax.broadcasted_iota(jnp.int32, (width, ny), 1)


def first_body(zs, xs, width, ny, classes, *refs):
    eps, material, mask, field = refs[:4]
    halo, result, diag, edges = refs[4:10], refs[10], refs[11], refs[12:]
    total = eps[0]
    for level in range(1, classes):
        total = total + eps[level]
    shift = total / classes + CURL_CENTRE
    value = jnp.zeros(material.shape, jnp.float32)
    for level in range(classes):
        value = value + jnp.where(material[...] == level, eps[level], 0.0)
    diag[...] = value + ABSORB * mask[...].astype(jnp.float32) - shift

    def put(z, c, x, cell):
        result[z, c, x] = cell
        store_edges(edges, zs, xs, z, c, x, cell)

    apply_field(
        zs, xs, field, halo, lambda z, x: diag[z, x : x + 1, :], lanes(width, ny), ny - 1, put
    )


def parts3(value):
    high = value.astype(jnp.bfloat16)
    rest = value - high.astype(jnp.float32)
    middle = rest.astype(jnp.bfloat16)
    low = (rest - middle.astype(jnp.float32)).astype(jnp.bfloat16)
    return [high, middle, low]


def pair(ref, z, c, x):
    return jnp.concatenate([ref[z, c, x], ref[z, c, x + 1]], axis=1)


def product(left, right):
    return lax.dot_general(
        left, right, (((1,), (1,)), ((), ())), preferred_element_type=jnp.float32
    )


def fold(total, width, left, right):
    rows = sum(total[i * left * width : (i + 1) * left * width] for i in range(3))
    return sum(rows[:, i * right * width : (i + 1) * right * width] for i in range(3))


def early_gram_body(zs, xs, width, s0, s1, out):
    total = None
    for z in range(zs):
        for c in range(3):
            for x in range(0, xs, 2):
                both = jnp.concatenate([pair(s0, z, c, x), pair(s1, z, c, x)], axis=0)
                stack = jnp.concatenate(parts3(both), axis=0)
                term = product(stack, stack)
                total = term if total is None else total + term
    gram = fold(total, width, 2, 2)
    out[0] = gram[:width, :width]
    out[1] = gram[:width, width:]
    out[2] = gram[width:, width:]


def second_body(zs, xs, width, ny, *refs):
    diag, s1, halo, s2, out = refs[0], refs[1], refs[2:8], refs[8], refs[9]

    def put(z, c, x, cell):
        s2[z, c, x] = cell

    apply_field(
        zs, xs, s1, halo, lambda z, x: diag[z, x : x + 1, :], lanes(width, ny), ny - 1, put
    )
    total = None
    for z in range(zs):
        for c in range(3):
            for x in range(0, xs, 2):
                one, two = parts3(pair(s1, z, c, x)), parts3(pair(s2, z, c, x))
                stack = jnp.concatenate(
                    [jnp.concatenate([p, q], axis=0) for p, q in zip(one, two)], axis=0
                )
                term = product(stack, jnp.concatenate(two, axis=0))
                total = term if total is None else total + term
    gram = fold(total, width, 2, 1)
    out[0] = gram[:width]
    out[1] = gram[width:]


def precise(left, right, contract):
    return lax.dot_general(
        left,
        right,
        (((1,), (contract,)), ((), ())),
        precision=lax.Precision.HIGHEST,
        preferred_element_type=jnp.float32,
    )


def factor(gram, size):
    tiles = size // 8
    row8 = lax.broadcasted_iota(jnp.int32, (8, 1), 0)
    lane = lax.broadcasted_iota(jnp.int32, (8, size), 1)
    sub = lax.broadcasted_iota(jnp.int32, (8, size), 0)
    upper = [gram[8 * t : 8 * t + 8, :] for t in range(tiles)]
    inverse = [jnp.where(lane == sub + 8 * t, 1.0, 0.0) for t in range(tiles)]
    scales = []
    for t in range(tiles):
        cols = {
            u: [
                jnp.broadcast_to(upper[u][:, 8 * t + j : 8 * t + j + 1], (8, size))
                for j in range(8)
            ]
            for u in range(t, tiles)
        }
        pivots = jnp.zeros((8, size), jnp.float32)
        for s in range(8):
            pivot = jnp.broadcast_to(cols[t][s][s : s + 1, :], (8, size))
            pivots = jnp.where(sub == s, pivot, pivots)
            reciprocal = 1.0 / pivot
            heads = [cols[t][j][s : s + 1, :] for j in range(8)]
            row_u, row_i = upper[t][s : s + 1, :], inverse[t][s : s + 1, :]
            for u in range(t, tiles):
                f = cols[u][s] * reciprocal
                if u == t:
                    f = jnp.where(sub > s, f, 0.0)
                for j in range(s + 1, 8):
                    cols[u][j] = cols[u][j] - f * heads[j]
                upper[u] = upper[u] - f * row_u
                inverse[u] = inverse[u] - f * row_i
        scales.append(lax.rsqrt(pivots))
    upper = [a * s for a, s in zip(upper, scales)]
    inverse = [a * s for a, s in zip(inverse, scales)]
    return jnp.concatenate(upper, axis=0), jnp.concatenate(inverse, axis=0)


def last_body(zs, xs, width, ny, classes, entries, eps, moments, s0, s1, s2, out, couplings):
    total = eps[0]
    for level in range(1, classes):
        total = total + eps[level]
    shift = total / classes + CURL_CENTRE
    m = [moments[k] * (1.0 / entries) for k in range(5)]
    m = [0.5 * (a + a.T) for a in m]
    gram = jnp.concatenate(
        [jnp.concatenate([m[i + j] for j in range(3)], axis=1) for i in range(3)], axis=0
    )
    upper, inverse = factor(gram, 3 * width)
    w = width
    identity = jnp.where(
        lax.broadcasted_iota(jnp.int32, (w, w), 0) == lax.broadcasted_iota(jnp.int32, (w, w), 1),
        shift,
        0.0,
    )
    x0, x1 = inverse[:w, :w], inverse[w : 2 * w, w : 2 * w]
    u01, u11 = upper[:w, w : 2 * w], upper[w : 2 * w, w : 2 * w]
    u12, u22 = upper[w : 2 * w, 2 * w :], upper[2 * w :, 2 * w :]
    factor_one = precise(u11, x0, 1)
    couplings[0, 0] = precise(u01, x0, 1) + identity
    couplings[0, 1] = factor_one
    couplings[1, 0] = precise(u12 - precise(factor_one, u01, 0), x1, 1) + identity
    couplings[1, 1] = precise(u22, x1, 1)
    mix = inverse[w:]
    rows = 3 * zs * xs
    for z in range(zs):
        for c in range(3):
            for x in range(0, xs, 2):
                basis = jnp.concatenate([pair(s, z, c, x) for s in (s0, s1, s2)], axis=0)
                value = precise(mix, basis, 0)
                for k in range(2):
                    out[pl.ds((c * zs + z) * xs + x + k, 2 * w, stride=rows), :] = value[
                        :, k * ny : (k + 1) * ny
                    ]


def exchange(edges, slabs, trans):
    up_z, down_z, up_x, down_x, corner_up, corner_down = edges

    def moved(value, dz, dx):
        pairs = [
            (i * trans + j, (i + dz) * trans + j + dx)
            for i in range(slabs)
            for j in range(trans)
            if 0 <= i + dz < slabs and 0 <= j + dx < trans
        ]
        return lax.ppermute(value, AXES, pairs)

    return [
        moved(up_z, 1, 0),
        moved(down_z, -1, 0),
        moved(up_x, 0, 1),
        moved(down_x, 0, -1),
        moved(corner_up, 1, -1),
        moved(corner_down, -1, 1),
    ]


def total_sum(value, slabs, trans):
    devices = slabs * trans
    bits = devices.bit_length() - 1
    if bits == 8:
        groups = [(0, 1), (6, 7), (2, 3), (4, 5)]
    else:
        groups = [(b,) for b in range(bits)]
    for group in groups:
        masks = [0]
        for b in group:
            masks += [m ^ (1 << b) for m in masks]
        got = [
            lax.ppermute(value, AXES, [(i, i ^ m) for i in range(devices)]) for m in masks[1:]
        ]
        for other in got:
            value = value + other
    return value


def per_device(slabs, trans, start_block, material, pml_mask, eps_table):
    width, _, zs, xs, ny = start_block.shape
    classes = eps_table.shape[0]
    entries = float(3 * zs * xs * ny * slabs * trans)
    field = shape(zs, 3, xs, width, ny)
    edges = edge_shapes(zs, xs, width, ny)
    rows = width * 3 * zs * xs

    s0, *e0 = call(
        functools.partial(split_body, zs, xs, width),
        [field] + edges,
        [start_block.reshape(rows, ny)],
    )
    h0 = exchange(e0, slabs, trans)
    s1, diag, *e1 = call(
        functools.partial(first_body, zs, xs, width, ny, classes),
        [field, shape(zs, xs, ny)] + edges,
        [eps_table, material, pml_mask, s0] + h0,
        smem=(0,),
    )
    h1 = exchange(e1, slabs, trans)
    (early,) = call(
        functools.partial(early_gram_body, zs, xs, width), [shape(3, width, width)], [s0, s1]
    )
    s2, late = call(
        functools.partial(second_body, zs, xs, width, ny),
        [field, shape(2, width, width)],
        [diag, s1] + h1,
    )
    moments = jnp.concatenate([early, late], axis=0)
    moments = total_sum(moments.reshape(-1, 128), slabs, trans).reshape(5, width, width)
    blocks, couplings = call(
        functools.partial(last_body, zs, xs, width, ny, classes, entries),
        [shape(2 * rows, ny), shape(2, 2, width, width)],
        [eps_table, moments, s0, s1, s2],
        smem=(0,),
    )
    return blocks.reshape(2, width, 3, zs, xs, ny), couplings


def solution(mesh):
    sizes = dict(zip(mesh.axis_names, mesh.devices.shape))
    return jax.shard_map(
        functools.partial(per_device, sizes["slab"], sizes["trans"]),
        mesh=mesh,
        in_specs=(
            P(None, None, "slab", "trans", None),
            P("slab", "trans", None),
            P("slab", "trans", None),
            P(),
        ),
        out_specs=(P(None, None, None, "slab", "trans", None), P()),
        check_vma=False,
    )
```

```python
import functools

import jax
import jax.numpy as jnp
from jax import lax
from jax.experimental import pallas as pl
from jax.experimental.pallas import tpu as pltpu
from jax.sharding import PartitionSpec as P

AXES = ("slab", "trans")
ABSORB = 4.0
CURL_CENTRE = 5.0
VMEM_LIMIT = 40 * 1024 * 1024


def call(body, out_shape, operands, smem=(), scratch=()):
    specs = [
        pl.BlockSpec(memory_space=pltpu.SMEM if i in smem else pltpu.VMEM)
        for i in range(len(operands))
    ]
    outs = [pl.BlockSpec(memory_space=pltpu.VMEM) for _ in out_shape]
    return pl.pallas_call(
        body,
        out_shape=out_shape,
        in_specs=specs,
        out_specs=outs,
        scratch_shapes=list(scratch),
        compiler_params=pltpu.CompilerParams(vmem_limit_bytes=VMEM_LIMIT),
    )(*operands)


def shape(*dims):
    return jax.ShapeDtypeStruct(dims, jnp.float32)


class Halo:
    def __init__(self, zs, xs):
        self.zs, self.xs = zs, xs
        self.first = set()
        for c in range(3):
            for z in range(zs):
                for x in range(xs):
                    self.first.add((c, z, x))
                    self.first |= reach(c, z, x)
        cells = set(self.first)
        for cell in self.first:
            cells |= reach(*cell)
        self.blocks, self.diagonal = {}, {}
        self.sides = sorted({self.side(z, x) for _, z, x in cells} - {(0, 0)}, key=side_order)
        for side in self.sides:
            self.blocks[side] = sorted(q for q in cells if self.side(q[1], q[2]) == side)
            near = {q[1:] for q in self.first if self.side(q[1], q[2]) == side}
            self.diagonal[side] = sorted(near)

    def side(self, z, x):
        return (
            -1 if z < 0 else int(z >= self.zs),
            -1 if x < 0 else int(x >= self.xs),
        )

    def own(self, side, z, x):
        return z - side[0] * self.zs, x - side[1] * self.xs

    def rows(self, side, width):
        return len(self.blocks[side]) * width + (8 if self.diagonal[side] else 0)


def side_order(side):
    return (abs(side[0]) + abs(side[1]), -abs(side[0]), side)


CURL = (
    lambda z, x: {(2, z, x), (1, z + 1, x), (1, z, x)},
    lambda z, x: {(0, z + 1, x), (0, z, x), (2, z, x + 1), (2, z, x)},
    lambda z, x: {(1, z, x + 1), (1, z, x), (0, z, x)},
)
BACK = (
    lambda z, x: {(2, z, x), (1, z, x), (1, z - 1, x)},
    lambda z, x: {(0, z, x), (0, z - 1, x), (2, z, x), (2, z, x - 1)},
    lambda z, x: {(1, z, x), (1, z, x - 1), (0, z, x)},
)


def reach(c, z, x):
    cells = {(c, z, x)}
    for k, hz, hx in BACK[c](z, x):
        cells |= CURL[k](hz, hx)
    return cells


def stencil(e, lane, last):
    known = {}

    def step_y(value):
        return jnp.where(lane == last, 0.0, pltpu.roll(value, last, 1)) - value

    def h(k, z, x):
        if (k, z, x) not in known:
            if k == 0:
                value = step_y(e(2, z, x)) - (e(1, z + 1, x) - e(1, z, x))
            elif k == 1:
                value = (e(0, z + 1, x) - e(0, z, x)) - (e(2, z, x + 1) - e(2, z, x))
            else:
                value = (e(1, z, x + 1) - e(1, z, x)) - step_y(e(0, z, x))
            known[k, z, x] = value
        return known[k, z, x]

    def result(c, z, x):
        if c == 0:
            here = h(2, z, x)
            before = jnp.where(lane == 0, -e(0, z, x), pltpu.roll(here, 1, 1))
            return (here - before) - (h(1, z, x) - h(1, z - 1, x))
        if c == 1:
            return (h(0, z, x) - h(0, z - 1, x)) - (h(2, z, x) - h(2, z, x - 1))
        here = h(0, z, x)
        before = jnp.where(lane == 0, e(2, z, x), pltpu.roll(here, 1, 1))
        return (h(1, z, x) - h(1, z, x - 1)) - (here - before)

    return result


def split_body(halo, width, classes, eps, material, mask, start, field, diag, *messages):
    zs, xs = halo.zs, halo.xs
    rows = 3 * zs * xs
    total = eps[0]
    for level in range(1, classes):
        total = total + eps[level]
    shift = total / classes + CURL_CENTRE
    value = jnp.zeros(material.shape, jnp.float32)
    for level in range(classes):
        value = value + jnp.where(material[...] == level, eps[level], 0.0)
    diag[...] = value + ABSORB * mask[...].astype(jnp.float32) - shift

    places = {}
    for side, message in zip(halo.sides, messages):
        for i, (c, z, x) in enumerate(halo.blocks[side]):
            places.setdefault((c, *halo.own(side, z, x)), []).append((message, i))
        base = len(halo.blocks[side]) * width
        if halo.diagonal[side]:
            message[base : base + 8, :] = jnp.zeros((8, message.shape[1]), jnp.float32)
        for i, (z, x) in enumerate(halo.diagonal[side]):
            oz, ox = halo.own(side, z, x)
            message[base + i : base + i + 1, :] = diag[oz, ox : ox + 1, :]
    for z in range(zs):
        for c in range(3):
            for x in range(xs):
                cell = start[pl.ds((c * zs + z) * xs + x, width, stride=rows), :]
                field[z, c, x] = cell
                for message, i in places.get((c, z, x), ()):
                    message[i * width : (i + 1) * width, :] = cell


def parts(value, count):
    found, rest = [], value
    for i in range(count):
        found.append(rest.astype(jnp.bfloat16))
        if i + 1 < count:
            rest = rest - found[-1].astype(jnp.float32)
    return found


def pair(ref, z, c, x):
    return jnp.concatenate([ref[z, c, x], ref[z, c, x + 1]], axis=1)


def product(left, right, contract):
    return lax.dot_general(
        left, right, (((1,), (contract,)), ((), ())), preferred_element_type=jnp.float32
    )


def fold(total, left, right):
    rows = total[:left] + total[left : 2 * left] + total[2 * left :]
    return rows[:, :right] + rows[:, right : 2 * right] + rows[:, 2 * right :]


def start_gram_body(zs, xs, s0, out):
    total = None
    for z in range(zs):
        for c in range(3):
            for x in range(0, xs, 2):
                stack = jnp.concatenate(parts(pair(s0, z, c, x), 3), axis=0)
                term = product(stack, stack, 1)
                total = term if total is None else total + term
    out[...] = fold(total, *out.shape)


def apply_body(halo, width, ny, slabs, trans, s0, diag, gram, *refs):
    zs, xs = halo.zs, halo.xs
    count = len(halo.sides)
    messages = dict(zip(halo.sides, refs[:count]))
    s1, s2, moments, outer = refs[count:]
    slab, across = lax.axis_index("slab"), lax.axis_index("trans")
    inside = {
        (-1, 0): slab > 0,
        (1, 0): slab < slabs - 1,
        (0, -1): across > 0,
        (0, 1): across < trans - 1,
    }
    inside = {side: jnp.where(held, 1.0, 0.0) for side, held in inside.items()}
    for side in halo.sides:
        if side not in inside:
            inside[side] = inside[side[0], 0] * inside[0, side[1]]
    block = {s: {q: i for i, q in enumerate(halo.blocks[s])} for s in halo.sides}
    extra = sorted(q for q in halo.first if halo.side(q[1], q[2]) != (0, 0))
    extra = {q: i for i, q in enumerate(extra)}
    lane = lax.broadcasted_iota(jnp.int32, (8, ny), 1)

    def diagonal(z, x):
        side = halo.side(z, x)
        if side == (0, 0):
            return diag[z, x : x + 1, :]
        row = len(halo.blocks[side]) * width + halo.diagonal[side].index((z, x))
        return messages[side][row : row + 1, :]

    def group(g, carry):
        at = pl.multiple_of(g * 8, 8)

        def start(c, z, x):
            side = halo.side(z, x)
            if side == (0, 0):
                return s0[z, c, x, pl.ds(at, 8), :]
            place = block[side][c, z, x] * width
            return messages[side][pl.ds(place + at, 8), :] * inside[side]

        def once(c, z, x):
            if halo.side(z, x) == (0, 0):
                return s1[z, c, x, pl.ds(at, 8), :]
            return outer[extra[c, z, x]]

        apply = stencil(start, lane, ny - 1)
        for x in range(-1, xs + 1):
            for z in range(-1, zs + 1):
                for c in range(3):
                    if (c, z, x) not in halo.first:
                        continue
                    value = apply(c, z, x) + diagonal(z, x) * start(c, z, x)
                    side = halo.side(z, x)
                    if side == (0, 0):
                        s1[z, c, x, pl.ds(at, 8), :] = value
                    else:
                        outer[extra[c, z, x]] = value * inside[side]
        apply = stencil(once, lane, ny - 1)
        for x in range(xs):
            for z in range(zs):
                for c in range(3):
                    value = apply(c, z, x) + diagonal(z, x) * once(c, z, x)
                    s2[z, c, x, pl.ds(at, 8), :] = value
        return carry

    lax.fori_loop(0, width // 8, group, 0)

    total = None
    for z in range(zs):
        for c in range(3):
            for x in range(0, xs, 2):
                split = [parts(pair(s, z, c, x), 3) for s in (s0, s1, s2)]
                left = jnp.concatenate([p for i in range(3) for p in (s[i] for s in split)], axis=0)
                right = jnp.concatenate(
                    [p for i in range(3) for p in (s[i] for s in split[1:])], axis=0
                )
                term = product(left, right, 1)
                total = term if total is None else total + term
    found = fold(total, 3 * width, 2 * width)
    w = width
    found = [
        gram[...],
        found[:w, :w],
        found[w : 2 * w, :w],
        found[w : 2 * w, w:],
        found[2 * w :, w:],
    ]
    for k, m in enumerate(found):
        for j in range(w // 8):
            moments[8 * k : 8 * k + 8, w * j : w * j + w] = m[8 * j : 8 * j + 8]


def precise(left, right, contract):
    return lax.dot_general(
        left,
        right,
        (((1,), (contract,)), ((), ())),
        precision=lax.Precision.HIGHEST,
        preferred_element_type=jnp.float32,
    )


def factor(gram, size):
    tiles = size // 8
    lane = lax.broadcasted_iota(jnp.int32, (8, size), 1)
    sub = lax.broadcasted_iota(jnp.int32, (8, size), 0)
    upper = [gram[8 * t : 8 * t + 8, :] for t in range(tiles)]
    inverse = [jnp.where(lane == sub + 8 * t, 1.0, 0.0) for t in range(tiles)]
    scales = []
    for t in range(tiles):
        cols = {
            u: [
                jnp.broadcast_to(upper[u][:, 8 * t + j : 8 * t + j + 1], (8, size))
                for j in range(8)
            ]
            for u in range(t, tiles)
        }
        pivots = jnp.zeros((8, size), jnp.float32)
        for s in range(8):
            pivot = jnp.broadcast_to(cols[t][s][s : s + 1, :], (8, size))
            pivots = jnp.where(sub == s, pivot, pivots)
            reciprocal = 1.0 / pivot
            heads = [cols[t][j][s : s + 1, :] for j in range(8)]
            row_u, row_i = upper[t][s : s + 1, :], inverse[t][s : s + 1, :]
            for u in range(t, tiles):
                f = cols[u][s] * reciprocal
                if u == t:
                    f = jnp.where(sub > s, f, 0.0)
                for j in range(s + 1, 8):
                    cols[u][j] = cols[u][j] - f * heads[j]
                upper[u] = upper[u] - f * row_u
                inverse[u] = inverse[u] - f * row_i
        scales.append(lax.rsqrt(pivots))
    upper = [a * s for a, s in zip(upper, scales)]
    inverse = [a * s for a, s in zip(inverse, scales)]
    return jnp.concatenate(upper, axis=0), jnp.concatenate(inverse, axis=0)


def last_body(zs, xs, width, ny, classes, entries, eps, moments, s0, s1, s2, out, couplings):
    w = width
    total = eps[0]
    for level in range(1, classes):
        total = total + eps[level]
    shift = total / classes + CURL_CENTRE
    m = []
    for k in range(5):
        rows = moments[8 * k : 8 * k + 8, :] * (1.0 / entries)
        found = jnp.concatenate([rows[:, w * j : w * j + w] for j in range(w // 8)], axis=0)
        m.append(0.5 * (found + found.T))
    gram = jnp.concatenate(
        [jnp.concatenate([m[i + j] for j in range(3)], axis=1) for i in range(3)], axis=0
    )
    upper, inverse = factor(gram, 3 * width)
    mix = jnp.concatenate(
        [jnp.concatenate([p, p], axis=1) for p in parts(inverse[w:], 3)], axis=0
    )
    rows = 3 * zs * xs
    for z in range(zs):
        for c in range(3):
            for x in range(0, xs, 2):
                basis = jnp.concatenate([pair(s, z, c, x) for s in (s0, s1, s2)], axis=0)
                terms = product(mix, jnp.concatenate(parts(basis, 2), axis=0), 0)
                value = terms[: 2 * w] + terms[2 * w : 4 * w] + terms[4 * w :]
                for k in range(2):
                    out[pl.ds((c * zs + z) * xs + x + k, 2 * w, stride=rows), :] = value[
                        :, k * ny : (k + 1) * ny
                    ]
    identity = jnp.where(
        lax.broadcasted_iota(jnp.int32, (w, w), 0) == lax.broadcasted_iota(jnp.int32, (w, w), 1),
        shift,
        0.0,
    )
    x0, x1 = inverse[:w, :w], inverse[w : 2 * w, w : 2 * w]
    u01, u11 = upper[:w, w : 2 * w], upper[w : 2 * w, w : 2 * w]
    u12, u22 = upper[w : 2 * w, 2 * w :], upper[2 * w :, 2 * w :]
    factor_one = precise(u11, x0, 1)
    couplings[0, 0] = precise(u01, x0, 1) + identity
    couplings[0, 1] = factor_one
    couplings[1, 0] = precise(u12 - precise(factor_one, u01, 0), x1, 1) + identity
    couplings[1, 1] = precise(u22, x1, 1)


def exchange(halo, messages, slabs, trans):
    def moved(side, value):
        pairs = [
            (i * trans + j, (i - side[0]) % slabs * trans + (j - side[1]) % trans)
            for i in range(slabs)
            for j in range(trans)
        ]
        return lax.ppermute(value, AXES, pairs)

    return [moved(side, value) for side, value in zip(halo.sides, messages)]


def total_sum(value, slabs, trans):
    devices = slabs * trans
    groups = [(4, 1, 5), (3, 64, 67), (192, 8, 200), (24, 56, 32)]
    if devices != 256:
        groups = [(1 << b,) for b in range(devices.bit_length() - 1)]
    for group in groups:
        got = [lax.ppermute(value, AXES, [(i, i ^ m) for i in range(devices)]) for m in group]
        for other in got:
            value = value + other
    return value


def per_device(slabs, trans, start_block, material, pml_mask, eps_table):
    width, _, zs, xs, ny = start_block.shape
    classes = eps_table.shape[0]
    entries = float(3 * zs * xs * ny * slabs * trans)
    field = shape(zs, 3, xs, width, ny)
    rows = width * 3 * zs * xs
    halo = Halo(zs, xs)

    s0, diag, *messages = call(
        functools.partial(split_body, halo, width, classes),
        [field, shape(zs, xs, ny)] + [shape(halo.rows(s, width), ny) for s in halo.sides],
        [eps_table, material, pml_mask, start_block.reshape(rows, ny)],
        smem=(0,),
    )
    messages = exchange(halo, messages, slabs, trans)
    (gram,) = call(functools.partial(start_gram_body, zs, xs), [shape(width, width)], [s0])
    outside = len(halo.first) - 3 * zs * xs
    s1, s2, moments = call(
        functools.partial(apply_body, halo, width, ny, slabs, trans),
        [field, field, shape(40, 4 * width)],
        [s0, diag, gram] + messages,
        scratch=[pltpu.VMEM((outside, 8, ny), jnp.float32)],
    )
    moments = total_sum(moments, slabs, trans)
    blocks, couplings = call(
        functools.partial(last_body, zs, xs, width, ny, classes, entries),
        [shape(2 * rows, ny), shape(2, 2, width, width)],
        [eps_table, moments, s0, s1, s2],
        smem=(0,),
    )
    return blocks.reshape(2, width, 3, zs, xs, ny), couplings


def solution(mesh):
    sizes = dict(zip(mesh.axis_names, mesh.devices.shape))
    return jax.shard_map(
        functools.partial(per_device, sizes["slab"], sizes["trans"]),
        mesh=mesh,
        in_specs=(
            P(None, None, "slab", "trans", None),
            P("slab", "trans", None),
            P("slab", "trans", None),
            P(),
        ),
        out_specs=(P(None, None, None, "slab", "trans", None), P()),
        check_vma=False,
    )
```

```python
import functools

import jax
import jax.numpy as jnp
from jax import lax
from jax.experimental import pallas as pl
from jax.experimental.pallas import tpu as pltpu
from jax.sharding import PartitionSpec as P

AXES = ("y", "z", "core", "x")
ABSORB = 4.0
CURL_CENTRE = 5.0
VMEM_LIMIT = 40 * 1024 * 1024


def call(body, out_shape, operands, smem=(), hbm=(), hbm_out=(), scratch=()):
    special = {**{i: pltpu.SMEM for i in smem}, **{i: pltpu.HBM for i in hbm}}
    specs = [
        pl.BlockSpec(memory_space=special.get(i, pltpu.VMEM)) for i in range(len(operands))
    ]
    outs = [
        pl.BlockSpec(memory_space=pltpu.HBM if i in hbm_out else pltpu.VMEM)
        for i in range(len(out_shape))
    ]
    return pl.pallas_call(
        body,
        out_shape=out_shape,
        in_specs=specs,
        out_specs=outs,
        scratch_shapes=list(scratch),
        compiler_params=pltpu.CompilerParams(vmem_limit_bytes=VMEM_LIMIT),
    )(
        *(
            pltpu.with_memory_space_constraint(a, pltpu.HBM) if i in hbm else a
            for i, a in enumerate(operands)
        )
    )


def shape(*dims):
    return jax.ShapeDtypeStruct(dims, jnp.float32)


class Halo:
    def __init__(self, zs, xs):
        self.zs, self.xs = zs, xs
        self.first = set()
        for c in range(3):
            for z in range(zs):
                for x in range(xs):
                    self.first.add((c, z, x))
                    self.first |= reach(c, z, x)
        cells = set(self.first)
        for cell in self.first:
            cells |= reach(*cell)
        self.names = [(0, -1), (0, 1), (-1, 0), (1, 0), (-1, 2), (1, 2)]
        self.blocks, self.diagonal = {}, {}
        for name in self.names:
            self.blocks[name] = sorted(q for q in cells if self.name(q[1], q[2]) == name)
            near = {q[1:] for q in self.first if self.name(q[1], q[2]) == name}
            self.diagonal[name] = sorted(near)

    def name(self, z, x):
        side = self.side(z, x)
        return (side[0], 2) if side[0] and side[1] else side

    def side(self, z, x):
        return (
            -1 if z < 0 else int(z >= self.zs),
            -1 if x < 0 else int(x >= self.xs),
        )

    def own(self, name, z, x):
        return z - name[0] * self.zs, x - name[1] % 2 * name[1] * self.xs

    def rows(self, name, width):
        return len(self.blocks[name]) * width + 8

    def block_row(self, name, c, z, x, width):
        return self.blocks[name].index((c, z, x)) * width

    def diagonal_row(self, name, z, x, width):
        return len(self.blocks[name]) * width + self.diagonal[name].index((z, x))


CURL = (
    lambda z, x: {(2, z, x), (1, z + 1, x), (1, z, x)},
    lambda z, x: {(0, z + 1, x), (0, z, x), (2, z, x + 1), (2, z, x)},
    lambda z, x: {(1, z, x + 1), (1, z, x), (0, z, x)},
)
BACK = (
    lambda z, x: {(2, z, x), (1, z, x), (1, z - 1, x)},
    lambda z, x: {(0, z, x), (0, z - 1, x), (2, z, x), (2, z, x - 1)},
    lambda z, x: {(1, z, x), (1, z, x - 1), (0, z, x)},
)


def reach(c, z, x):
    cells = {(c, z, x)}
    for k, hz, hx in BACK[c](z, x):
        cells |= CURL[k](hz, hx)
    return cells


def stencil(e, lane, last):
    known = {}

    def step_y(value):
        return jnp.where(lane == last, 0.0, pltpu.roll(value, last, 1)) - value

    def h(k, z, x):
        if (k, z, x) not in known:
            if k == 0:
                value = step_y(e(2, z, x)) - (e(1, z + 1, x) - e(1, z, x))
            elif k == 1:
                value = (e(0, z + 1, x) - e(0, z, x)) - (e(2, z, x + 1) - e(2, z, x))
            else:
                value = (e(1, z, x + 1) - e(1, z, x)) - step_y(e(0, z, x))
            known[k, z, x] = value
        return known[k, z, x]

    def result(c, z, x):
        if c == 0:
            here = h(2, z, x)
            before = jnp.where(lane == 0, -e(0, z, x), pltpu.roll(here, 1, 1))
            return (here - before) - (h(1, z, x) - h(1, z - 1, x))
        if c == 1:
            return (h(0, z, x) - h(0, z - 1, x)) - (h(2, z, x) - h(2, z, x - 1))
        here = h(0, z, x)
        before = jnp.where(lane == 0, e(2, z, x), pltpu.roll(here, 1, 1))
        return (h(1, z, x) - h(1, z, x - 1)) - (here - before)

    return result


def split_body(halo, width, classes, eps, material, mask, start, field, diag, *refs):
    zs, xs = halo.zs, halo.xs
    rows = 3 * zs * xs
    messages, (start_in, material_in, mask_in, eps_in, sems) = refs[:4], refs[4:]
    copies = [
        pltpu.make_async_copy(source, target, sems.at[i])
        for i, (source, target) in enumerate(
            [(eps, eps_in), (material, material_in), (mask, mask_in), (start, start_in)]
        )
    ]
    for copy in copies:
        copy.start()
    for copy in copies[:3]:
        copy.wait()
    eps = eps_in
    total = eps[0]
    for level in range(1, classes):
        total = total + eps[level]
    shift = total / classes + CURL_CENTRE
    value = jnp.zeros(material_in.shape, jnp.float32)
    for level in range(classes):
        value = value + jnp.where(material_in[...] == level, eps[level], 0.0)
    diag[...] = value + ABSORB * mask_in[...].astype(jnp.float32) - shift

    places = {}
    for name, message in zip(halo.names, messages):
        for c, z, x in halo.blocks[name]:
            row = halo.block_row(name, c, z, x, width)
            places.setdefault((c, *halo.own(name, z, x)), []).append((message, row))
        base = len(halo.blocks[name]) * width
        message[base : base + 8, :] = jnp.zeros((8, message.shape[1]), jnp.float32)
        for z, x in halo.diagonal[name]:
            row = halo.diagonal_row(name, z, x, width)
            oz, ox = halo.own(name, z, x)
            message[row : row + 1, :] = diag[oz, ox : ox + 1, :]
    copies[3].wait()
    for z in range(zs):
        for c in range(3):
            for x in range(xs):
                cell = start_in[pl.ds((c * zs + z) * xs + x, width, stride=rows), :]
                field[z, c, x] = cell
                for message, row in places.get((c, z, x), ()):
                    message[row : row + width, :] = cell


def relay_body(halo, width, before, after, *passed):
    received = {-1: ((0, -1), before), 1: ((0, 1), after)}
    for name, message in zip(halo.names[4:], passed):
        base = len(halo.blocks[name]) * width
        message[base : base + 8, :] = jnp.zeros((8, message.shape[1]), jnp.float32)
        for c, z, x in halo.blocks[name]:
            side, source = received[halo.side(z, x)[1]]
            at = halo.block_row(side, c, z - name[0] * halo.zs, x, width)
            row = halo.block_row(name, c, z, x, width)
            message[row : row + width, :] = source[at : at + width, :]
        for z, x in halo.diagonal[name]:
            side, source = received[halo.side(z, x)[1]]
            at = halo.diagonal_row(side, z - name[0] * halo.zs, x, width)
            row = halo.diagonal_row(name, z, x, width)
            message[row : row + 1, :] = source[at : at + 1, :]


def parts(value, count):
    found, rest = [], value
    for i in range(count):
        found.append(rest.astype(jnp.bfloat16))
        if i + 1 < count:
            rest = rest - found[-1].astype(jnp.float32)
    return found


def pair(ref, z, c, x):
    return jnp.concatenate([ref[z, c, x], ref[z, c, x + 1]], axis=1)


def product(left, right, contract):
    return lax.dot_general(
        left, right, (((1,), (contract,)), ((), ())), preferred_element_type=jnp.float32
    )


def fold(total, left, right):
    rows = total[:left] + total[left : 2 * left] + total[2 * left :]
    return rows[:, :right] + rows[:, right : 2 * right] + rows[:, 2 * right :]


def start_gram_body(zs, xs, s0, out):
    total = None
    for z in range(zs):
        for c in range(3):
            for x in range(0, xs, 2):
                stack = jnp.concatenate(parts(pair(s0, z, c, x), 3), axis=0)
                term = product(stack, stack, 1)
                total = term if total is None else total + term
    out[...] = fold(total, *out.shape)


def apply_body(halo, width, ny, slabs, trans, s0, diag, gram, *refs):
    zs, xs = halo.zs, halo.xs
    messages = dict(zip(halo.names, refs[:6]))
    s1, s2, moments, outer = refs[6:]
    slab, across = lax.axis_index(AXES[:3]), lax.axis_index("x")
    held_z = {-1: slab > 0, 0: slab >= 0, 1: slab < slabs - 1}
    held_x = {-1: across > 0, 0: across >= 0, 1: across < trans - 1}
    inside = {
        (i, j): jnp.where(jnp.logical_and(held_z[i], held_x[j]), 1.0, 0.0)
        for i in (-1, 0, 1)
        for j in (-1, 0, 1)
    }
    extra = sorted(q for q in halo.first if halo.side(q[1], q[2]) != (0, 0))
    extra = {q: i for i, q in enumerate(extra)}
    lane = lax.broadcasted_iota(jnp.int32, (8, ny), 1)

    def diagonal(z, x):
        name = halo.name(z, x)
        if name == (0, 0):
            return diag[z, x : x + 1, :]
        row = halo.diagonal_row(name, z, x, width)
        return messages[name][row : row + 1, :]

    def group(g, carry):
        at = pl.multiple_of(g * 8, 8)

        def start(c, z, x):
            name = halo.name(z, x)
            if name == (0, 0):
                return s0[z, c, x, pl.ds(at, 8), :]
            row = halo.block_row(name, c, z, x, width)
            return messages[name][pl.ds(row + at, 8), :] * inside[halo.side(z, x)]

        def once(c, z, x):
            if halo.side(z, x) == (0, 0):
                return s1[z, c, x, pl.ds(at, 8), :]
            return outer[extra[c, z, x]]

        apply = stencil(start, lane, ny - 1)
        for x in range(-1, xs + 1):
            for z in range(-1, zs + 1):
                for c in range(3):
                    if (c, z, x) not in halo.first:
                        continue
                    value = apply(c, z, x) + diagonal(z, x) * start(c, z, x)
                    side = halo.side(z, x)
                    if side == (0, 0):
                        s1[z, c, x, pl.ds(at, 8), :] = value
                    else:
                        outer[extra[c, z, x]] = value * inside[side]
        apply = stencil(once, lane, ny - 1)
        for x in range(xs):
            for z in range(zs):
                for c in range(3):
                    value = apply(c, z, x) + diagonal(z, x) * once(c, z, x)
                    s2[z, c, x, pl.ds(at, 8), :] = value
        return carry

    lax.fori_loop(0, width // 8, group, 0)

    total = None
    for z in range(zs):
        for c in range(3):
            for x in range(0, xs, 2):
                split = [parts(pair(s, z, c, x), 3) for s in (s0, s1, s2)]
                left = jnp.concatenate([p for i in range(3) for p in (s[i] for s in split)], axis=0)
                right = jnp.concatenate(
                    [p for i in range(3) for p in (s[i] for s in split[1:])], axis=0
                )
                term = product(left, right, 1)
                total = term if total is None else total + term
    found = fold(total, 3 * width, 2 * width)
    w = width
    found = [
        gram[...],
        found[:w, :w],
        found[w : 2 * w, :w],
        found[w : 2 * w, w:],
        found[2 * w :, w:],
    ]
    for k, m in enumerate(found):
        for j in range(w // 8):
            moments[8 * k : 8 * k + 8, w * j : w * j + w] = m[8 * j : 8 * j + 8]


def precise(left, right, contract):
    return lax.dot_general(
        left,
        right,
        (((1,), (contract,)), ((), ())),
        precision=lax.Precision.HIGHEST,
        preferred_element_type=jnp.float32,
    )


def factor(gram, size):
    tiles = size // 8
    lane = lax.broadcasted_iota(jnp.int32, (8, size), 1)
    sub = lax.broadcasted_iota(jnp.int32, (8, size), 0)
    upper = [gram[8 * t : 8 * t + 8, :] for t in range(tiles)]
    inverse = [jnp.where(lane == sub + 8 * t, 1.0, 0.0) for t in range(tiles)]
    scales = []
    for t in range(tiles):
        cols = {
            u: [
                jnp.broadcast_to(upper[u][:, 8 * t + j : 8 * t + j + 1], (8, size))
                for j in range(8)
            ]
            for u in range(t, tiles)
        }
        pivots = jnp.zeros((8, size), jnp.float32)
        for s in range(8):
            pivot = jnp.broadcast_to(cols[t][s][s : s + 1, :], (8, size))
            pivots = jnp.where(sub == s, pivot, pivots)
            reciprocal = 1.0 / pivot
            heads = [cols[t][j][s : s + 1, :] for j in range(8)]
            row_u, row_i = upper[t][s : s + 1, :], inverse[t][s : s + 1, :]
            for u in range(t, tiles):
                f = cols[u][s] * reciprocal
                if u == t:
                    f = jnp.where(sub > s, f, 0.0)
                for j in range(s + 1, 8):
                    cols[u][j] = cols[u][j] - f * heads[j]
                upper[u] = upper[u] - f * row_u
                inverse[u] = inverse[u] - f * row_i
        scales.append(lax.rsqrt(pivots))
    upper = [a * s for a, s in zip(upper, scales)]
    inverse = [a * s for a, s in zip(inverse, scales)]
    return jnp.concatenate(upper, axis=0), jnp.concatenate(inverse, axis=0)


def last_body(zs, xs, width, ny, classes, entries, eps, moments, s0, s1, s2, out, couplings):
    w = width
    total = eps[0]
    for level in range(1, classes):
        total = total + eps[level]
    shift = total / classes + CURL_CENTRE
    m = []
    summed = moments[0]
    for i in range(1, moments.shape[0]):
        summed = summed + moments[i]
    for k in range(5):
        rows = summed[8 * k : 8 * k + 8, :] * (1.0 / entries)
        found = jnp.concatenate([rows[:, w * j : w * j + w] for j in range(w // 8)], axis=0)
        m.append(0.5 * (found + found.T))
    gram = jnp.concatenate(
        [jnp.concatenate([m[i + j] for j in range(3)], axis=1) for i in range(3)], axis=0
    )
    upper, inverse = factor(gram, 3 * width)
    mix = jnp.concatenate(
        [jnp.concatenate([p, p], axis=1) for p in parts(inverse[w:], 3)], axis=0
    )
    rows = 3 * zs * xs
    for z in range(zs):
        for c in range(3):
            for x in range(0, xs, 2):
                basis = jnp.concatenate([pair(s, z, c, x) for s in (s0, s1, s2)], axis=0)
                terms = product(mix, jnp.concatenate(parts(basis, 2), axis=0), 0)
                value = terms[: 2 * w] + terms[2 * w : 4 * w] + terms[4 * w :]
                for k in range(2):
                    out[pl.ds((c * zs + z) * xs + x + k, 2 * w, stride=rows), :] = value[
                        :, k * ny : (k + 1) * ny
                    ]
    identity = jnp.where(
        lax.broadcasted_iota(jnp.int32, (w, w), 0) == lax.broadcasted_iota(jnp.int32, (w, w), 1),
        shift,
        0.0,
    )
    x0, x1 = inverse[:w, :w], inverse[w : 2 * w, w : 2 * w]
    u01, u11 = upper[:w, w : 2 * w], upper[w : 2 * w, w : 2 * w]
    u12, u22 = upper[w : 2 * w, 2 * w :], upper[2 * w :, 2 * w :]
    factor_one = precise(u11, x0, 1)
    couplings[0, 0] = precise(u01, x0, 1) + identity
    couplings[0, 1] = factor_one
    couplings[1, 0] = precise(u12 - precise(factor_one, u01, 0), x1, 1) + identity
    couplings[1, 1] = precise(u22, x1, 1)


def moved(name, value, slabs, trans):
    dz, dx = name[0], name[1] % 2 * name[1]
    pairs = [
        (i * trans + j, (i - dz) % slabs * trans + (j - dx) % trans)
        for i in range(slabs)
        for j in range(trans)
    ]
    return lax.ppermute(value, AXES, pairs)


def total_sum(value, deep, trans, devices):
    core, near = trans, 2 * trans
    rounds = [(core, near, core ^ near)]
    if deep == 8:
        middle, far = 4 * trans, 8 * trans
        rounds.append((middle, far ^ near, far ^ middle))
    for masks in rounds:
        one, two, three = (
            lax.ppermute(value, AXES, [(i, i ^ m) for i in range(devices)]) for m in masks
        )
        value = (value + one) + (two + three)
    count = devices // (2 * deep)
    copies = jnp.broadcast_to(value[None], (count, *value.shape))
    return lax.all_to_all(copies, ("y", "x"), 0, 0, tiled=True)


def per_device(slabs, deep, trans, start_block, material, pml_mask, eps_table):
    width, _, zs, xs, ny = start_block.shape
    classes = eps_table.shape[0]
    entries = float(3 * zs * xs * ny * slabs * trans)
    field = shape(zs, 3, xs, width, ny)
    rows = width * 3 * zs * xs
    halo = Halo(zs, xs)

    s0, diag, *messages = call(
        functools.partial(split_body, halo, width, classes),
        [field, shape(zs, xs, ny)] + [shape(halo.rows(n, width), ny) for n in halo.names[:4]],
        [eps_table, material, pml_mask, start_block.reshape(rows, ny)],
        hbm=(0, 1, 2, 3),
        scratch=[
            pltpu.VMEM((rows, ny), jnp.float32),
            pltpu.VMEM((zs, xs, ny), jnp.int32),
            pltpu.VMEM((zs, xs, ny), jnp.int32),
            pltpu.SMEM((classes,), jnp.float32),
            pltpu.SemaphoreType.DMA((4,)),
        ],
    )
    messages = [moved(n, m, slabs, trans) for n, m in zip(halo.names, messages)]
    passed = call(
        functools.partial(relay_body, halo, width),
        [shape(halo.rows(n, width), ny) for n in halo.names[4:]],
        messages[:2],
    )
    messages += [moved(n, m, slabs, trans) for n, m in zip(halo.names[4:], passed)]
    (gram,) = call(functools.partial(start_gram_body, zs, xs), [shape(width, width)], [s0])
    outside = len(halo.first) - 3 * zs * xs
    s1, s2, moments = call(
        functools.partial(apply_body, halo, width, ny, slabs, trans),
        [field, field, shape(40, 4 * width)],
        [s0, diag, gram] + messages,
        scratch=[pltpu.VMEM((outside, 8, ny), jnp.float32)],
    )
    moments = total_sum(moments, deep, trans, slabs * trans)
    blocks, couplings = call(
        functools.partial(last_body, zs, xs, width, ny, classes, entries),
        [shape(2 * rows, ny), shape(2, 2, width, width)],
        [eps_table, moments, s0, s1, s2],
        smem=(0,),
    )
    return blocks.reshape(2, width, 3, zs, xs, ny), couplings


def solution(mesh):
    slabs, trans = mesh.devices.shape
    deep = 8 if slabs == 64 else 2
    sizes = (slabs // (2 * deep), deep, 2, trans)
    split = jax.sharding.Mesh(mesh.devices.reshape(sizes), AXES)
    slab = AXES[:3]
    return jax.shard_map(
        functools.partial(per_device, slabs, deep, trans),
        mesh=split,
        in_specs=(
            P(None, None, slab, "x", None),
            P(slab, "x", None),
            P(slab, "x", None),
            P(),
        ),
        out_specs=(P(None, None, None, slab, "x", None), P()),
        check_vma=False,
    )
```

```python
import functools

import jax
import jax.numpy as jnp
from jax import lax
from jax.experimental import pallas as pl
from jax.experimental.pallas import tpu as pltpu
from jax.sharding import PartitionSpec as P

AXES = ("y", "z", "core", "x")
ABSORB = 4.0
CURL_CENTRE = 5.0
VMEM_LIMIT = 40 * 1024 * 1024


def call(body, out_shape, operands, smem=(), hbm=(), hbm_out=(), scratch=()):
    special = {**{i: pltpu.SMEM for i in smem}, **{i: pltpu.HBM for i in hbm}}
    specs = [
        pl.BlockSpec(memory_space=special.get(i, pltpu.VMEM)) for i in range(len(operands))
    ]
    outs = [
        pl.BlockSpec(memory_space=pltpu.HBM if i in hbm_out else pltpu.VMEM)
        for i in range(len(out_shape))
    ]
    return pl.pallas_call(
        body,
        out_shape=out_shape,
        in_specs=specs,
        out_specs=outs,
        scratch_shapes=list(scratch),
        compiler_params=pltpu.CompilerParams(vmem_limit_bytes=VMEM_LIMIT),
    )(
        *(
            pltpu.with_memory_space_constraint(a, pltpu.HBM) if i in hbm else a
            for i, a in enumerate(operands)
        )
    )


def shape(*dims):
    return jax.ShapeDtypeStruct(dims, jnp.float32)


class Halo:
    def __init__(self, zs, xs):
        self.zs, self.xs = zs, xs
        self.first = set()
        for c in range(3):
            for z in range(zs):
                for x in range(xs):
                    self.first.add((c, z, x))
                    self.first |= reach(c, z, x)
        cells = set(self.first)
        for cell in self.first:
            cells |= reach(*cell)
        self.names = [(0, -1), (0, 1), (-1, 0), (1, 0), (-1, 2), (1, 2)]
        self.blocks, self.diagonal = {}, {}
        for name in self.names:
            self.blocks[name] = sorted(q for q in cells if self.name(q[1], q[2]) == name)
            near = {q[1:] for q in self.first if self.name(q[1], q[2]) == name}
            self.diagonal[name] = sorted(near)

    def name(self, z, x):
        side = self.side(z, x)
        return (side[0], 2) if side[0] and side[1] else side

    def side(self, z, x):
        return (
            -1 if z < 0 else int(z >= self.zs),
            -1 if x < 0 else int(x >= self.xs),
        )

    def own(self, name, z, x):
        return z - name[0] * self.zs, x - name[1] % 2 * name[1] * self.xs

    def rows(self, name, width):
        return len(self.blocks[name]) * width + 8

    def block_row(self, name, c, z, x, width):
        return self.blocks[name].index((c, z, x)) * width

    def diagonal_row(self, name, z, x, width):
        return len(self.blocks[name]) * width + self.diagonal[name].index((z, x))


CURL = (
    lambda z, x: {(2, z, x), (1, z + 1, x), (1, z, x)},
    lambda z, x: {(0, z + 1, x), (0, z, x), (2, z, x + 1), (2, z, x)},
    lambda z, x: {(1, z, x + 1), (1, z, x), (0, z, x)},
)
BACK = (
    lambda z, x: {(2, z, x), (1, z, x), (1, z - 1, x)},
    lambda z, x: {(0, z, x), (0, z - 1, x), (2, z, x), (2, z, x - 1)},
    lambda z, x: {(1, z, x), (1, z, x - 1), (0, z, x)},
)


def reach(c, z, x):
    cells = {(c, z, x)}
    for k, hz, hx in BACK[c](z, x):
        cells |= CURL[k](hz, hx)
    return cells


def stencil(e, lane, last):
    known = {}

    def step_y(value):
        return jnp.where(lane == last, 0.0, pltpu.roll(value, last, 1)) - value

    def h(k, z, x):
        if (k, z, x) not in known:
            if k == 0:
                value = step_y(e(2, z, x)) - (e(1, z + 1, x) - e(1, z, x))
            elif k == 1:
                value = (e(0, z + 1, x) - e(0, z, x)) - (e(2, z, x + 1) - e(2, z, x))
            else:
                value = (e(1, z, x + 1) - e(1, z, x)) - step_y(e(0, z, x))
            known[k, z, x] = value
        return known[k, z, x]

    def result(c, z, x):
        if c == 0:
            here = h(2, z, x)
            before = jnp.where(lane == 0, -e(0, z, x), pltpu.roll(here, 1, 1))
            return (here - before) - (h(1, z, x) - h(1, z - 1, x))
        if c == 1:
            return (h(0, z, x) - h(0, z - 1, x)) - (h(2, z, x) - h(2, z, x - 1))
        here = h(0, z, x)
        before = jnp.where(lane == 0, e(2, z, x), pltpu.roll(here, 1, 1))
        return (h(1, z, x) - h(1, z, x - 1)) - (here - before)

    return result


def split_body(halo, width, classes, eps, material, mask, start, field, diag, *refs):
    zs, xs = halo.zs, halo.xs
    rows = 3 * zs * xs
    messages, (start_in, material_in, mask_in, eps_in, sems) = refs[:4], refs[4:]
    copies = [
        pltpu.make_async_copy(source, target, sems.at[i])
        for i, (source, target) in enumerate(
            [(eps, eps_in), (material, material_in), (mask, mask_in), (start, start_in)]
        )
    ]
    for copy in copies:
        copy.start()
    for copy in copies[:3]:
        copy.wait()
    eps = eps_in
    total = eps[0]
    for level in range(1, classes):
        total = total + eps[level]
    shift = total / classes + CURL_CENTRE
    value = jnp.zeros(material_in.shape, jnp.float32)
    for level in range(classes):
        value = value + jnp.where(material_in[...] == level, eps[level], 0.0)
    diag[...] = value + ABSORB * mask_in[...].astype(jnp.float32) - shift

    places = {}
    for name, message in zip(halo.names, messages):
        for c, z, x in halo.blocks[name]:
            row = halo.block_row(name, c, z, x, width)
            places.setdefault((c, *halo.own(name, z, x)), []).append((message, row))
        base = len(halo.blocks[name]) * width
        message[base : base + 8, :] = jnp.zeros((8, message.shape[1]), jnp.float32)
        for z, x in halo.diagonal[name]:
            row = halo.diagonal_row(name, z, x, width)
            oz, ox = halo.own(name, z, x)
            message[row : row + 1, :] = diag[oz, ox : ox + 1, :]
    copies[3].wait()
    for z in range(zs):
        for c in range(3):
            for x in range(xs):
                cell = start_in[pl.ds((c * zs + z) * xs + x, width, stride=rows), :]
                field[z, c, x] = cell
                for message, row in places.get((c, z, x), ()):
                    message[row : row + width, :] = cell


def relay_body(halo, width, before, after, *passed):
    received = {-1: ((0, -1), before), 1: ((0, 1), after)}
    for name, message in zip(halo.names[4:], passed):
        base = len(halo.blocks[name]) * width
        message[base : base + 8, :] = jnp.zeros((8, message.shape[1]), jnp.float32)
        for c, z, x in halo.blocks[name]:
            side, source = received[halo.side(z, x)[1]]
            at = halo.block_row(side, c, z - name[0] * halo.zs, x, width)
            row = halo.block_row(name, c, z, x, width)
            message[row : row + width, :] = source[at : at + width, :]
        for z, x in halo.diagonal[name]:
            side, source = received[halo.side(z, x)[1]]
            at = halo.diagonal_row(side, z - name[0] * halo.zs, x, width)
            row = halo.diagonal_row(name, z, x, width)
            message[row : row + 1, :] = source[at : at + 1, :]


def parts(value, count):
    found, rest = [], value
    for i in range(count):
        found.append(rest.astype(jnp.bfloat16))
        if i + 1 < count:
            rest = rest - found[-1].astype(jnp.float32)
    return found


def pair(ref, z, c, x):
    return jnp.concatenate([ref[z, c, x], ref[z, c, x + 1]], axis=1)


def product(left, right, contract):
    return lax.dot_general(
        left, right, (((1,), (contract,)), ((), ())), preferred_element_type=jnp.float32
    )


def fold(total, left, right):
    rows = total[:left] + total[left : 2 * left] + total[2 * left :]
    return rows[:, :right] + rows[:, right : 2 * right] + rows[:, 2 * right :]


def start_gram_body(zs, xs, s0, out):
    total = None
    for z in range(zs):
        for c in range(3):
            for x in range(0, xs, 2):
                stack = jnp.concatenate(parts(pair(s0, z, c, x), 3), axis=0)
                term = product(stack, stack, 1)
                total = term if total is None else total + term
    out[...] = fold(total, *out.shape)


def apply_body(halo, width, ny, slabs, trans, s0, diag, gram, *refs):
    zs, xs = halo.zs, halo.xs
    messages = dict(zip(halo.names, refs[:6]))
    s1, s2, moments, outer = refs[6:]
    slab, across = lax.axis_index(AXES[:3]), lax.axis_index("x")
    held_z = {-1: slab > 0, 0: slab >= 0, 1: slab < slabs - 1}
    held_x = {-1: across > 0, 0: across >= 0, 1: across < trans - 1}
    inside = {
        (i, j): jnp.where(jnp.logical_and(held_z[i], held_x[j]), 1.0, 0.0)
        for i in (-1, 0, 1)
        for j in (-1, 0, 1)
    }
    extra = sorted(q for q in halo.first if halo.side(q[1], q[2]) != (0, 0))
    extra = {q: i for i, q in enumerate(extra)}
    lane = lax.broadcasted_iota(jnp.int32, (8, ny), 1)

    def diagonal(z, x):
        name = halo.name(z, x)
        if name == (0, 0):
            return diag[z, x : x + 1, :]
        row = halo.diagonal_row(name, z, x, width)
        return messages[name][row : row + 1, :]

    def group(at):
        def start(c, z, x):
            name = halo.name(z, x)
            if name == (0, 0):
                return s0[z, c, x, pl.ds(at, 8), :]
            row = halo.block_row(name, c, z, x, width)
            return messages[name][pl.ds(row + at, 8), :] * inside[halo.side(z, x)]

        def once(c, z, x):
            if halo.side(z, x) == (0, 0):
                return s1[z, c, x, pl.ds(at, 8), :]
            return outer[extra[c, z, x]]

        apply = stencil(start, lane, ny - 1)
        for x in range(-1, xs + 1):
            for z in range(-1, zs + 1):
                for c in range(3):
                    if (c, z, x) not in halo.first:
                        continue
                    value = apply(c, z, x) + diagonal(z, x) * start(c, z, x)
                    side = halo.side(z, x)
                    if side == (0, 0):
                        s1[z, c, x, pl.ds(at, 8), :] = value
                    else:
                        outer[extra[c, z, x]] = value * inside[side]
        apply = stencil(once, lane, ny - 1)
        for x in range(xs):
            for z in range(zs):
                for c in range(3):
                    value = apply(c, z, x) + diagonal(z, x) * once(c, z, x)
                    s2[z, c, x, pl.ds(at, 8), :] = value

    for at in range(0, width, 8):
        group(at)

    total = None
    for z in range(zs):
        for c in range(3):
            for x in range(0, xs, 2):
                split = [parts(pair(s, z, c, x), 3) for s in (s0, s1, s2)]
                left = jnp.concatenate([p for i in range(3) for p in (s[i] for s in split)], axis=0)
                right = jnp.concatenate(
                    [p for i in range(3) for p in (s[i] for s in split[1:])], axis=0
                )
                term = product(left, right, 1)
                total = term if total is None else total + term
    found = fold(total, 3 * width, 2 * width)
    w = width
    found = [
        gram[...],
        found[:w, :w],
        found[w : 2 * w, :w],
        found[w : 2 * w, w:],
        found[2 * w :, w:],
    ]
    for k, m in enumerate(found):
        for j in range(w // 8):
            moments[8 * k : 8 * k + 8, w * j : w * j + w] = m[8 * j : 8 * j + 8]


def precise(left, right, contract):
    return lax.dot_general(
        left,
        right,
        (((1,), (contract,)), ((), ())),
        precision=lax.Precision.HIGHEST,
        preferred_element_type=jnp.float32,
    )


def factor(gram, size, pauses):
    tiles = size // 8
    lane = lax.broadcasted_iota(jnp.int32, (8, size), 1)
    sub = lax.broadcasted_iota(jnp.int32, (8, size), 0)
    upper = [gram[8 * t : 8 * t + 8, :] for t in range(tiles)]
    inverse = [jnp.where(lane == sub + 8 * t, 1.0, 0.0) for t in range(tiles)]
    found_u, found_i = [], []

    def column(u, j):
        return jnp.broadcast_to(upper[u][:, j : j + 1], (8, size))

    ahead = [column(0, j) for j in range(8)]
    for t in range(tiles):
        cols = {u: [column(u, 8 * t + j) for j in range(8)] for u in range(t + 1, tiles)}
        cols[t] = ahead
        if t + 1 < tiles:
            ahead = [column(t + 1, 8 * t + 8 + j) for j in range(8)]
        pivots = jnp.zeros((8, size), jnp.float32)
        for s in range(8):
            pivot = jnp.broadcast_to(cols[t][s][s : s + 1, :], (8, size))
            pivots = jnp.where(sub == s, pivot, pivots)
            reciprocal = 1.0 / pivot
            heads = [cols[t][j][s : s + 1, :] for j in range(8)]
            row_u, row_i = upper[t][s : s + 1, :], inverse[t][s : s + 1, :]
            for u in range(t, tiles):
                f = cols[u][s] * reciprocal
                if u == t:
                    f = jnp.where(sub > s, f, 0.0)
                if u == t + 1:
                    for j in range(8):
                        ahead[j] = ahead[j] - f * cols[u][s][j : j + 1, :]
                for j in range(s + 1, 8):
                    cols[u][j] = cols[u][j] - f * heads[j]
                upper[u] = upper[u] - f * row_u
                inverse[u] = inverse[u] - f * row_i
        scale = lax.rsqrt(pivots)
        found_u.append(upper[t] * scale)
        found_i.append(inverse[t] * scale)
        if t + 1 in pauses:
            yield jnp.concatenate(found_u, axis=0), jnp.concatenate(found_i, axis=0)


def basis_body(zs, xs, width, s0, s1, s2, out):
    w = width
    for i, (z, c, x) in enumerate(cell_pairs(zs, xs)):
        first = jnp.concatenate([pair(s0, z, c, x), pair(s1, z, c, x)], axis=0)
        out[i, : 4 * w] = jnp.concatenate(parts(first, 2), axis=0)
        out[i, 4 * w :] = jnp.concatenate(parts(pair(s2, z, c, x), 2), axis=0)


def cell_pairs(zs, xs):
    return [(z, c, x) for z in range(zs) for c in range(3) for x in range(0, xs, 2)]


def last_body(zs, xs, width, ny, classes, entries, eps, moments, basis, out, couplings, *scratch):
    w = width
    staged, sems = scratch
    total = eps[0]
    for level in range(1, classes):
        total = total + eps[level]
    shift = total / classes + CURL_CENTRE
    m = []
    summed = moments[0]
    for i in range(1, moments.shape[0]):
        summed = summed + moments[i]
    for k in range(5):
        rows = summed[8 * k : 8 * k + 8, :] * (1.0 / entries)
        m.append(jnp.concatenate([rows[:, w * j : w * j + w] for j in range(w // 8)], axis=0))
    gram = jnp.concatenate(
        [jnp.concatenate([m[i + j] for j in range(3)], axis=1) for i in range(3)], axis=0
    )
    rows = 3 * zs * xs

    def combine(block, mix, depth):
        for i, (z, c, x) in enumerate(cell_pairs(zs, xs)):
            terms = product(mix, basis[i, :depth], 0)
            value = terms[:w] + terms[w : 2 * w] + terms[2 * w :]
            for k in range(2):
                at = (c * zs + z) * xs + x + k
                staged[block, pl.ds(at, w, stride=rows), :] = value[:, k * ny : (k + 1) * ny]
        copy = pltpu.make_async_copy(staged.at[block], out.at[block], sems.at[block])
        copy.start()
        return copy

    steps = factor(gram, 3 * w, (w // 4, 3 * w // 8))
    upper, inverse = next(steps)
    mix = [jnp.concatenate([p, p], axis=1) for p in parts(inverse[w:, : 2 * w], 3)]
    copies = [combine(0, jnp.concatenate(mix, axis=0), 4 * w)]
    upper, inverse = next(steps)
    mix = [
        jnp.concatenate([p[:, : 2 * w], p[:, : 2 * w], p[:, 2 * w :], p[:, 2 * w :]], axis=1)
        for p in parts(inverse[2 * w :], 3)
    ]
    copies.append(combine(1, jnp.concatenate(mix, axis=0), 6 * w))
    identity = jnp.where(
        lax.broadcasted_iota(jnp.int32, (w, w), 0) == lax.broadcasted_iota(jnp.int32, (w, w), 1),
        shift,
        0.0,
    )
    x0, x1 = inverse[:w, :w], inverse[w : 2 * w, w : 2 * w]
    u01, u11 = upper[:w, w : 2 * w], upper[w : 2 * w, w : 2 * w]
    u12, u22 = upper[w : 2 * w, 2 * w :], upper[2 * w :, 2 * w :]
    factor_one = precise(u11, x0, 1)
    couplings[0, 0] = precise(u01, x0, 1) + identity
    couplings[0, 1] = factor_one
    couplings[1, 0] = precise(u12 - precise(factor_one, u01, 0), x1, 1) + identity
    couplings[1, 1] = precise(u22, x1, 1)
    for copy in copies:
        copy.wait()


def moved(name, value, slabs, trans):
    dz, dx = name[0], name[1] % 2 * name[1]
    pairs = [
        (i * trans + j, (i - dz) % slabs * trans + (j - dx) % trans)
        for i in range(slabs)
        for j in range(trans)
    ]
    return lax.ppermute(value, AXES, pairs)


def total_sum(value, deep, trans, devices):
    core, near = trans, 2 * trans
    rounds = [(core, near, core ^ near)]
    if deep == 8:
        middle, far = 4 * trans, 8 * trans
        rounds.append((middle, far ^ near, far ^ middle))
    for masks in rounds:
        one, two, three = (
            lax.ppermute(value, AXES, [(i, i ^ m) for i in range(devices)]) for m in masks
        )
        value = (value + one) + (two + three)
    count = devices // (2 * deep)
    copies = jnp.broadcast_to(value[None], (count, *value.shape))
    return lax.all_to_all(copies, ("y", "x"), 0, 0, tiled=True)


def per_device(slabs, deep, trans, start_block, material, pml_mask, eps_table):
    width, _, zs, xs, ny = start_block.shape
    classes = eps_table.shape[0]
    entries = float(3 * zs * xs * ny * slabs * trans)
    field = shape(zs, 3, xs, width, ny)
    rows = width * 3 * zs * xs
    halo = Halo(zs, xs)

    s0, diag, *messages = call(
        functools.partial(split_body, halo, width, classes),
        [field, shape(zs, xs, ny)] + [shape(halo.rows(n, width), ny) for n in halo.names[:4]],
        [eps_table, material, pml_mask, start_block.reshape(rows, ny)],
        hbm=(0, 1, 2, 3),
        scratch=[
            pltpu.VMEM((rows, ny), jnp.float32),
            pltpu.VMEM((zs, xs, ny), jnp.int32),
            pltpu.VMEM((zs, xs, ny), jnp.int32),
            pltpu.SMEM((classes,), jnp.float32),
            pltpu.SemaphoreType.DMA((4,)),
        ],
    )
    messages = [moved(n, m, slabs, trans) for n, m in zip(halo.names, messages)]
    passed = call(
        functools.partial(relay_body, halo, width),
        [shape(halo.rows(n, width), ny) for n in halo.names[4:]],
        messages[:2],
    )
    messages += [moved(n, m, slabs, trans) for n, m in zip(halo.names[4:], passed)]
    (gram,) = call(functools.partial(start_gram_body, zs, xs), [shape(width, width)], [s0])
    outside = len(halo.first) - 3 * zs * xs
    s1, s2, moments = call(
        functools.partial(apply_body, halo, width, ny, slabs, trans),
        [field, field, shape(40, 4 * width)],
        [s0, diag, gram] + messages,
        scratch=[pltpu.VMEM((outside, 8, ny), jnp.float32)],
    )
    moments = total_sum(moments, deep, trans, slabs * trans)
    (basis,) = call(
        functools.partial(basis_body, zs, xs, width),
        [jax.ShapeDtypeStruct((len(cell_pairs(zs, xs)), 6 * width, 2 * ny), jnp.bfloat16)],
        [s0, s1, s2],
    )
    blocks, couplings = call(
        functools.partial(last_body, zs, xs, width, ny, classes, entries),
        [shape(2, rows, ny), shape(2, 2, width, width)],
        [eps_table, moments, basis],
        smem=(0,),
        hbm_out=(0,),
        scratch=[pltpu.VMEM((2, rows, ny), jnp.float32), pltpu.SemaphoreType.DMA((2,))],
    )
    return blocks.reshape(2, width, 3, zs, xs, ny), couplings


def solution(mesh):
    slabs, trans = mesh.devices.shape
    deep = 8 if slabs == 64 else 2
    sizes = (slabs // (2 * deep), deep, 2, trans)
    split = jax.sharding.Mesh(mesh.devices.reshape(sizes), AXES)
    slab = AXES[:3]
    return jax.shard_map(
        functools.partial(per_device, slabs, deep, trans),
        mesh=split,
        in_specs=(
            P(None, None, slab, "x", None),
            P(slab, "x", None),
            P(slab, "x", None),
            P(),
        ),
        out_specs=(P(None, None, None, slab, "x", None), P()),
        check_vma=False,
    )
```

```python
import functools

import jax
import jax.numpy as jnp
from jax import lax
from jax.experimental import pallas as pl
from jax.experimental.pallas import tpu as pltpu
from jax.sharding import PartitionSpec as P

AXES = ("y", "z", "core", "x")
ABSORB = 4.0
CURL_CENTRE = 5.0
VMEM_LIMIT = 40 * 1024 * 1024


def call(body, out_shape, operands, smem=(), hbm=(), hbm_out=(), scratch=()):
    special = {**{i: pltpu.SMEM for i in smem}, **{i: pltpu.HBM for i in hbm}}
    specs = [
        pl.BlockSpec(memory_space=special.get(i, pltpu.VMEM)) for i in range(len(operands))
    ]
    outs = [
        pl.BlockSpec(memory_space=pltpu.HBM if i in hbm_out else pltpu.VMEM)
        for i in range(len(out_shape))
    ]
    return pl.pallas_call(
        body,
        out_shape=out_shape,
        in_specs=specs,
        out_specs=outs,
        scratch_shapes=list(scratch),
        compiler_params=pltpu.CompilerParams(vmem_limit_bytes=VMEM_LIMIT),
    )(
        *(
            pltpu.with_memory_space_constraint(a, pltpu.HBM) if i in hbm else a
            for i, a in enumerate(operands)
        )
    )


def shape(*dims):
    return jax.ShapeDtypeStruct(dims, jnp.float32)


class Halo:
    def __init__(self, zs, xs):
        self.zs, self.xs = zs, xs
        self.first = set()
        for c in range(3):
            for z in range(zs):
                for x in range(xs):
                    self.first.add((c, z, x))
                    self.first |= reach(c, z, x)
        cells = set(self.first)
        for cell in self.first:
            cells |= reach(*cell)
        self.names = [(0, -1), (0, 1), (-1, 0), (1, 0), (-1, 2), (1, 2)]
        self.blocks, self.diagonal = {}, {}
        for name in self.names:
            self.blocks[name] = sorted(q for q in cells if self.name(q[1], q[2]) == name)
            near = {q[1:] for q in self.first if self.name(q[1], q[2]) == name}
            self.diagonal[name] = sorted(near)

    def name(self, z, x):
        side = self.side(z, x)
        return (side[0], 2) if side[0] and side[1] else side

    def side(self, z, x):
        return (
            -1 if z < 0 else int(z >= self.zs),
            -1 if x < 0 else int(x >= self.xs),
        )

    def own(self, name, z, x):
        return z - name[0] * self.zs, x - name[1] % 2 * name[1] * self.xs

    def rows(self, name, width):
        return len(self.blocks[name]) * width + 8

    def block_row(self, name, c, z, x, width):
        return self.blocks[name].index((c, z, x)) * width

    def diagonal_row(self, name, z, x, width):
        return len(self.blocks[name]) * width + self.diagonal[name].index((z, x))


CURL = (
    lambda z, x: {(2, z, x), (1, z + 1, x), (1, z, x)},
    lambda z, x: {(0, z + 1, x), (0, z, x), (2, z, x + 1), (2, z, x)},
    lambda z, x: {(1, z, x + 1), (1, z, x), (0, z, x)},
)
BACK = (
    lambda z, x: {(2, z, x), (1, z, x), (1, z - 1, x)},
    lambda z, x: {(0, z, x), (0, z - 1, x), (2, z, x), (2, z, x - 1)},
    lambda z, x: {(1, z, x), (1, z, x - 1), (0, z, x)},
)


def reach(c, z, x):
    cells = {(c, z, x)}
    for k, hz, hx in BACK[c](z, x):
        cells |= CURL[k](hz, hx)
    return cells


def stencil(e, lane, last):
    known = {}

    def step_y(value):
        return jnp.where(lane == last, 0.0, pltpu.roll(value, last, 1)) - value

    def h(k, z, x):
        if (k, z, x) not in known:
            if k == 0:
                value = step_y(e(2, z, x)) - (e(1, z + 1, x) - e(1, z, x))
            elif k == 1:
                value = (e(0, z + 1, x) - e(0, z, x)) - (e(2, z, x + 1) - e(2, z, x))
            else:
                value = (e(1, z, x + 1) - e(1, z, x)) - step_y(e(0, z, x))
            known[k, z, x] = value
        return known[k, z, x]

    def result(c, z, x):
        if c == 0:
            here = h(2, z, x)
            before = jnp.where(lane == 0, -e(0, z, x), pltpu.roll(here, 1, 1))
            return (here - before) - (h(1, z, x) - h(1, z - 1, x))
        if c == 1:
            return (h(0, z, x) - h(0, z - 1, x)) - (h(2, z, x) - h(2, z, x - 1))
        here = h(0, z, x)
        before = jnp.where(lane == 0, e(2, z, x), pltpu.roll(here, 1, 1))
        return (h(1, z, x) - h(1, z, x - 1)) - (here - before)

    return result


def split_body(halo, width, classes, eps, material, mask, start, field, diag, *refs):
    zs, xs = halo.zs, halo.xs
    rows = 3 * zs * xs
    messages, (start_in, material_in, mask_in, eps_in, sems) = refs[:4], refs[4:]
    copies = [
        pltpu.make_async_copy(source, target, sems.at[i])
        for i, (source, target) in enumerate(
            [(eps, eps_in), (material, material_in), (mask, mask_in), (start, start_in)]
        )
    ]
    for copy in copies:
        copy.start()
    for copy in copies[:3]:
        copy.wait()
    eps = eps_in
    total = eps[0]
    for level in range(1, classes):
        total = total + eps[level]
    shift = total / classes + CURL_CENTRE
    value = jnp.zeros(material_in.shape, jnp.float32)
    for level in range(classes):
        value = value + jnp.where(material_in[...] == level, eps[level], 0.0)
    diag[...] = value + ABSORB * mask_in[...].astype(jnp.float32) - shift

    places = {}
    for name, message in zip(halo.names, messages):
        for c, z, x in halo.blocks[name]:
            row = halo.block_row(name, c, z, x, width)
            places.setdefault((c, *halo.own(name, z, x)), []).append((message, row))
        base = len(halo.blocks[name]) * width
        message[base : base + 8, :] = jnp.zeros((8, message.shape[1]), jnp.float32)
        for z, x in halo.diagonal[name]:
            row = halo.diagonal_row(name, z, x, width)
            oz, ox = halo.own(name, z, x)
            message[row : row + 1, :] = diag[oz, ox : ox + 1, :]
    copies[3].wait()
    for z in range(zs):
        for c in range(3):
            for x in range(xs):
                cell = start_in[pl.ds((c * zs + z) * xs + x, width, stride=rows), :]
                field[z, c, x] = cell
                for message, row in places.get((c, z, x), ()):
                    message[row : row + width, :] = cell


def relay_body(halo, width, before, after, *passed):
    received = {-1: ((0, -1), before), 1: ((0, 1), after)}
    for name, message in zip(halo.names[4:], passed):
        base = len(halo.blocks[name]) * width
        message[base : base + 8, :] = jnp.zeros((8, message.shape[1]), jnp.float32)
        for c, z, x in halo.blocks[name]:
            side, source = received[halo.side(z, x)[1]]
            at = halo.block_row(side, c, z - name[0] * halo.zs, x, width)
            row = halo.block_row(name, c, z, x, width)
            message[row : row + width, :] = source[at : at + width, :]
        for z, x in halo.diagonal[name]:
            side, source = received[halo.side(z, x)[1]]
            at = halo.diagonal_row(side, z - name[0] * halo.zs, x, width)
            row = halo.diagonal_row(name, z, x, width)
            message[row : row + 1, :] = source[at : at + 1, :]


def parts(value, count):
    found, rest = [], value
    for i in range(count):
        found.append(rest.astype(jnp.bfloat16))
        if i + 1 < count:
            rest = rest - found[-1].astype(jnp.float32)
    return found


def pair(ref, z, c, x):
    return jnp.concatenate([ref[z, c, x], ref[z, c, x + 1]], axis=1)


def product(left, right, contract):
    return lax.dot_general(
        left, right, (((1,), (contract,)), ((), ())), preferred_element_type=jnp.float32
    )


def fold(total, left, right):
    rows = total[:left] + total[left : 2 * left] + total[2 * left :]
    return rows[:, :right] + rows[:, right : 2 * right] + rows[:, 2 * right :]


def cell_pairs(zs, xs):
    return [(z, c, x) for z in range(zs) for c in range(3) for x in range(0, xs, 2)]


def start_gram_body(zs, xs, s0, out):
    total = None
    for z, c, x in cell_pairs(zs, xs):
        stack = jnp.concatenate(parts(pair(s0, z, c, x), 3), axis=0)
        term = product(stack, stack, 1)
        total = term if total is None else total + term
    out[...] = fold(total, *out.shape)


def apply_body(halo, width, ny, slabs, trans, s0, diag, gram, *refs):
    zs, xs = halo.zs, halo.xs
    messages = dict(zip(halo.names, refs[:6]))
    basis, moments, s1, s2, outer = refs[6:]
    slab, across = lax.axis_index(AXES[:3]), lax.axis_index("x")
    held_z = {-1: slab > 0, 0: slab >= 0, 1: slab < slabs - 1}
    held_x = {-1: across > 0, 0: across >= 0, 1: across < trans - 1}
    inside = {
        (i, j): jnp.where(jnp.logical_and(held_z[i], held_x[j]), 1.0, 0.0)
        for i in (-1, 0, 1)
        for j in (-1, 0, 1)
    }
    extra = sorted(q for q in halo.first if halo.side(q[1], q[2]) != (0, 0))
    extra = {q: i for i, q in enumerate(extra)}
    lane = lax.broadcasted_iota(jnp.int32, (8, ny), 1)

    def diagonal(z, x):
        name = halo.name(z, x)
        if name == (0, 0):
            return diag[z, x : x + 1, :]
        row = halo.diagonal_row(name, z, x, width)
        return messages[name][row : row + 1, :]

    def group(at):
        def start(c, z, x):
            name = halo.name(z, x)
            if name == (0, 0):
                return s0[z, c, x, pl.ds(at, 8), :]
            row = halo.block_row(name, c, z, x, width)
            return messages[name][pl.ds(row + at, 8), :] * inside[halo.side(z, x)]

        def once(c, z, x):
            if halo.side(z, x) == (0, 0):
                return s1[z, c, x, pl.ds(at, 8), :]
            return outer[extra[c, z, x]]

        apply = stencil(start, lane, ny - 1)
        for x in range(-1, xs + 1):
            for z in range(-1, zs + 1):
                for c in range(3):
                    if (c, z, x) not in halo.first:
                        continue
                    value = apply(c, z, x) + diagonal(z, x) * start(c, z, x)
                    side = halo.side(z, x)
                    if side == (0, 0):
                        s1[z, c, x, pl.ds(at, 8), :] = value
                    else:
                        outer[extra[c, z, x]] = value * inside[side]
        apply = stencil(once, lane, ny - 1)
        for x in range(xs):
            for z in range(zs):
                for c in range(3):
                    value = apply(c, z, x) + diagonal(z, x) * once(c, z, x)
                    s2[z, c, x, pl.ds(at, 8), :] = value

    for at in range(0, width, 8):
        group(at)

    total = None
    for i, (z, c, x) in enumerate(cell_pairs(zs, xs)):
        k0, k1, k2 = (parts(pair(s, z, c, x), 3) for s in (s0, s1, s2))
        basis[i] = jnp.concatenate([k0[0], k1[0], k0[1], k1[1], k2[0], k2[1]], axis=0)
        left = jnp.concatenate([p for three in zip(k0, k1, k2) for p in three], axis=0)
        right = jnp.concatenate([p for two in zip(k1, k2) for p in two], axis=0)
        term = product(left, right, 1)
        total = term if total is None else total + term
    found = fold(total, 3 * width, 2 * width)
    w = width
    found = [
        gram[...],
        found[:w, :w],
        found[w : 2 * w, :w],
        found[w : 2 * w, w:],
        found[2 * w :, w:],
    ]
    for k, m in enumerate(found):
        for j in range(w // 8):
            moments[8 * k : 8 * k + 8, w * j : w * j + w] = m[8 * j : 8 * j + 8]


def precise(left, right, contract):
    return lax.dot_general(
        left,
        right,
        (((1,), (contract,)), ((), ())),
        precision=lax.Precision.HIGHEST,
        preferred_element_type=jnp.float32,
    )


def factor(gram, size, pauses):
    tiles = size // 8
    lane = lax.broadcasted_iota(jnp.int32, (8, size), 1)
    sub = lax.broadcasted_iota(jnp.int32, (8, size), 0)
    upper = [gram[8 * t : 8 * t + 8, :] for t in range(tiles)]
    inverse = [jnp.where(lane == sub + 8 * t, 1.0, 0.0) for t in range(tiles)]
    found_u, found_i = [], []

    def column(u, j):
        return jnp.broadcast_to(upper[u][:, j : j + 1], (8, size))

    ahead = [column(0, j) for j in range(8)]
    for t in range(tiles):
        cols = {u: [column(u, 8 * t + j) for j in range(8)] for u in range(t + 1, tiles)}
        cols[t] = ahead
        if t + 1 < tiles:
            ahead = [column(t + 1, 8 * t + 8 + j) for j in range(8)]
        pivots = jnp.zeros((8, size), jnp.float32)
        for s in range(8):
            pivot = jnp.broadcast_to(cols[t][s][s : s + 1, :], (8, size))
            pivots = jnp.where(sub == s, pivot, pivots)
            reciprocal = 1.0 / pivot
            heads = [cols[t][j][s : s + 1, :] for j in range(8)]
            row_u, row_i = upper[t][s : s + 1, :], inverse[t][s : s + 1, :]
            for u in range(t, tiles):
                f = cols[u][s] * reciprocal
                if u == t:
                    f = jnp.where(sub > s, f, 0.0)
                if u == t + 1:
                    for j in range(8):
                        ahead[j] = ahead[j] - f * cols[u][s][j : j + 1, :]
                for j in range(s + 1, 8):
                    cols[u][j] = cols[u][j] - f * heads[j]
                upper[u] = upper[u] - f * row_u
                inverse[u] = inverse[u] - f * row_i
        scale = lax.rsqrt(pivots)
        found_u.append(upper[t] * scale)
        found_i.append(inverse[t] * scale)
        if t + 1 in pauses:
            yield jnp.concatenate(found_u, axis=0), jnp.concatenate(found_i, axis=0)


def last_body(zs, xs, width, ny, classes, entries, eps, moments, basis, out, couplings, *scratch):
    w = width
    staged, sems = scratch
    total = eps[0]
    for level in range(1, classes):
        total = total + eps[level]
    shift = total / classes + CURL_CENTRE
    m = []
    summed = moments[0]
    for i in range(1, moments.shape[0]):
        summed = summed + moments[i]
    for k in range(5):
        rows = summed[8 * k : 8 * k + 8, :] * (1.0 / entries)
        m.append(jnp.concatenate([rows[:, w * j : w * j + w] for j in range(w // 8)], axis=0))
    gram = jnp.concatenate(
        [jnp.concatenate([m[i + j] for j in range(3)], axis=1) for i in range(3)], axis=0
    )
    rows = 3 * zs * xs

    def combine(block, mix, depth):
        for i, (z, c, x) in enumerate(cell_pairs(zs, xs)):
            terms = product(mix, basis[i, :depth], 0)
            value = terms[:w] + terms[w : 2 * w] + terms[2 * w :]
            for k in range(2):
                at = (c * zs + z) * xs + x + k
                staged[block, pl.ds(at, w, stride=rows), :] = value[:, k * ny : (k + 1) * ny]
        copy = pltpu.make_async_copy(staged.at[block], out.at[block], sems.at[block])
        copy.start()
        return copy

    steps = factor(gram, 3 * w, (w // 4, 3 * w // 8))
    upper, inverse = next(steps)
    mix = [jnp.concatenate([p, p], axis=1) for p in parts(inverse[w:, : 2 * w], 3)]
    copies = [combine(0, jnp.concatenate(mix, axis=0), 4 * w)]
    upper, inverse = next(steps)
    mix = [
        jnp.concatenate([p[:, : 2 * w], p[:, : 2 * w], p[:, 2 * w :], p[:, 2 * w :]], axis=1)
        for p in parts(inverse[2 * w :], 3)
    ]
    copies.append(combine(1, jnp.concatenate(mix, axis=0), 6 * w))
    identity = jnp.where(
        lax.broadcasted_iota(jnp.int32, (w, w), 0) == lax.broadcasted_iota(jnp.int32, (w, w), 1),
        shift,
        0.0,
    )
    x0, x1 = inverse[:w, :w], inverse[w : 2 * w, w : 2 * w]
    u01, u11 = upper[:w, w : 2 * w], upper[w : 2 * w, w : 2 * w]
    u12, u22 = upper[w : 2 * w, 2 * w :], upper[2 * w :, 2 * w :]
    factor_one = precise(u11, x0, 1)
    couplings[0, 0] = precise(u01, x0, 1) + identity
    couplings[0, 1] = factor_one
    couplings[1, 0] = precise(u12 - precise(factor_one, u01, 0), x1, 1) + identity
    couplings[1, 1] = precise(u22, x1, 1)
    for copy in copies:
        copy.wait()


def moved(name, value, slabs, trans):
    dz, dx = name[0], name[1] % 2 * name[1]
    pairs = [
        (i * trans + j, (i - dz) % slabs * trans + (j - dx) % trans)
        for i in range(slabs)
        for j in range(trans)
    ]
    return lax.ppermute(value, AXES, pairs)


def total_sum(value, deep, trans, devices):
    core, near = trans, 2 * trans
    rounds = [(core, near, core ^ near)]
    if deep == 8:
        middle, far = 4 * trans, 8 * trans
        rounds.append((middle, far ^ near, far ^ middle))
    for masks in rounds:
        one, two, three = (
            lax.ppermute(value, AXES, [(i, i ^ m) for i in range(devices)]) for m in masks
        )
        value = (value + one) + (two + three)
    count = devices // (2 * deep)
    copies = jnp.broadcast_to(value[None], (count, *value.shape))
    return lax.all_to_all(copies, ("y", "x"), 0, 0, tiled=True)


def per_device(slabs, deep, trans, start_block, material, pml_mask, eps_table):
    width, _, zs, xs, ny = start_block.shape
    classes = eps_table.shape[0]
    entries = float(3 * zs * xs * ny * slabs * trans)
    field = shape(zs, 3, xs, width, ny)
    rows = width * 3 * zs * xs
    halo = Halo(zs, xs)

    s0, diag, *messages = call(
        functools.partial(split_body, halo, width, classes),
        [field, shape(zs, xs, ny)] + [shape(halo.rows(n, width), ny) for n in halo.names[:4]],
        [eps_table, material, pml_mask, start_block.reshape(rows, ny)],
        hbm=(0, 1, 2, 3),
        scratch=[
            pltpu.VMEM((rows, ny), jnp.float32),
            pltpu.VMEM((zs, xs, ny), jnp.int32),
            pltpu.VMEM((zs, xs, ny), jnp.int32),
            pltpu.SMEM((classes,), jnp.float32),
            pltpu.SemaphoreType.DMA((4,)),
        ],
    )
    messages = [moved(n, m, slabs, trans) for n, m in zip(halo.names, messages)]
    passed = call(
        functools.partial(relay_body, halo, width),
        [shape(halo.rows(n, width), ny) for n in halo.names[4:]],
        messages[:2],
    )
    messages += [moved(n, m, slabs, trans) for n, m in zip(halo.names[4:], passed)]
    (gram,) = call(functools.partial(start_gram_body, zs, xs), [shape(width, width)], [s0])
    outside = len(halo.first) - 3 * zs * xs
    basis, moments = call(
        functools.partial(apply_body, halo, width, ny, slabs, trans),
        [
            jax.ShapeDtypeStruct((len(cell_pairs(zs, xs)), 6 * width, 2 * ny), jnp.bfloat16),
            shape(40, 4 * width),
        ],
        [s0, diag, gram] + messages,
        scratch=[
            pltpu.VMEM(field.shape, jnp.float32),
            pltpu.VMEM(field.shape, jnp.float32),
            pltpu.VMEM((outside, 8, ny), jnp.float32),
        ],
    )
    moments = total_sum(moments, deep, trans, slabs * trans)
    blocks, couplings = call(
        functools.partial(last_body, zs, xs, width, ny, classes, entries),
        [shape(2, rows, ny), shape(2, 2, width, width)],
        [eps_table, moments, basis],
        smem=(0,),
        hbm_out=(0,),
        scratch=[pltpu.VMEM((2, rows, ny), jnp.float32), pltpu.SemaphoreType.DMA((2,))],
    )
    return blocks.reshape(2, width, 3, zs, xs, ny), couplings


def solution(mesh):
    slabs, trans = mesh.devices.shape
    deep = 8 if slabs == 64 else 2
    sizes = (slabs // (2 * deep), deep, 2, trans)
    split = jax.sharding.Mesh(mesh.devices.reshape(sizes), AXES)
    slab = AXES[:3]
    return jax.shard_map(
        functools.partial(per_device, slabs, deep, trans),
        mesh=split,
        in_specs=(
            P(None, None, slab, "x", None),
            P(slab, "x", None),
            P(slab, "x", None),
            P(),
        ),
        out_specs=(P(None, None, None, slab, "x", None), P()),
        check_vma=False,
    )
```

```python
import functools

import jax
import jax.numpy as jnp
from jax import lax
from jax.experimental import pallas as pl
from jax.experimental.pallas import tpu as pltpu
from jax.sharding import PartitionSpec as P

AXES = ("y", "z", "core", "x")
ABSORB = 4.0
CURL_CENTRE = 5.0
VMEM_LIMIT = 40 * 1024 * 1024


def call(body, out_shape, operands, smem=(), hbm=(), hbm_out=(), scratch=()):
    special = {**{i: pltpu.SMEM for i in smem}, **{i: pltpu.HBM for i in hbm}}
    specs = [
        pl.BlockSpec(memory_space=special.get(i, pltpu.VMEM)) for i in range(len(operands))
    ]
    outs = [
        pl.BlockSpec(memory_space=pltpu.HBM if i in hbm_out else pltpu.VMEM)
        for i in range(len(out_shape))
    ]
    return pl.pallas_call(
        body,
        out_shape=out_shape,
        in_specs=specs,
        out_specs=outs,
        scratch_shapes=list(scratch),
        compiler_params=pltpu.CompilerParams(vmem_limit_bytes=VMEM_LIMIT),
    )(
        *(
            pltpu.with_memory_space_constraint(a, pltpu.HBM) if i in hbm else a
            for i, a in enumerate(operands)
        )
    )


def shape(*dims):
    return jax.ShapeDtypeStruct(dims, jnp.float32)


class Halo:
    def __init__(self, zs, xs):
        self.zs, self.xs = zs, xs
        self.first = set()
        for c in range(3):
            for z in range(zs):
                for x in range(xs):
                    self.first.add((c, z, x))
                    self.first |= reach(c, z, x)
        cells = set(self.first)
        for cell in self.first:
            cells |= reach(*cell)
        self.edge = set()
        for c, z, x in cells:
            side = self.side(z, x)
            if side[0] and side[1]:
                self.edge.add((c, z, x - side[1] * xs))
        cells |= self.edge
        self.names = [
            ("edge", -1, 0),
            ("edge", 1, 0),
            ("main", -1, 0),
            ("main", 1, 0),
            ("x", 0, -1),
            ("x", 0, 1),
        ]
        near = {q[1:] for q in self.first}
        self.blocks = {n: sorted(q for q in cells if self.name(*q) == n) for n in self.names}
        self.diagonal = {n: sorted(q for q in near if self.row_name(*q) == n) for n in self.names}

    def side(self, z, x):
        return (
            -1 if z < 0 else int(z >= self.zs),
            -1 if x < 0 else int(x >= self.xs),
        )

    def name(self, c, z, x):
        dz, dx = self.side(z, x)
        if dx:
            return ("x", 0, dx)
        if dz:
            return ("edge" if (c, z, x) in self.edge else "main", dz, 0)
        return None

    def row_name(self, z, x):
        dz, dx = self.side(z, x)
        if dx:
            return ("x", 0, dx)
        return ("edge", dz, 0) if dz else None

    def own(self, name, z, x):
        return z - name[1] * self.zs, x - name[2] * self.xs

    def rows(self, name, width):
        return len(self.blocks[name]) * width + (8 if self.diagonal[name] else 0)

    def block_row(self, c, z, x, width):
        return self.blocks[self.name(c, z, x)].index((c, z, x)) * width

    def diagonal_row(self, z, x, width):
        name = self.row_name(z, x)
        return len(self.blocks[name]) * width + self.diagonal[name].index((z, x))


CURL = (
    lambda z, x: {(2, z, x), (1, z + 1, x), (1, z, x)},
    lambda z, x: {(0, z + 1, x), (0, z, x), (2, z, x + 1), (2, z, x)},
    lambda z, x: {(1, z, x + 1), (1, z, x), (0, z, x)},
)
BACK = (
    lambda z, x: {(2, z, x), (1, z, x), (1, z - 1, x)},
    lambda z, x: {(0, z, x), (0, z - 1, x), (2, z, x), (2, z, x - 1)},
    lambda z, x: {(1, z, x), (1, z, x - 1), (0, z, x)},
)


def reach(c, z, x):
    cells = {(c, z, x)}
    for k, hz, hx in BACK[c](z, x):
        cells |= CURL[k](hz, hx)
    return cells


def stencil(e, lane, last):
    known = {}

    def step_y(value):
        return jnp.where(lane == last, 0.0, pltpu.roll(value, last, 1)) - value

    def h(k, z, x):
        if (k, z, x) not in known:
            if k == 0:
                value = step_y(e(2, z, x)) - (e(1, z + 1, x) - e(1, z, x))
            elif k == 1:
                value = (e(0, z + 1, x) - e(0, z, x)) - (e(2, z, x + 1) - e(2, z, x))
            else:
                value = (e(1, z, x + 1) - e(1, z, x)) - step_y(e(0, z, x))
            known[k, z, x] = value
        return known[k, z, x]

    def result(c, z, x):
        if c == 0:
            here = h(2, z, x)
            before = jnp.where(lane == 0, -e(0, z, x), pltpu.roll(here, 1, 1))
            return (here - before) - (h(1, z, x) - h(1, z - 1, x))
        if c == 1:
            return (h(0, z, x) - h(0, z - 1, x)) - (h(2, z, x) - h(2, z, x - 1))
        here = h(0, z, x)
        before = jnp.where(lane == 0, e(2, z, x), pltpu.roll(here, 1, 1))
        return (h(1, z, x) - h(1, z, x - 1)) - (here - before)

    return result


def split_body(halo, width, classes, eps, material, mask, start, field, diag, *refs):
    zs, xs = halo.zs, halo.xs
    rows = 3 * zs * xs
    messages, (start_in, material_in, mask_in, eps_in, sems) = refs[:2], refs[2:]
    copies = [
        pltpu.make_async_copy(source, target, sems.at[i])
        for i, (source, target) in enumerate(
            [(eps, eps_in), (material, material_in), (mask, mask_in), (start, start_in)]
        )
    ]
    for copy in copies:
        copy.start()
    for copy in copies[:3]:
        copy.wait()
    eps = eps_in
    total = eps[0]
    for level in range(1, classes):
        total = total + eps[level]
    shift = total / classes + CURL_CENTRE
    value = jnp.zeros(material_in.shape, jnp.float32)
    for level in range(classes):
        value = value + jnp.where(material_in[...] == level, eps[level], 0.0)
    diag[...] = value + ABSORB * mask_in[...].astype(jnp.float32) - shift

    places = {}
    for name, message in zip(halo.names, messages):
        for c, z, x in halo.blocks[name]:
            row = halo.block_row(c, z, x, width)
            places.setdefault((c, *halo.own(name, z, x)), []).append((message, row))
        fill_rows(halo, name, message, width, lambda z, x: diag[z, x : x + 1, :])
    copies[3].wait()
    for z in range(zs):
        for c in range(3):
            for x in range(xs):
                cell = start_in[pl.ds((c * zs + z) * xs + x, width, stride=rows), :]
                field[z, c, x] = cell
                for message, row in places.get((c, z, x), ()):
                    message[row : row + width, :] = cell


def fill_rows(halo, name, message, width, row_of):
    if halo.diagonal[name]:
        base = len(halo.blocks[name]) * width
        message[base : base + 8, :] = jnp.zeros((8, message.shape[1]), jnp.float32)
    for z, x in halo.diagonal[name]:
        row = halo.diagonal_row(z, x, width)
        message[row : row + 1, :] = row_of(*halo.own(name, z, x))


def across_body(halo, width, field, diag, before, after, *messages):
    edges = {-1: before, 1: after}

    def row_of(z, x):
        dz = halo.side(z, x)[0]
        if dz == 0:
            return diag[z, x : x + 1, :]
        row = halo.diagonal_row(z, x, width)
        return edges[dz][row : row + 1, :]

    for name, message in zip(halo.names[2:], messages):
        for c, z, x in halo.blocks[name]:
            row = halo.block_row(c, z, x, width)
            z, x = halo.own(name, z, x)
            dz = halo.side(z, x)[0]
            if dz == 0:
                message[row : row + width, :] = field[z, c, x]
            else:
                at = halo.block_row(c, z, x, width)
                message[row : row + width, :] = edges[dz][at : at + width, :]
        fill_rows(halo, name, message, width, row_of)


def parts(value, count):
    found, rest = [], value
    for i in range(count):
        found.append(rest.astype(jnp.bfloat16))
        if i + 1 < count:
            rest = rest - found[-1].astype(jnp.float32)
    return found


def pair(ref, z, c, x):
    return jnp.concatenate([ref[z, c, x], ref[z, c, x + 1]], axis=1)


def product(left, right, contract):
    return lax.dot_general(
        left, right, (((1,), (contract,)), ((), ())), preferred_element_type=jnp.float32
    )


def fold(total, left, right):
    rows = total[:left] + total[left : 2 * left] + total[2 * left :]
    return rows[:, :right] + rows[:, right : 2 * right] + rows[:, 2 * right :]


def cell_pairs(zs, xs):
    return [(z, c, x) for z in range(zs) for c in range(3) for x in range(0, xs, 2)]


def start_gram_body(zs, xs, s0, out):
    total = None
    for z, c, x in cell_pairs(zs, xs):
        stack = jnp.concatenate(parts(pair(s0, z, c, x), 3), axis=0)
        term = product(stack, stack, 1)
        total = term if total is None else total + term
    out[...] = fold(total, *out.shape)


def apply_body(halo, width, ny, slabs, trans, s0, diag, gram, *refs):
    zs, xs = halo.zs, halo.xs
    messages = dict(zip(halo.names, refs[:6]))
    basis, moments, s1, s2, outer = refs[6:]
    slab, across = lax.axis_index(AXES[:3]), lax.axis_index("x")
    held_z = {-1: slab > 0, 0: slab >= 0, 1: slab < slabs - 1}
    held_x = {-1: across > 0, 0: across >= 0, 1: across < trans - 1}
    inside = {
        (i, j): jnp.where(jnp.logical_and(held_z[i], held_x[j]), 1.0, 0.0)
        for i in (-1, 0, 1)
        for j in (-1, 0, 1)
    }
    extra = sorted(q for q in halo.first if halo.side(q[1], q[2]) != (0, 0))
    extra = {q: i for i, q in enumerate(extra)}
    lane = lax.broadcasted_iota(jnp.int32, (8, ny), 1)

    def diagonal(z, x):
        name = halo.row_name(z, x)
        if name is None:
            return diag[z, x : x + 1, :]
        row = halo.diagonal_row(z, x, width)
        return messages[name][row : row + 1, :]

    def group(at):
        def start(c, z, x):
            name = halo.name(c, z, x)
            if name is None:
                return s0[z, c, x, pl.ds(at, 8), :]
            row = halo.block_row(c, z, x, width)
            return messages[name][pl.ds(row + at, 8), :] * inside[halo.side(z, x)]

        def once(c, z, x):
            if halo.side(z, x) == (0, 0):
                return s1[z, c, x, pl.ds(at, 8), :]
            return outer[extra[c, z, x]]

        apply = stencil(start, lane, ny - 1)
        for x in range(-1, xs + 1):
            for z in range(-1, zs + 1):
                for c in range(3):
                    if (c, z, x) not in halo.first:
                        continue
                    value = apply(c, z, x) + diagonal(z, x) * start(c, z, x)
                    side = halo.side(z, x)
                    if side == (0, 0):
                        s1[z, c, x, pl.ds(at, 8), :] = value
                    else:
                        outer[extra[c, z, x]] = value * inside[side]
        apply = stencil(once, lane, ny - 1)
        for x in range(xs):
            for z in range(zs):
                for c in range(3):
                    value = apply(c, z, x) + diagonal(z, x) * once(c, z, x)
                    s2[z, c, x, pl.ds(at, 8), :] = value

    for at in range(0, width, 8):
        group(at)

    total = None
    for i, (z, c, x) in enumerate(cell_pairs(zs, xs)):
        k0, k1, k2 = (parts(pair(s, z, c, x), 3) for s in (s0, s1, s2))
        basis[i] = jnp.concatenate([k0[0], k1[0], k0[1], k1[1], k2[0], k2[1]], axis=0)
        left = jnp.concatenate([p for three in zip(k0, k1, k2) for p in three], axis=0)
        right = jnp.concatenate([p for two in zip(k1, k2) for p in two], axis=0)
        term = product(left, right, 1)
        total = term if total is None else total + term
    found = fold(total, 3 * width, 2 * width)
    w = width
    found = [
        gram[...],
        found[:w, :w],
        found[w : 2 * w, :w],
        found[w : 2 * w, w:],
        found[2 * w :, w:],
    ]
    for k, m in enumerate(found):
        for j in range(w // 8):
            moments[8 * k : 8 * k + 8, w * j : w * j + w] = m[8 * j : 8 * j + 8]


def precise(left, right, contract):
    return lax.dot_general(
        left,
        right,
        (((1,), (contract,)), ((), ())),
        precision=lax.Precision.HIGHEST,
        preferred_element_type=jnp.float32,
    )


def factor(gram, size, pauses):
    tiles = size // 8
    lane = lax.broadcasted_iota(jnp.int32, (8, size), 1)
    sub = lax.broadcasted_iota(jnp.int32, (8, size), 0)
    upper = [gram[8 * t : 8 * t + 8, :] for t in range(tiles)]
    inverse = [jnp.where(lane == sub + 8 * t, 1.0, 0.0) for t in range(tiles)]
    found_u, found_i = [], []

    def column(u, j):
        return jnp.broadcast_to(upper[u][:, j : j + 1], (8, size))

    ahead = [column(0, j) for j in range(8)]
    for t in range(tiles):
        cols = {u: [column(u, 8 * t + j) for j in range(8)] for u in range(t + 1, tiles)}
        cols[t] = ahead
        if t + 1 < tiles:
            ahead = [column(t + 1, 8 * t + 8 + j) for j in range(8)]
        pivots = jnp.zeros((8, size), jnp.float32)
        for s in range(8):
            pivot = jnp.broadcast_to(cols[t][s][s : s + 1, :], (8, size))
            pivots = jnp.where(sub == s, pivot, pivots)
            reciprocal = 1.0 / pivot
            heads = [cols[t][j][s : s + 1, :] for j in range(8)]
            row_u, row_i = upper[t][s : s + 1, :], inverse[t][s : s + 1, :]
            for u in range(t, tiles):
                f = cols[u][s] * reciprocal
                if u == t:
                    f = jnp.where(sub > s, f, 0.0)
                if u == t + 1:
                    for j in range(8):
                        ahead[j] = ahead[j] - f * cols[u][s][j : j + 1, :]
                for j in range(s + 1, 8):
                    cols[u][j] = cols[u][j] - f * heads[j]
                upper[u] = upper[u] - f * row_u
                inverse[u] = inverse[u] - f * row_i
        scale = lax.rsqrt(pivots)
        found_u.append(upper[t] * scale)
        found_i.append(inverse[t] * scale)
        if t + 1 in pauses:
            yield jnp.concatenate(found_u, axis=0), jnp.concatenate(found_i, axis=0)


def last_body(zs, xs, width, ny, classes, entries, eps, moments, basis, out, couplings, *scratch):
    w = width
    staged, sems = scratch
    total = eps[0]
    for level in range(1, classes):
        total = total + eps[level]
    shift = total / classes + CURL_CENTRE
    m = []
    summed = moments[0]
    for i in range(1, moments.shape[0]):
        summed = summed + moments[i]
    for k in range(5):
        rows = summed[8 * k : 8 * k + 8, :] * (1.0 / entries)
        m.append(jnp.concatenate([rows[:, w * j : w * j + w] for j in range(w // 8)], axis=0))
    gram = jnp.concatenate(
        [jnp.concatenate([m[i + j] for j in range(3)], axis=1) for i in range(3)], axis=0
    )
    rows = 3 * zs * xs

    def combine(block, mix, depth):
        for i, (z, c, x) in enumerate(cell_pairs(zs, xs)):
            terms = product(mix, basis[i, :depth], 0)
            value = terms[:w] + terms[w : 2 * w] + terms[2 * w :]
            for k in range(2):
                at = (c * zs + z) * xs + x + k
                staged[block, pl.ds(at, w, stride=rows), :] = value[:, k * ny : (k + 1) * ny]
        copy = pltpu.make_async_copy(staged.at[block], out.at[block], sems.at[block])
        copy.start()
        return copy

    steps = factor(gram, 3 * w, (w // 4, 3 * w // 8))
    upper, inverse = next(steps)
    mix = [jnp.concatenate([p, p], axis=1) for p in parts(inverse[w:, : 2 * w], 3)]
    copies = [combine(0, jnp.concatenate(mix, axis=0), 4 * w)]
    upper, inverse = next(steps)
    mix = [
        jnp.concatenate([p[:, : 2 * w], p[:, : 2 * w], p[:, 2 * w :], p[:, 2 * w :]], axis=1)
        for p in parts(inverse[2 * w :], 3)
    ]
    copies.append(combine(1, jnp.concatenate(mix, axis=0), 6 * w))
    identity = jnp.where(
        lax.broadcasted_iota(jnp.int32, (w, w), 0) == lax.broadcasted_iota(jnp.int32, (w, w), 1),
        shift,
        0.0,
    )
    x0, x1 = inverse[:w, :w], inverse[w : 2 * w, w : 2 * w]
    u01, u11 = upper[:w, w : 2 * w], upper[w : 2 * w, w : 2 * w]
    u12, u22 = upper[w : 2 * w, 2 * w :], upper[2 * w :, 2 * w :]
    factor_one = precise(u11, x0, 1)
    couplings[0, 0] = precise(u01, x0, 1) + identity
    couplings[0, 1] = factor_one
    couplings[1, 0] = precise(u12 - precise(factor_one, u01, 0), x1, 1) + identity
    couplings[1, 1] = precise(u22, x1, 1)
    for copy in copies:
        copy.wait()


def moved(name, value, slabs, trans):
    _, dz, dx = name
    pairs = [
        (i * trans + j, (i - dz) % slabs * trans + (j - dx) % trans)
        for i in range(slabs)
        for j in range(trans)
    ]
    return lax.ppermute(value, AXES, pairs)


def total_sum(value, deep, trans, devices):
    core, near = trans, 2 * trans
    rounds = [(core, near, core ^ near)]
    if deep == 8:
        middle, far = 4 * trans, 8 * trans
        rounds.append((middle, far ^ near, far ^ middle))
    for masks in rounds:
        one, two, three = (
            lax.ppermute(value, AXES, [(i, i ^ m) for i in range(devices)]) for m in masks
        )
        value = (value + one) + (two + three)
    count = devices // (2 * deep)
    copies = jnp.broadcast_to(value[None], (count, *value.shape))
    return lax.all_to_all(copies, ("y", "x"), 0, 0, tiled=True)


def per_device(slabs, deep, trans, start_block, material, pml_mask, eps_table):
    width, _, zs, xs, ny = start_block.shape
    classes = eps_table.shape[0]
    entries = float(3 * zs * xs * ny * slabs * trans)
    field = shape(zs, 3, xs, width, ny)
    rows = width * 3 * zs * xs
    halo = Halo(zs, xs)

    s0, diag, *messages = call(
        functools.partial(split_body, halo, width, classes),
        [field, shape(zs, xs, ny)] + [shape(halo.rows(n, width), ny) for n in halo.names[:2]],
        [eps_table, material, pml_mask, start_block.reshape(rows, ny)],
        hbm=(0, 1, 2, 3),
        scratch=[
            pltpu.VMEM((rows, ny), jnp.float32),
            pltpu.VMEM((zs, xs, ny), jnp.int32),
            pltpu.VMEM((zs, xs, ny), jnp.int32),
            pltpu.SMEM((classes,), jnp.float32),
            pltpu.SemaphoreType.DMA((4,)),
        ],
    )
    messages = [moved(n, m, slabs, trans) for n, m in zip(halo.names, messages)]
    others = call(
        functools.partial(across_body, halo, width),
        [shape(halo.rows(n, width), ny) for n in halo.names[2:]],
        [s0, diag] + messages,
    )
    messages += [moved(n, m, slabs, trans) for n, m in zip(halo.names[2:], others)]
    (gram,) = call(functools.partial(start_gram_body, zs, xs), [shape(width, width)], [s0])
    outside = len(halo.first) - 3 * zs * xs
    basis, moments = call(
        functools.partial(apply_body, halo, width, ny, slabs, trans),
        [
            jax.ShapeDtypeStruct((len(cell_pairs(zs, xs)), 6 * width, 2 * ny), jnp.bfloat16),
            shape(40, 4 * width),
        ],
        [s0, diag, gram] + messages,
        scratch=[
            pltpu.VMEM(field.shape, jnp.float32),
            pltpu.VMEM(field.shape, jnp.float32),
            pltpu.VMEM((outside, 8, ny), jnp.float32),
        ],
    )
    moments = total_sum(moments, deep, trans, slabs * trans)
    blocks, couplings = call(
        functools.partial(last_body, zs, xs, width, ny, classes, entries),
        [shape(2, rows, ny), shape(2, 2, width, width)],
        [eps_table, moments, basis],
        smem=(0,),
        hbm_out=(0,),
        scratch=[pltpu.VMEM((2, rows, ny), jnp.float32), pltpu.SemaphoreType.DMA((2,))],
    )
    return blocks.reshape(2, width, 3, zs, xs, ny), couplings


def solution(mesh):
    slabs, trans = mesh.devices.shape
    deep = 8 if slabs == 64 else 2
    sizes = (slabs // (2 * deep), deep, 2, trans)
    split = jax.sharding.Mesh(mesh.devices.reshape(sizes), AXES)
    slab = AXES[:3]
    return jax.shard_map(
        functools.partial(per_device, slabs, deep, trans),
        mesh=split,
        in_specs=(
            P(None, None, slab, "x", None),
            P(slab, "x", None),
            P(slab, "x", None),
            P(),
        ),
        out_specs=(P(None, None, None, slab, "x", None), P()),
        check_vma=False,
    )
```

```python
import functools

import jax
import jax.numpy as jnp
from jax import lax
from jax.experimental import pallas as pl
from jax.experimental.pallas import tpu as pltpu
from jax.sharding import PartitionSpec as P

AXES = ("y", "z", "core", "x")
ABSORB = 4.0
CURL_CENTRE = 5.0
VMEM_LIMIT = 40 * 1024 * 1024


def call(body, out_shape, operands, smem=(), hbm=(), hbm_out=(), scratch=()):
    special = {**{i: pltpu.SMEM for i in smem}, **{i: pltpu.HBM for i in hbm}}
    specs = [
        pl.BlockSpec(memory_space=special.get(i, pltpu.VMEM)) for i in range(len(operands))
    ]
    outs = [
        pl.BlockSpec(memory_space=pltpu.HBM if i in hbm_out else pltpu.VMEM)
        for i in range(len(out_shape))
    ]
    return pl.pallas_call(
        body,
        out_shape=out_shape,
        in_specs=specs,
        out_specs=outs,
        scratch_shapes=list(scratch),
        compiler_params=pltpu.CompilerParams(vmem_limit_bytes=VMEM_LIMIT),
    )(
        *(
            pltpu.with_memory_space_constraint(a, pltpu.HBM) if i in hbm else a
            for i, a in enumerate(operands)
        )
    )


def shape(*dims):
    return jax.ShapeDtypeStruct(dims, jnp.float32)


class Halo:
    def __init__(self, zs, xs):
        self.zs, self.xs = zs, xs
        self.first = set()
        for c in range(3):
            for z in range(zs):
                for x in range(xs):
                    self.first.add((c, z, x))
                    self.first |= reach(c, z, x)
        cells = set(self.first)
        for cell in self.first:
            cells |= reach(*cell)
        self.names = [(0, -1), (0, 1), (-1, 0), (1, 0), (-1, 2), (1, 2)]
        self.blocks, self.diagonal = {}, {}
        for name in self.names:
            self.blocks[name] = sorted(q for q in cells if self.name(q[1], q[2]) == name)
            near = {q[1:] for q in self.first if self.name(q[1], q[2]) == name}
            self.diagonal[name] = sorted(near)

    def name(self, z, x):
        side = self.side(z, x)
        return (side[0], 2) if side[0] and side[1] else side

    def side(self, z, x):
        return (
            -1 if z < 0 else int(z >= self.zs),
            -1 if x < 0 else int(x >= self.xs),
        )

    def own(self, name, z, x):
        return z - name[0] * self.zs, x - name[1] % 2 * name[1] * self.xs

    def rows(self, name, width):
        return len(self.blocks[name]) * width + 8

    def block_row(self, name, c, z, x, width):
        return self.blocks[name].index((c, z, x)) * width

    def diagonal_row(self, name, z, x, width):
        return len(self.blocks[name]) * width + self.diagonal[name].index((z, x))


CURL = (
    lambda z, x: {(2, z, x), (1, z + 1, x), (1, z, x)},
    lambda z, x: {(0, z + 1, x), (0, z, x), (2, z, x + 1), (2, z, x)},
    lambda z, x: {(1, z, x + 1), (1, z, x), (0, z, x)},
)
BACK = (
    lambda z, x: {(2, z, x), (1, z, x), (1, z - 1, x)},
    lambda z, x: {(0, z, x), (0, z - 1, x), (2, z, x), (2, z, x - 1)},
    lambda z, x: {(1, z, x), (1, z, x - 1), (0, z, x)},
)


def reach(c, z, x):
    cells = {(c, z, x)}
    for k, hz, hx in BACK[c](z, x):
        cells |= CURL[k](hz, hx)
    return cells


def stencil(e, lane, last):
    known = {}

    def step_y(value):
        return jnp.where(lane == last, 0.0, pltpu.roll(value, last, 1)) - value

    def h(k, z, x):
        if (k, z, x) not in known:
            if k == 0:
                value = step_y(e(2, z, x)) - (e(1, z + 1, x) - e(1, z, x))
            elif k == 1:
                value = (e(0, z + 1, x) - e(0, z, x)) - (e(2, z, x + 1) - e(2, z, x))
            else:
                value = (e(1, z, x + 1) - e(1, z, x)) - step_y(e(0, z, x))
            known[k, z, x] = value
        return known[k, z, x]

    def result(c, z, x):
        if c == 0:
            here = h(2, z, x)
            before = jnp.where(lane == 0, -e(0, z, x), pltpu.roll(here, 1, 1))
            return (here - before) - (h(1, z, x) - h(1, z - 1, x))
        if c == 1:
            return (h(0, z, x) - h(0, z - 1, x)) - (h(2, z, x) - h(2, z, x - 1))
        here = h(0, z, x)
        before = jnp.where(lane == 0, e(2, z, x), pltpu.roll(here, 1, 1))
        return (h(1, z, x) - h(1, z, x - 1)) - (here - before)

    return result


def split_body(halo, width, classes, eps, material, mask, start, field, diag, *refs):
    zs, xs = halo.zs, halo.xs
    rows = 3 * zs * xs
    messages, (start_in, material_in, mask_in, eps_in, sems) = refs[:4], refs[4:]
    pairs = [(eps, eps_in), (material, material_in), (mask, mask_in)]
    for g in range(0, width, 8):
        part = pl.ds(g * rows, 8 * rows)
        pairs.append((start.at[part], start_in.at[part]))
    copies = [
        pltpu.make_async_copy(source, target, sems.at[i])
        for i, (source, target) in enumerate(pairs)
    ]
    for copy in copies:
        copy.start()
    for copy in copies[:3]:
        copy.wait()
    eps = eps_in
    total = eps[0]
    for level in range(1, classes):
        total = total + eps[level]
    shift = total / classes + CURL_CENTRE
    value = jnp.zeros(material_in.shape, jnp.float32)
    for level in range(classes):
        value = value + jnp.where(material_in[...] == level, eps[level], 0.0)
    diag[...] = value + ABSORB * mask_in[...].astype(jnp.float32) - shift

    places = {}
    for name, message in zip(halo.names, messages):
        for c, z, x in halo.blocks[name]:
            row = halo.block_row(name, c, z, x, width)
            places.setdefault((c, *halo.own(name, z, x)), []).append((message, row))
        base = len(halo.blocks[name]) * width
        message[base : base + 8, :] = jnp.zeros((8, message.shape[1]), jnp.float32)
        for z, x in halo.diagonal[name]:
            row = halo.diagonal_row(name, z, x, width)
            oz, ox = halo.own(name, z, x)
            message[row : row + 1, :] = diag[oz, ox : ox + 1, :]
    for g in range(0, width, 8):
        copies[3 + g // 8].wait()
        for z in range(zs):
            for c in range(3):
                for x in range(xs):
                    at = g * rows + (c * zs + z) * xs + x
                    cell = start_in[pl.ds(at, 8, stride=rows), :]
                    field[z, c, x, g : g + 8] = cell
                    for message, row in places.get((c, z, x), ()):
                        message[row + g : row + g + 8, :] = cell


def relay_body(halo, width, before, after, *passed):
    received = {-1: ((0, -1), before), 1: ((0, 1), after)}
    for name, message in zip(halo.names[4:], passed):
        base = len(halo.blocks[name]) * width
        message[base : base + 8, :] = jnp.zeros((8, message.shape[1]), jnp.float32)
        for c, z, x in halo.blocks[name]:
            side, source = received[halo.side(z, x)[1]]
            at = halo.block_row(side, c, z - name[0] * halo.zs, x, width)
            row = halo.block_row(name, c, z, x, width)
            message[row : row + width, :] = source[at : at + width, :]
        for z, x in halo.diagonal[name]:
            side, source = received[halo.side(z, x)[1]]
            at = halo.diagonal_row(side, z - name[0] * halo.zs, x, width)
            row = halo.diagonal_row(name, z, x, width)
            message[row : row + 1, :] = source[at : at + 1, :]


def parts(value, count):
    found, rest = [], value
    for i in range(count):
        found.append(rest.astype(jnp.bfloat16))
        if i + 1 < count:
            rest = rest - found[-1].astype(jnp.float32)
    return found


def pair(ref, z, c, x):
    return jnp.concatenate([ref[z, c, x], ref[z, c, x + 1]], axis=1)


def product(left, right, contract):
    return lax.dot_general(
        left, right, (((1,), (contract,)), ((), ())), preferred_element_type=jnp.float32
    )


def fold(total, left, right):
    rows = total[:left] + total[left : 2 * left] + total[2 * left :]
    return rows[:, :right] + rows[:, right : 2 * right] + rows[:, 2 * right :]


def cell_pairs(zs, xs):
    return [(z, c, x) for z in range(zs) for c in range(3) for x in range(0, xs, 2)]


def start_gram_body(zs, xs, s0, out):
    total = None
    for z, c, x in cell_pairs(zs, xs):
        stack = jnp.concatenate(parts(pair(s0, z, c, x), 3), axis=0)
        term = product(stack, stack, 1)
        total = term if total is None else total + term
    out[...] = fold(total, *out.shape)


def apply_body(halo, width, ny, slabs, trans, s0, diag, gram, *refs):
    zs, xs = halo.zs, halo.xs
    messages = dict(zip(halo.names, refs[:6]))
    basis, moments, s1, s2, outer = refs[6:]
    slab, across = lax.axis_index(AXES[:3]), lax.axis_index("x")
    held_z = {-1: slab > 0, 0: slab >= 0, 1: slab < slabs - 1}
    held_x = {-1: across > 0, 0: across >= 0, 1: across < trans - 1}
    inside = {
        (i, j): jnp.where(jnp.logical_and(held_z[i], held_x[j]), 1.0, 0.0)
        for i in (-1, 0, 1)
        for j in (-1, 0, 1)
    }
    extra = sorted(q for q in halo.first if halo.side(q[1], q[2]) != (0, 0))
    extra = {q: i for i, q in enumerate(extra)}
    lane = lax.broadcasted_iota(jnp.int32, (8, ny), 1)

    def diagonal(z, x):
        name = halo.name(z, x)
        if name == (0, 0):
            return diag[z, x : x + 1, :]
        row = halo.diagonal_row(name, z, x, width)
        return messages[name][row : row + 1, :]

    def group(at):
        def start(c, z, x):
            name = halo.name(z, x)
            if name == (0, 0):
                return s0[z, c, x, pl.ds(at, 8), :]
            row = halo.block_row(name, c, z, x, width)
            return messages[name][pl.ds(row + at, 8), :] * inside[halo.side(z, x)]

        def once(c, z, x):
            if halo.side(z, x) == (0, 0):
                return s1[z, c, x, pl.ds(at, 8), :]
            return outer[extra[c, z, x]]

        apply = stencil(start, lane, ny - 1)
        for x in range(-1, xs + 1):
            for z in range(-1, zs + 1):
                for c in range(3):
                    if (c, z, x) not in halo.first:
                        continue
                    value = apply(c, z, x) + diagonal(z, x) * start(c, z, x)
                    side = halo.side(z, x)
                    if side == (0, 0):
                        s1[z, c, x, pl.ds(at, 8), :] = value
                    else:
                        outer[extra[c, z, x]] = value * inside[side]
        apply = stencil(once, lane, ny - 1)
        for x in range(xs):
            for z in range(zs):
                for c in range(3):
                    value = apply(c, z, x) + diagonal(z, x) * once(c, z, x)
                    s2[z, c, x, pl.ds(at, 8), :] = value

    for at in range(0, width, 8):
        group(at)

    total = None
    for i, (z, c, x) in enumerate(cell_pairs(zs, xs)):
        k0, k1, k2 = (parts(pair(s, z, c, x), 3) for s in (s0, s1, s2))
        basis[i] = jnp.concatenate([k0[0], k1[0], k0[1], k1[1], k2[0], k2[1]], axis=0)
        left = jnp.concatenate([p for three in zip(k0, k1, k2) for p in three], axis=0)
        right = jnp.concatenate([p for two in zip(k1, k2) for p in two], axis=0)
        term = product(left, right, 1)
        total = term if total is None else total + term
    found = fold(total, 3 * width, 2 * width)
    w = width
    found = [
        gram[...],
        found[:w, :w],
        found[w : 2 * w, :w],
        found[w : 2 * w, w:],
        found[2 * w :, w:],
    ]
    for k, m in enumerate(found):
        for j in range(w // 8):
            moments[8 * k : 8 * k + 8, w * j : w * j + w] = m[8 * j : 8 * j + 8]


def precise(left, right, contract):
    return lax.dot_general(
        left,
        right,
        (((1,), (contract,)), ((), ())),
        precision=lax.Precision.HIGHEST,
        preferred_element_type=jnp.float32,
    )


def factor(gram, size, pauses):
    tiles = size // 8
    lane = lax.broadcasted_iota(jnp.int32, (8, size), 1)
    sub = lax.broadcasted_iota(jnp.int32, (8, size), 0)
    upper = [gram[8 * t : 8 * t + 8, :] for t in range(tiles)]
    inverse = [jnp.where(lane == sub + 8 * t, 1.0, 0.0) for t in range(tiles)]
    found_u, found_i = [], []

    def column(u, j):
        return jnp.broadcast_to(upper[u][:, j : j + 1], (8, size))

    ahead = [column(0, j) for j in range(8)]
    for t in range(tiles):
        cols = {u: [column(u, 8 * t + j) for j in range(8)] for u in range(t + 1, tiles)}
        cols[t] = ahead
        if t + 1 < tiles:
            ahead = [column(t + 1, 8 * t + 8 + j) for j in range(8)]
        pivots = jnp.zeros((8, size), jnp.float32)
        for s in range(8):
            pivot = jnp.broadcast_to(cols[t][s][s : s + 1, :], (8, size))
            pivots = jnp.where(sub == s, pivot, pivots)
            reciprocal = 1.0 / pivot
            heads = [cols[t][j][s : s + 1, :] for j in range(8)]
            row_u, row_i = upper[t][s : s + 1, :], inverse[t][s : s + 1, :]
            for u in range(t, tiles):
                f = cols[u][s] * reciprocal
                if u == t:
                    f = jnp.where(sub > s, f, 0.0)
                if u == t + 1:
                    for j in range(8):
                        ahead[j] = ahead[j] - f * cols[u][s][j : j + 1, :]
                for j in range(s + 1, 8):
                    cols[u][j] = cols[u][j] - f * heads[j]
                upper[u] = upper[u] - f * row_u
                inverse[u] = inverse[u] - f * row_i
        scale = lax.rsqrt(pivots)
        found_u.append(upper[t] * scale)
        found_i.append(inverse[t] * scale)
        if t + 1 in pauses:
            yield jnp.concatenate(found_u, axis=0), jnp.concatenate(found_i, axis=0)


def last_body(zs, xs, width, ny, classes, entries, eps, moments, basis, out, couplings, *scratch):
    w = width
    staged, sems = scratch
    total = eps[0]
    for level in range(1, classes):
        total = total + eps[level]
    shift = total / classes + CURL_CENTRE
    m = []
    for k in range(5):
        rows = moments[8 * k : 8 * k + 8, :] * (1.0 / entries)
        m.append(jnp.concatenate([rows[:, w * j : w * j + w] for j in range(w // 8)], axis=0))
    gram = jnp.concatenate(
        [jnp.concatenate([m[i + j] for j in range(3)], axis=1) for i in range(3)], axis=0
    )
    rows = 3 * zs * xs

    flat = staged.reshape(2, w * rows, ny)

    def combine(block, mix, depth):
        found = []
        for i, (z, c, x) in enumerate(cell_pairs(zs, xs)):
            terms = product(mix, basis[i, :depth], 0)
            value = terms[:w] + terms[w : 2 * w] + terms[2 * w :]
            for k in range(2):
                at = (c * zs + z) * xs + x + k
                flat[block, pl.ds(at, w, stride=rows), :] = value[:, k * ny : (k + 1) * ny]
            if x == xs - 2:
                plane = c * zs + z
                source, target = staged.at[block, :, plane], out.at[block, :, plane]
                found.append(pltpu.make_async_copy(source, target, sems.at[block, plane]))
                found[-1].start()
        return found

    steps = factor(gram, 3 * w, (w // 4, 3 * w // 8))
    upper, inverse = next(steps)
    mix = [jnp.concatenate([p, p], axis=1) for p in parts(inverse[w:, : 2 * w], 3)]
    copies = combine(0, jnp.concatenate(mix, axis=0), 4 * w)
    upper, inverse = next(steps)
    mix = [
        jnp.concatenate([p[:, : 2 * w], p[:, : 2 * w], p[:, 2 * w :], p[:, 2 * w :]], axis=1)
        for p in parts(inverse[2 * w :], 3)
    ]
    copies += combine(1, jnp.concatenate(mix, axis=0), 6 * w)
    identity = jnp.where(
        lax.broadcasted_iota(jnp.int32, (w, w), 0) == lax.broadcasted_iota(jnp.int32, (w, w), 1),
        shift,
        0.0,
    )
    x0, x1 = inverse[:w, :w], inverse[w : 2 * w, w : 2 * w]
    u01, u11 = upper[:w, w : 2 * w], upper[w : 2 * w, w : 2 * w]
    u12, u22 = upper[w : 2 * w, 2 * w :], upper[2 * w :, 2 * w :]
    factor_one = precise(u11, x0, 1)
    couplings[0, 0] = precise(u01, x0, 1) + identity
    couplings[0, 1] = factor_one
    couplings[1, 0] = precise(u12 - precise(factor_one, u01, 0), x1, 1) + identity
    couplings[1, 1] = precise(u22, x1, 1)
    for copy in copies:
        copy.wait()


def moved(name, value, slabs, trans):
    dz, dx = name[0], name[1] % 2 * name[1]
    pairs = [
        (i * trans + j, (i - dz) % slabs * trans + (j - dx) % trans)
        for i in range(slabs)
        for j in range(trans)
    ]
    return lax.ppermute(value, AXES, pairs)


def total_sum(value, deep, trans, devices):
    count = devices // (2 * deep)
    copies = jnp.broadcast_to(value[None], (count, *value.shape))
    value = lax.all_to_all(copies, ("y", "x"), 0, 0, tiled=True).sum(0)
    core, near, middle, far = trans, 2 * trans, 4 * trans, 8 * trans
    rounds = [(middle, far ^ near, far ^ middle)] if deep == 8 else []
    rounds.append((core, near, core ^ near))
    for masks in rounds:
        one, two, three = (
            lax.ppermute(value, AXES, [(i, i ^ m) for i in range(devices)]) for m in masks
        )
        value = (value + one) + (two + three)
    return value


def per_device(slabs, deep, trans, start_block, material, pml_mask, eps_table):
    width, _, zs, xs, ny = start_block.shape
    classes = eps_table.shape[0]
    entries = float(3 * zs * xs * ny * slabs * trans)
    field = shape(zs, 3, xs, width, ny)
    rows = width * 3 * zs * xs
    halo = Halo(zs, xs)

    s0, diag, *messages = call(
        functools.partial(split_body, halo, width, classes),
        [field, shape(zs, xs, ny)] + [shape(halo.rows(n, width), ny) for n in halo.names[:4]],
        [eps_table, material, pml_mask, start_block.reshape(rows, ny)],
        hbm=(0, 1, 2, 3),
        scratch=[
            pltpu.VMEM((rows, ny), jnp.float32),
            pltpu.VMEM((zs, xs, ny), jnp.int32),
            pltpu.VMEM((zs, xs, ny), jnp.int32),
            pltpu.SMEM((classes,), jnp.float32),
            pltpu.SemaphoreType.DMA((3 + width // 8,)),
        ],
    )
    messages = [moved(n, m, slabs, trans) for n, m in zip(halo.names, messages)]
    passed = call(
        functools.partial(relay_body, halo, width),
        [shape(halo.rows(n, width), ny) for n in halo.names[4:]],
        messages[:2],
    )
    messages += [moved(n, m, slabs, trans) for n, m in zip(halo.names[4:], passed)]
    (gram,) = call(functools.partial(start_gram_body, zs, xs), [shape(width, width)], [s0])
    outside = len(halo.first) - 3 * zs * xs
    basis, moments = call(
        functools.partial(apply_body, halo, width, ny, slabs, trans),
        [
            jax.ShapeDtypeStruct((len(cell_pairs(zs, xs)), 6 * width, 2 * ny), jnp.bfloat16),
            shape(40, 4 * width),
        ],
        [s0, diag, gram] + messages,
        scratch=[
            pltpu.VMEM(field.shape, jnp.float32),
            pltpu.VMEM(field.shape, jnp.float32),
            pltpu.VMEM((outside, 8, ny), jnp.float32),
        ],
    )
    moments = total_sum(moments, deep, trans, slabs * trans)
    blocks, couplings = call(
        functools.partial(last_body, zs, xs, width, ny, classes, entries),
        [shape(2, width, 3 * zs, xs, ny), shape(2, 2, width, width)],
        [eps_table, moments, basis],
        smem=(0,),
        hbm_out=(0,),
        scratch=[
            pltpu.VMEM((2, width, 3 * zs, xs, ny), jnp.float32),
            pltpu.SemaphoreType.DMA((2, 3 * zs)),
        ],
    )
    return blocks.reshape(2, width, 3, zs, xs, ny), couplings


def solution(mesh):
    slabs, trans = mesh.devices.shape
    deep = 8 if slabs == 64 else 2
    sizes = (slabs // (2 * deep), deep, 2, trans)
    split = jax.sharding.Mesh(mesh.devices.reshape(sizes), AXES)
    slab = AXES[:3]
    return jax.shard_map(
        functools.partial(per_device, slabs, deep, trans),
        mesh=split,
        in_specs=(
            P(None, None, slab, "x", None),
            P(slab, "x", None),
            P(slab, "x", None),
            P(),
        ),
        out_specs=(P(None, None, None, slab, "x", None), P()),
        check_vma=False,
    )
```

```python
import functools

import jax
import jax.numpy as jnp
from jax import lax
from jax.experimental import pallas as pl
from jax.experimental.pallas import tpu as pltpu
from jax.sharding import PartitionSpec as P

AXES = ("y", "z", "core", "x")
ABSORB = 4.0
CURL_CENTRE = 5.0
VMEM_LIMIT = 40 * 1024 * 1024


def call(body, out_shape, operands, smem=(), hbm=(), hbm_out=(), scratch=()):
    special = {**{i: pltpu.SMEM for i in smem}, **{i: pltpu.HBM for i in hbm}}
    specs = [
        pl.BlockSpec(memory_space=special.get(i, pltpu.VMEM)) for i in range(len(operands))
    ]
    outs = [
        pl.BlockSpec(memory_space=pltpu.HBM if i in hbm_out else pltpu.VMEM)
        for i in range(len(out_shape))
    ]
    return pl.pallas_call(
        body,
        out_shape=out_shape,
        in_specs=specs,
        out_specs=outs,
        scratch_shapes=list(scratch),
        compiler_params=pltpu.CompilerParams(vmem_limit_bytes=VMEM_LIMIT),
    )(
        *(
            pltpu.with_memory_space_constraint(a, pltpu.HBM) if i in hbm else a
            for i, a in enumerate(operands)
        )
    )


def shape(*dims):
    return jax.ShapeDtypeStruct(dims, jnp.float32)


class Halo:
    def __init__(self, zs, xs):
        self.zs, self.xs = zs, xs
        self.first = set()
        for c in range(3):
            for z in range(zs):
                for x in range(xs):
                    self.first.add((c, z, x))
                    self.first |= reach(c, z, x)
        cells = set(self.first)
        for cell in self.first:
            cells |= reach(*cell)
        self.names = [(0, -1), (0, 1), (-1, 0), (1, 0), (-1, 2), (1, 2)]
        self.blocks, self.diagonal = {}, {}
        for name in self.names:
            self.blocks[name] = sorted(q for q in cells if self.name(q[1], q[2]) == name)
            near = {q[1:] for q in self.first if self.name(q[1], q[2]) == name}
            self.diagonal[name] = sorted(near)

    def name(self, z, x):
        side = self.side(z, x)
        return (side[0], 2) if side[0] and side[1] else side

    def side(self, z, x):
        return (
            -1 if z < 0 else int(z >= self.zs),
            -1 if x < 0 else int(x >= self.xs),
        )

    def own(self, name, z, x):
        return z - name[0] * self.zs, x - name[1] % 2 * name[1] * self.xs

    def rows(self, name, width):
        return len(self.blocks[name]) * width + 8

    def block_row(self, name, c, z, x, width):
        return self.blocks[name].index((c, z, x)) * width

    def diagonal_row(self, name, z, x, width):
        return len(self.blocks[name]) * width + self.diagonal[name].index((z, x))


CURL = (
    lambda z, x: {(2, z, x), (1, z + 1, x), (1, z, x)},
    lambda z, x: {(0, z + 1, x), (0, z, x), (2, z, x + 1), (2, z, x)},
    lambda z, x: {(1, z, x + 1), (1, z, x), (0, z, x)},
)
BACK = (
    lambda z, x: {(2, z, x), (1, z, x), (1, z - 1, x)},
    lambda z, x: {(0, z, x), (0, z - 1, x), (2, z, x), (2, z, x - 1)},
    lambda z, x: {(1, z, x), (1, z, x - 1), (0, z, x)},
)


def reach(c, z, x):
    cells = {(c, z, x)}
    for k, hz, hx in BACK[c](z, x):
        cells |= CURL[k](hz, hx)
    return cells


def stencil(e, lane, last):
    known = {}

    def step_y(value):
        return jnp.where(lane == last, 0.0, pltpu.roll(value, last, 1)) - value

    def h(k, z, x):
        if (k, z, x) not in known:
            if k == 0:
                value = step_y(e(2, z, x)) - (e(1, z + 1, x) - e(1, z, x))
            elif k == 1:
                value = (e(0, z + 1, x) - e(0, z, x)) - (e(2, z, x + 1) - e(2, z, x))
            else:
                value = (e(1, z, x + 1) - e(1, z, x)) - step_y(e(0, z, x))
            known[k, z, x] = value
        return known[k, z, x]

    def result(c, z, x):
        if c == 0:
            here = h(2, z, x)
            before = jnp.where(lane == 0, -e(0, z, x), pltpu.roll(here, 1, 1))
            return (here - before) - (h(1, z, x) - h(1, z - 1, x))
        if c == 1:
            return (h(0, z, x) - h(0, z - 1, x)) - (h(2, z, x) - h(2, z, x - 1))
        here = h(0, z, x)
        before = jnp.where(lane == 0, e(2, z, x), pltpu.roll(here, 1, 1))
        return (h(1, z, x) - h(1, z, x - 1)) - (here - before)

    return result


def split_body(halo, width, classes, eps, material, mask, start, field, diag, *refs):
    zs, xs = halo.zs, halo.xs
    rows = 3 * zs * xs
    messages, (start_in, material_in, mask_in, eps_in, sems) = refs[:4], refs[4:]
    pairs = [(eps, eps_in), (material, material_in), (mask, mask_in)]
    for g in range(0, width, 8):
        part = pl.ds(g * rows, 8 * rows)
        pairs.append((start.at[part], start_in.at[part]))
    copies = [
        pltpu.make_async_copy(source, target, sems.at[i])
        for i, (source, target) in enumerate(pairs)
    ]
    for copy in copies:
        copy.start()
    for copy in copies[:3]:
        copy.wait()
    eps = eps_in
    total = eps[0]
    for level in range(1, classes):
        total = total + eps[level]
    shift = total / classes + CURL_CENTRE
    value = jnp.zeros(material_in.shape, jnp.float32)
    for level in range(classes):
        value = value + jnp.where(material_in[...] == level, eps[level], 0.0)
    diag[...] = value + ABSORB * mask_in[...].astype(jnp.float32) - shift

    places = {}
    for name, message in zip(halo.names, messages):
        for c, z, x in halo.blocks[name]:
            row = halo.block_row(name, c, z, x, width)
            places.setdefault((c, *halo.own(name, z, x)), []).append((message, row))
        base = len(halo.blocks[name]) * width
        message[base : base + 8, :] = jnp.zeros((8, message.shape[1]), jnp.float32)
        for z, x in halo.diagonal[name]:
            row = halo.diagonal_row(name, z, x, width)
            oz, ox = halo.own(name, z, x)
            message[row : row + 1, :] = diag[oz, ox : ox + 1, :]
    for g in range(0, width, 8):
        copies[3 + g // 8].wait()
        for z in range(zs):
            for c in range(3):
                for x in range(xs):
                    at = g * rows + (c * zs + z) * xs + x
                    cell = start_in[pl.ds(at, 8, stride=rows), :]
                    field[z, c, x, g : g + 8] = cell
                    for message, row in places.get((c, z, x), ()):
                        message[row + g : row + g + 8, :] = cell


def relay_body(halo, width, before, after, *passed):
    received = {-1: ((0, -1), before), 1: ((0, 1), after)}
    for name, message in zip(halo.names[4:], passed):
        base = len(halo.blocks[name]) * width
        message[base : base + 8, :] = jnp.zeros((8, message.shape[1]), jnp.float32)
        for c, z, x in halo.blocks[name]:
            side, source = received[halo.side(z, x)[1]]
            at = halo.block_row(side, c, z - name[0] * halo.zs, x, width)
            row = halo.block_row(name, c, z, x, width)
            message[row : row + width, :] = source[at : at + width, :]
        for z, x in halo.diagonal[name]:
            side, source = received[halo.side(z, x)[1]]
            at = halo.diagonal_row(side, z - name[0] * halo.zs, x, width)
            row = halo.diagonal_row(name, z, x, width)
            message[row : row + 1, :] = source[at : at + 1, :]


def parts(value, count):
    found, rest = [], value
    for i in range(count):
        found.append(rest.astype(jnp.bfloat16))
        if i + 1 < count:
            rest = rest - found[-1].astype(jnp.float32)
    return found


def pair(ref, z, c, x):
    return jnp.concatenate([ref[z, c, x], ref[z, c, x + 1]], axis=1)


def product(left, right, contract):
    return lax.dot_general(
        left, right, (((1,), (contract,)), ((), ())), preferred_element_type=jnp.float32
    )


def fold(total, left, right):
    rows = total[:left] + total[left : 2 * left] + total[2 * left :]
    return rows[:, :right] + rows[:, right : 2 * right] + rows[:, 2 * right :]


def cell_pairs(zs, xs):
    return [(z, c, x) for z in range(zs) for c in range(3) for x in range(0, xs, 2)]


def start_gram_body(zs, xs, s0, out):
    total = None
    for z, c, x in cell_pairs(zs, xs):
        stack = jnp.concatenate(parts(pair(s0, z, c, x), 3), axis=0)
        term = product(stack, stack, 1)
        total = term if total is None else total + term
    out[...] = fold(total, *out.shape)


def apply_body(halo, width, ny, slabs, trans, s0, diag, gram, *refs):
    zs, xs = halo.zs, halo.xs
    messages = dict(zip(halo.names, refs[:6]))
    basis, moments, s1, s2, outer = refs[6:]
    slab, across = lax.axis_index(AXES[:3]), lax.axis_index("x")
    held_z = {-1: slab > 0, 0: slab >= 0, 1: slab < slabs - 1}
    held_x = {-1: across > 0, 0: across >= 0, 1: across < trans - 1}
    inside = {
        (i, j): jnp.where(jnp.logical_and(held_z[i], held_x[j]), 1.0, 0.0)
        for i in (-1, 0, 1)
        for j in (-1, 0, 1)
    }
    extra = sorted(q for q in halo.first if halo.side(q[1], q[2]) != (0, 0))
    extra = {q: i for i, q in enumerate(extra)}
    lane = lax.broadcasted_iota(jnp.int32, (8, ny), 1)

    def diagonal(z, x):
        name = halo.name(z, x)
        if name == (0, 0):
            return diag[z, x : x + 1, :]
        row = halo.diagonal_row(name, z, x, width)
        return messages[name][row : row + 1, :]

    def group(at):
        def start(c, z, x):
            name = halo.name(z, x)
            if name == (0, 0):
                return s0[z, c, x, pl.ds(at, 8), :]
            row = halo.block_row(name, c, z, x, width)
            return messages[name][pl.ds(row + at, 8), :] * inside[halo.side(z, x)]

        def once(c, z, x):
            if halo.side(z, x) == (0, 0):
                return s1[z, c, x, pl.ds(at, 8), :]
            return outer[extra[c, z, x]]

        apply = stencil(start, lane, ny - 1)
        for x in range(-1, xs + 1):
            for z in range(-1, zs + 1):
                for c in range(3):
                    if (c, z, x) not in halo.first:
                        continue
                    value = apply(c, z, x) + diagonal(z, x) * start(c, z, x)
                    side = halo.side(z, x)
                    if side == (0, 0):
                        s1[z, c, x, pl.ds(at, 8), :] = value
                    else:
                        outer[extra[c, z, x]] = value * inside[side]
        apply = stencil(once, lane, ny - 1)
        for x in range(xs):
            for z in range(zs):
                for c in range(3):
                    value = apply(c, z, x) + diagonal(z, x) * once(c, z, x)
                    s2[z, c, x, pl.ds(at, 8), :] = value

    for at in range(0, width, 8):
        group(at)

    total = None
    for i, (z, c, x) in enumerate(cell_pairs(zs, xs)):
        k0, k1, k2 = (parts(pair(s, z, c, x), 3) for s in (s0, s1, s2))
        basis[i] = jnp.concatenate([k0[0], k1[0], k0[1], k1[1], k2[0], k2[1]], axis=0)
        left = jnp.concatenate([p for three in zip(k0, k1, k2) for p in three], axis=0)
        right = jnp.concatenate([p for two in zip(k1, k2) for p in two], axis=0)
        term = product(left, right, 1)
        total = term if total is None else total + term
    found = fold(total, 3 * width, 2 * width)
    w = width
    found = [
        gram[...],
        found[:w, :w],
        found[w : 2 * w, :w],
        found[w : 2 * w, w:],
        found[2 * w :, w:],
    ]
    for k, m in enumerate(found):
        for j in range(w // 8):
            moments[8 * k : 8 * k + 8, w * j : w * j + w] = m[8 * j : 8 * j + 8]


def precise(left, right, contract):
    return lax.dot_general(
        left,
        right,
        (((1,), (contract,)), ((), ())),
        precision=lax.Precision.HIGHEST,
        preferred_element_type=jnp.float32,
    )


def factor(gram, size, pauses):
    tiles = size // 8
    lane = lax.broadcasted_iota(jnp.int32, (8, size), 1)
    sub = lax.broadcasted_iota(jnp.int32, (8, size), 0)
    upper = [gram[8 * t : 8 * t + 8, :] for t in range(tiles)]
    inverse = [jnp.where(lane == sub + 8 * t, 1.0, 0.0) for t in range(tiles)]
    found_u, found_i = [], []

    def column(u, j):
        return jnp.broadcast_to(upper[u][:, j : j + 1], (8, size))

    ahead = [column(0, j) for j in range(8)]
    for t in range(tiles):
        cols = {u: [column(u, 8 * t + j) for j in range(8)] for u in range(t + 1, tiles)}
        cols[t] = ahead
        if t + 1 < tiles:
            ahead = [column(t + 1, 8 * t + 8 + j) for j in range(8)]
        pivots = jnp.zeros((8, size), jnp.float32)
        for s in range(8):
            pivot = jnp.broadcast_to(cols[t][s][s : s + 1, :], (8, size))
            pivots = jnp.where(sub == s, pivot, pivots)
            reciprocal = 1.0 / pivot
            heads = [cols[t][j][s : s + 1, :] for j in range(8)]
            row_u, row_i = upper[t][s : s + 1, :], inverse[t][s : s + 1, :]
            for u in range(t, tiles):
                f = cols[u][s] * reciprocal
                if u == t:
                    f = jnp.where(sub > s, f, 0.0)
                if u == t + 1:
                    for j in range(8):
                        ahead[j] = ahead[j] - f * cols[u][s][j : j + 1, :]
                for j in range(s + 1, 8):
                    cols[u][j] = cols[u][j] - f * heads[j]
                upper[u] = upper[u] - f * row_u
                inverse[u] = inverse[u] - f * row_i
        scale = lax.rsqrt(pivots)
        found_u.append(upper[t] * scale)
        found_i.append(inverse[t] * scale)
        if t + 1 in pauses:
            yield jnp.concatenate(found_u, axis=0), jnp.concatenate(found_i, axis=0)


def last_body(zs, xs, width, ny, classes, entries, eps, moments, basis, out, couplings, *scratch):
    w = width
    staged, sems = scratch
    total = eps[0]
    for level in range(1, classes):
        total = total + eps[level]
    shift = total / classes + CURL_CENTRE
    m = []
    for k in range(5):
        rows = moments[8 * k : 8 * k + 8, :] * (1.0 / entries)
        m.append(jnp.concatenate([rows[:, w * j : w * j + w] for j in range(w // 8)], axis=0))
    gram = jnp.concatenate(
        [jnp.concatenate([m[i + j] for j in range(3)], axis=1) for i in range(3)], axis=0
    )
    rows = 3 * zs * xs

    flat = staged.reshape(2, w * rows, ny)

    def combine(block, mix, depth):
        found = []
        for i, (z, c, x) in enumerate(cell_pairs(zs, xs)):
            terms = product(mix, basis[i, :depth], 0)
            value = terms[:w] + terms[w : 2 * w] + terms[2 * w :]
            for k in range(2):
                at = (c * zs + z) * xs + x + k
                flat[block, pl.ds(at, w, stride=rows), :] = value[:, k * ny : (k + 1) * ny]
            if x == xs - 2:
                plane = c * zs + z
                source, target = staged.at[block, :, plane], out.at[block, :, plane]
                found.append(pltpu.make_async_copy(source, target, sems.at[block, plane]))
                found[-1].start()
        return found

    steps = factor(gram, 3 * w, (w // 4, 3 * w // 8))
    upper, inverse = next(steps)
    mix = [jnp.concatenate([p, p], axis=1) for p in parts(inverse[w:, : 2 * w], 3)]
    copies = combine(0, jnp.concatenate(mix, axis=0), 4 * w)
    upper, inverse = next(steps)
    mix = [
        jnp.concatenate([p[:, : 2 * w], p[:, : 2 * w], p[:, 2 * w :], p[:, 2 * w :]], axis=1)
        for p in parts(inverse[2 * w :], 3)
    ]
    copies += combine(1, jnp.concatenate(mix, axis=0), 6 * w)
    identity = jnp.where(
        lax.broadcasted_iota(jnp.int32, (w, w), 0) == lax.broadcasted_iota(jnp.int32, (w, w), 1),
        shift,
        0.0,
    )
    x0, x1 = inverse[:w, :w], inverse[w : 2 * w, w : 2 * w]
    u01, u11 = upper[:w, w : 2 * w], upper[w : 2 * w, w : 2 * w]
    u12, u22 = upper[w : 2 * w, 2 * w :], upper[2 * w :, 2 * w :]
    factor_one = precise(u11, x0, 1)
    couplings[0, 0] = precise(u01, x0, 1) + identity
    couplings[0, 1] = factor_one
    couplings[1, 0] = precise(u12 - precise(factor_one, u01, 0), x1, 1) + identity
    couplings[1, 1] = precise(u22, x1, 1)
    for copy in copies:
        copy.wait()


def moved(name, value, slabs, trans):
    dz, dx = name[0], name[1] % 2 * name[1]
    pairs = [
        (i * trans + j, (i - dz) % slabs * trans + (j - dx) % trans)
        for i in range(slabs)
        for j in range(trans)
    ]
    return lax.ppermute(value, AXES, pairs)


def total_sum(value, deep, trans, devices):
    count = devices // (2 * deep)
    copies = jnp.broadcast_to(value[None], (count, *value.shape))
    value = lax.all_to_all(copies, ("x", "y"), 0, 0, tiled=True).sum(0)
    core, near, middle, far = trans, 2 * trans, 4 * trans, 8 * trans
    rounds = [(middle, far ^ near, far ^ middle)] if deep == 8 else []
    rounds.append((core, near, core ^ near))
    for masks in rounds:
        one, two, three = (
            lax.ppermute(value, AXES, [(i, i ^ m) for i in range(devices)]) for m in masks
        )
        value = (value + one) + (two + three)
    return value


def per_device(slabs, deep, trans, start_block, material, pml_mask, eps_table):
    width, _, zs, xs, ny = start_block.shape
    classes = eps_table.shape[0]
    entries = float(3 * zs * xs * ny * slabs * trans)
    field = shape(zs, 3, xs, width, ny)
    rows = width * 3 * zs * xs
    halo = Halo(zs, xs)

    s0, diag, *messages = call(
        functools.partial(split_body, halo, width, classes),
        [field, shape(zs, xs, ny)] + [shape(halo.rows(n, width), ny) for n in halo.names[:4]],
        [eps_table, material, pml_mask, start_block.reshape(rows, ny)],
        hbm=(0, 1, 2, 3),
        scratch=[
            pltpu.VMEM((rows, ny), jnp.float32),
            pltpu.VMEM((zs, xs, ny), jnp.int32),
            pltpu.VMEM((zs, xs, ny), jnp.int32),
            pltpu.SMEM((classes,), jnp.float32),
            pltpu.SemaphoreType.DMA((3 + width // 8,)),
        ],
    )
    messages = [moved(n, m, slabs, trans) for n, m in zip(halo.names, messages)]
    passed = call(
        functools.partial(relay_body, halo, width),
        [shape(halo.rows(n, width), ny) for n in halo.names[4:]],
        messages[:2],
    )
    messages += [moved(n, m, slabs, trans) for n, m in zip(halo.names[4:], passed)]
    (gram,) = call(functools.partial(start_gram_body, zs, xs), [shape(width, width)], [s0])
    outside = len(halo.first) - 3 * zs * xs
    basis, moments = call(
        functools.partial(apply_body, halo, width, ny, slabs, trans),
        [
            jax.ShapeDtypeStruct((len(cell_pairs(zs, xs)), 6 * width, 2 * ny), jnp.bfloat16),
            shape(40, 4 * width),
        ],
        [s0, diag, gram] + messages,
        scratch=[
            pltpu.VMEM(field.shape, jnp.float32),
            pltpu.VMEM(field.shape, jnp.float32),
            pltpu.VMEM((outside, 8, ny), jnp.float32),
        ],
    )
    moments = total_sum(moments, deep, trans, slabs * trans)
    blocks, couplings = call(
        functools.partial(last_body, zs, xs, width, ny, classes, entries),
        [shape(2, width, 3 * zs, xs, ny), shape(2, 2, width, width)],
        [eps_table, moments, basis],
        smem=(0,),
        hbm_out=(0,),
        scratch=[
            pltpu.VMEM((2, width, 3 * zs, xs, ny), jnp.float32),
            pltpu.SemaphoreType.DMA((2, 3 * zs)),
        ],
    )
    return blocks.reshape(2, width, 3, zs, xs, ny), couplings


def solution(mesh):
    slabs, trans = mesh.devices.shape
    deep = 8 if slabs == 64 else 2
    sizes = (slabs // (2 * deep), deep, 2, trans)
    split = jax.sharding.Mesh(mesh.devices.reshape(sizes), AXES)
    slab = AXES[:3]
    return jax.shard_map(
        functools.partial(per_device, slabs, deep, trans),
        mesh=split,
        in_specs=(
            P(None, None, slab, "x", None),
            P(slab, "x", None),
            P(slab, "x", None),
            P(),
        ),
        out_specs=(P(None, None, None, slab, "x", None), P()),
        check_vma=False,
    )
```

```python
import functools

import jax
import jax.numpy as jnp
from jax import lax
from jax.experimental import pallas as pl
from jax.experimental.pallas import tpu as pltpu
from jax.sharding import PartitionSpec as P

AXES = ("y", "z", "core", "x")
ABSORB = 4.0
CURL_CENTRE = 5.0
VMEM_LIMIT = 40 * 1024 * 1024


def call(body, out_shape, operands, smem=(), hbm=(), hbm_out=(), scratch=()):
    special = {**{i: pltpu.SMEM for i in smem}, **{i: pltpu.HBM for i in hbm}}
    specs = [
        pl.BlockSpec(memory_space=special.get(i, pltpu.VMEM)) for i in range(len(operands))
    ]
    outs = [
        pl.BlockSpec(memory_space=pltpu.HBM if i in hbm_out else pltpu.VMEM)
        for i in range(len(out_shape))
    ]
    return pl.pallas_call(
        body,
        out_shape=out_shape,
        in_specs=specs,
        out_specs=outs,
        scratch_shapes=list(scratch),
        compiler_params=pltpu.CompilerParams(vmem_limit_bytes=VMEM_LIMIT),
    )(
        *(
            pltpu.with_memory_space_constraint(a, pltpu.HBM) if i in hbm else a
            for i, a in enumerate(operands)
        )
    )


def shape(*dims):
    return jax.ShapeDtypeStruct(dims, jnp.float32)


class Halo:
    def __init__(self, zs, xs):
        self.zs, self.xs = zs, xs
        self.first = set()
        for c in range(3):
            for z in range(zs):
                for x in range(xs):
                    self.first.add((c, z, x))
                    self.first |= reach(c, z, x)
        cells = set(self.first)
        for cell in self.first:
            cells |= reach(*cell)
        self.names = [(0, -1), (0, 1), (-1, 0), (1, 0), (-1, 2), (1, 2)]
        self.blocks, self.diagonal = {}, {}
        for name in self.names:
            self.blocks[name] = sorted(q for q in cells if self.name(q[1], q[2]) == name)
            near = {q[1:] for q in self.first if self.name(q[1], q[2]) == name}
            self.diagonal[name] = sorted(near)

    def name(self, z, x):
        side = self.side(z, x)
        return (side[0], 2) if side[0] and side[1] else side

    def side(self, z, x):
        return (
            -1 if z < 0 else int(z >= self.zs),
            -1 if x < 0 else int(x >= self.xs),
        )

    def own(self, name, z, x):
        return z - name[0] * self.zs, x - name[1] % 2 * name[1] * self.xs

    def rows(self, name, width):
        return len(self.blocks[name]) * width + 8

    def block_row(self, name, c, z, x, width):
        return self.blocks[name].index((c, z, x)) * width

    def diagonal_row(self, name, z, x, width):
        return len(self.blocks[name]) * width + self.diagonal[name].index((z, x))


CURL = (
    lambda z, x: {(2, z, x), (1, z + 1, x), (1, z, x)},
    lambda z, x: {(0, z + 1, x), (0, z, x), (2, z, x + 1), (2, z, x)},
    lambda z, x: {(1, z, x + 1), (1, z, x), (0, z, x)},
)
BACK = (
    lambda z, x: {(2, z, x), (1, z, x), (1, z - 1, x)},
    lambda z, x: {(0, z, x), (0, z - 1, x), (2, z, x), (2, z, x - 1)},
    lambda z, x: {(1, z, x), (1, z, x - 1), (0, z, x)},
)


def reach(c, z, x):
    cells = {(c, z, x)}
    for k, hz, hx in BACK[c](z, x):
        cells |= CURL[k](hz, hx)
    return cells


def stencil(e, lane, last):
    known = {}

    def step_y(value):
        return jnp.where(lane == last, 0.0, pltpu.roll(value, last, 1)) - value

    def h(k, z, x):
        if (k, z, x) not in known:
            if k == 0:
                value = step_y(e(2, z, x)) - (e(1, z + 1, x) - e(1, z, x))
            elif k == 1:
                value = (e(0, z + 1, x) - e(0, z, x)) - (e(2, z, x + 1) - e(2, z, x))
            else:
                value = (e(1, z, x + 1) - e(1, z, x)) - step_y(e(0, z, x))
            known[k, z, x] = value
        return known[k, z, x]

    def result(c, z, x):
        if c == 0:
            here = h(2, z, x)
            before = jnp.where(lane == 0, -e(0, z, x), pltpu.roll(here, 1, 1))
            return (here - before) - (h(1, z, x) - h(1, z - 1, x))
        if c == 1:
            return (h(0, z, x) - h(0, z - 1, x)) - (h(2, z, x) - h(2, z, x - 1))
        here = h(0, z, x)
        before = jnp.where(lane == 0, e(2, z, x), pltpu.roll(here, 1, 1))
        return (h(1, z, x) - h(1, z, x - 1)) - (here - before)

    return result


def split_body(halo, width, classes, eps, material, mask, start, field, diag, *refs):
    zs, xs = halo.zs, halo.xs
    rows = 3 * zs * xs
    messages, (start_in, material_in, mask_in, eps_in, sems) = refs[:4], refs[4:]
    pairs = [(eps, eps_in), (material, material_in), (mask, mask_in)]
    for g in range(0, width, 8):
        part = pl.ds(g * rows, 8 * rows)
        pairs.append((start.at[part], start_in.at[part]))
    copies = [
        pltpu.make_async_copy(source, target, sems.at[i])
        for i, (source, target) in enumerate(pairs)
    ]
    for copy in copies:
        copy.start()
    for copy in copies[:3]:
        copy.wait()
    eps = eps_in
    total = eps[0]
    for level in range(1, classes):
        total = total + eps[level]
    shift = total / classes + CURL_CENTRE
    value = jnp.zeros(material_in.shape, jnp.float32)
    for level in range(classes):
        value = value + jnp.where(material_in[...] == level, eps[level], 0.0)
    diag[...] = value + ABSORB * mask_in[...].astype(jnp.float32) - shift

    places = {}
    for name, message in zip(halo.names, messages):
        for c, z, x in halo.blocks[name]:
            row = halo.block_row(name, c, z, x, width)
            places.setdefault((c, *halo.own(name, z, x)), []).append((message, row))
        base = len(halo.blocks[name]) * width
        message[base : base + 8, :] = jnp.zeros((8, message.shape[1]), jnp.float32)
        for z, x in halo.diagonal[name]:
            row = halo.diagonal_row(name, z, x, width)
            oz, ox = halo.own(name, z, x)
            message[row : row + 1, :] = diag[oz, ox : ox + 1, :]
    for g in range(0, width, 8):
        copies[3 + g // 8].wait()
        for z in range(zs):
            for c in range(3):
                for x in range(xs):
                    at = g * rows + (c * zs + z) * xs + x
                    cell = start_in[pl.ds(at, 8, stride=rows), :]
                    field[z, c, x, g : g + 8] = cell
                    for message, row in places.get((c, z, x), ()):
                        message[row + g : row + g + 8, :] = cell


def relay_body(halo, width, before, after, *passed):
    received = {-1: ((0, -1), before), 1: ((0, 1), after)}
    for name, message in zip(halo.names[4:], passed):
        base = len(halo.blocks[name]) * width
        message[base : base + 8, :] = jnp.zeros((8, message.shape[1]), jnp.float32)
        for c, z, x in halo.blocks[name]:
            side, source = received[halo.side(z, x)[1]]
            at = halo.block_row(side, c, z - name[0] * halo.zs, x, width)
            row = halo.block_row(name, c, z, x, width)
            message[row : row + width, :] = source[at : at + width, :]
        for z, x in halo.diagonal[name]:
            side, source = received[halo.side(z, x)[1]]
            at = halo.diagonal_row(side, z - name[0] * halo.zs, x, width)
            row = halo.diagonal_row(name, z, x, width)
            message[row : row + 1, :] = source[at : at + 1, :]


def parts(value, count):
    found, rest = [], value
    for i in range(count):
        found.append(rest.astype(jnp.bfloat16))
        if i + 1 < count:
            rest = rest - found[-1].astype(jnp.float32)
    return found


def pair(ref, z, c, x):
    return jnp.concatenate([ref[z, c, x], ref[z, c, x + 1]], axis=1)


def product(left, right, contract):
    return lax.dot_general(
        left, right, (((1,), (contract,)), ((), ())), preferred_element_type=jnp.float32
    )


def fold(total, left, right):
    rows = total[:left] + total[left : 2 * left] + total[2 * left :]
    return rows[:, :right] + rows[:, right : 2 * right] + rows[:, 2 * right :]


def cell_pairs(zs, xs):
    return [(z, c, x) for z in range(zs) for c in range(3) for x in range(0, xs, 2)]


def start_gram_body(zs, xs, s0, out):
    total = None
    for z, c, x in cell_pairs(zs, xs):
        stack = jnp.concatenate(parts(pair(s0, z, c, x), 3), axis=0)
        term = product(stack, stack, 1)
        total = term if total is None else total + term
    out[...] = fold(total, *out.shape)


def apply_body(halo, width, ny, slabs, trans, s0, diag, gram, *refs):
    zs, xs = halo.zs, halo.xs
    messages = dict(zip(halo.names, refs[:6]))
    basis, moments, s1, s2, outer = refs[6:]
    slab, across = lax.axis_index(AXES[:3]), lax.axis_index("x")
    held_z = {-1: slab > 0, 0: slab >= 0, 1: slab < slabs - 1}
    held_x = {-1: across > 0, 0: across >= 0, 1: across < trans - 1}
    inside = {
        (i, j): jnp.where(jnp.logical_and(held_z[i], held_x[j]), 1.0, 0.0)
        for i in (-1, 0, 1)
        for j in (-1, 0, 1)
    }
    extra = sorted(q for q in halo.first if halo.side(q[1], q[2]) != (0, 0))
    extra = {q: i for i, q in enumerate(extra)}
    lane = lax.broadcasted_iota(jnp.int32, (8, ny), 1)

    def diagonal(z, x):
        name = halo.name(z, x)
        if name == (0, 0):
            return diag[z, x : x + 1, :]
        row = halo.diagonal_row(name, z, x, width)
        return messages[name][row : row + 1, :]

    def group(at):
        def start(c, z, x):
            name = halo.name(z, x)
            if name == (0, 0):
                return s0[z, c, x, pl.ds(at, 8), :]
            row = halo.block_row(name, c, z, x, width)
            return messages[name][pl.ds(row + at, 8), :] * inside[halo.side(z, x)]

        def once(c, z, x):
            if halo.side(z, x) == (0, 0):
                return s1[z, c, x, pl.ds(at, 8), :]
            return outer[extra[c, z, x]]

        apply = stencil(start, lane, ny - 1)
        for x in range(-1, xs + 1):
            for z in range(-1, zs + 1):
                for c in range(3):
                    if (c, z, x) not in halo.first:
                        continue
                    value = apply(c, z, x) + diagonal(z, x) * start(c, z, x)
                    side = halo.side(z, x)
                    if side == (0, 0):
                        s1[z, c, x, pl.ds(at, 8), :] = value
                    else:
                        outer[extra[c, z, x]] = value * inside[side]
        apply = stencil(once, lane, ny - 1)
        for x in range(xs):
            for z in range(zs):
                for c in range(3):
                    value = apply(c, z, x) + diagonal(z, x) * once(c, z, x)
                    s2[z, c, x, pl.ds(at, 8), :] = value

    for at in range(0, width, 8):
        group(at)

    total = None
    for i, (z, c, x) in enumerate(cell_pairs(zs, xs)):
        k0, k1, k2 = (parts(pair(s, z, c, x), 3) for s in (s0, s1, s2))
        basis[i] = jnp.concatenate([k0[0], k1[0], k0[1], k1[1], k2[0], k2[1]], axis=0)
        left = jnp.concatenate([p for three in zip(k0, k1, k2) for p in three], axis=0)
        right = jnp.concatenate([p for two in zip(k1, k2) for p in two], axis=0)
        term = product(left, right, 1)
        total = term if total is None else total + term
    found = fold(total, 3 * width, 2 * width)
    w = width
    found = [
        gram[...],
        found[:w, :w],
        found[w : 2 * w, :w],
        found[w : 2 * w, w:],
        found[2 * w :, w:],
    ]
    for k, m in enumerate(found):
        for j in range(w // 8):
            moments[8 * k : 8 * k + 8, w * j : w * j + w] = m[8 * j : 8 * j + 8]


def precise(left, right, contract):
    return lax.dot_general(
        left,
        right,
        (((1,), (contract,)), ((), ())),
        precision=lax.Precision.HIGHEST,
        preferred_element_type=jnp.float32,
    )


def factor(gram, size, pauses):
    tiles = size // 8
    lane = lax.broadcasted_iota(jnp.int32, (8, size), 1)
    sub = lax.broadcasted_iota(jnp.int32, (8, size), 0)
    upper = [gram[8 * t : 8 * t + 8, :] for t in range(tiles)]
    inverse = [jnp.where(lane == sub + 8 * t, 1.0, 0.0) for t in range(tiles)]
    found_u, found_i = [], []

    def column(u, j):
        return jnp.broadcast_to(upper[u][:, j : j + 1], (8, size))

    ahead = [column(0, j) for j in range(8)]
    for t in range(tiles):
        cols = {u: [column(u, 8 * t + j) for j in range(8)] for u in range(t + 1, tiles)}
        cols[t] = ahead
        if t + 1 < tiles:
            ahead = [column(t + 1, 8 * t + 8 + j) for j in range(8)]
        pivots = jnp.zeros((8, size), jnp.float32)
        for s in range(8):
            pivot = jnp.broadcast_to(cols[t][s][s : s + 1, :], (8, size))
            pivots = jnp.where(sub == s, pivot, pivots)
            reciprocal = 1.0 / pivot
            heads = [cols[t][j][s : s + 1, :] for j in range(8)]
            row_u, row_i = upper[t][s : s + 1, :], inverse[t][s : s + 1, :]
            for u in range(t, tiles):
                f = cols[u][s] * reciprocal
                if u == t:
                    f = jnp.where(sub > s, f, 0.0)
                if u == t + 1:
                    for j in range(8):
                        ahead[j] = ahead[j] - f * cols[u][s][j : j + 1, :]
                for j in range(s + 1, 8):
                    cols[u][j] = cols[u][j] - f * heads[j]
                upper[u] = upper[u] - f * row_u
                inverse[u] = inverse[u] - f * row_i
        scale = lax.rsqrt(pivots)
        found_u.append(upper[t] * scale)
        found_i.append(inverse[t] * scale)
        if t + 1 in pauses:
            yield jnp.concatenate(found_u, axis=0), jnp.concatenate(found_i, axis=0)


def last_body(zs, xs, width, ny, classes, entries, eps, moments, basis, out, couplings, *scratch):
    w = width
    staged, sems = scratch
    total = eps[0]
    for level in range(1, classes):
        total = total + eps[level]
    shift = total / classes + CURL_CENTRE
    m = []
    for k in range(5):
        rows = moments[8 * k : 8 * k + 8, :] * (1.0 / entries)
        m.append(jnp.concatenate([rows[:, w * j : w * j + w] for j in range(w // 8)], axis=0))
    gram = jnp.concatenate(
        [jnp.concatenate([m[i + j] for j in range(3)], axis=1) for i in range(3)], axis=0
    )
    rows = 3 * zs * xs

    flat = staged.reshape(2, (w + 1) * rows, ny)

    def combine(block, mix, depth):
        found = []
        for i, (z, c, x) in enumerate(cell_pairs(zs, xs)):
            terms = product(mix, basis[i, :depth], 0)
            value = terms[:w] + terms[w : 2 * w] + terms[2 * w :]
            for k in range(2):
                at = (c * zs + z) * xs + x + k
                flat[block, pl.ds(at, w, stride=rows), :] = value[:, k * ny : (k + 1) * ny]
            if x == xs - 2:
                plane = c * zs + z
                source = staged.at[block, pl.ds(0, w), plane]
                target = out.at[block, :, plane]
                found.append(pltpu.make_async_copy(source, target, sems.at[block, plane]))
                found[-1].start()
        return found

    steps = factor(gram, 3 * w, (w // 4, 3 * w // 8))
    upper, inverse = next(steps)
    mix = [jnp.concatenate([p, p], axis=1) for p in parts(inverse[w:, : 2 * w], 3)]
    copies = combine(0, jnp.concatenate(mix, axis=0), 4 * w)
    upper, inverse = next(steps)
    mix = [
        jnp.concatenate([p[:, : 2 * w], p[:, : 2 * w], p[:, 2 * w :], p[:, 2 * w :]], axis=1)
        for p in parts(inverse[2 * w :], 3)
    ]
    copies += combine(1, jnp.concatenate(mix, axis=0), 6 * w)
    identity = jnp.where(
        lax.broadcasted_iota(jnp.int32, (w, w), 0) == lax.broadcasted_iota(jnp.int32, (w, w), 1),
        shift,
        0.0,
    )
    x0, x1 = inverse[:w, :w], inverse[w : 2 * w, w : 2 * w]
    u01, u11 = upper[:w, w : 2 * w], upper[w : 2 * w, w : 2 * w]
    u12, u22 = upper[w : 2 * w, 2 * w :], upper[2 * w :, 2 * w :]
    factor_one = precise(u11, x0, 1)
    couplings[0, 0] = precise(u01, x0, 1) + identity
    couplings[0, 1] = factor_one
    couplings[1, 0] = precise(u12 - precise(factor_one, u01, 0), x1, 1) + identity
    couplings[1, 1] = precise(u22, x1, 1)
    for copy in copies:
        copy.wait()


def moved(name, value, slabs, trans):
    dz, dx = name[0], name[1] % 2 * name[1]
    pairs = [
        (i * trans + j, (i - dz) % slabs * trans + (j - dx) % trans)
        for i in range(slabs)
        for j in range(trans)
    ]
    return lax.ppermute(value, AXES, pairs)


def total_sum(value, deep, trans, devices):
    count = devices // (2 * deep)
    copies = jnp.broadcast_to(value[None], (count, *value.shape))
    value = lax.all_to_all(copies, ("x", "y"), 0, 0, tiled=True).sum(0)
    core, near, middle, far = trans, 2 * trans, 4 * trans, 8 * trans
    rounds = [(middle, far ^ near, far ^ middle)] if deep == 8 else []
    rounds.append((core, near, core ^ near))
    for masks in rounds:
        one, two, three = (
            lax.ppermute(value, AXES, [(i, i ^ m) for i in range(devices)]) for m in masks
        )
        value = (value + one) + (two + three)
    return value


def per_device(slabs, deep, trans, start_block, material, pml_mask, eps_table):
    width, _, zs, xs, ny = start_block.shape
    classes = eps_table.shape[0]
    entries = float(3 * zs * xs * ny * slabs * trans)
    field = shape(zs, 3, xs, width, ny)
    rows = width * 3 * zs * xs
    halo = Halo(zs, xs)

    s0, diag, *messages = call(
        functools.partial(split_body, halo, width, classes),
        [field, shape(zs, xs, ny)] + [shape(halo.rows(n, width), ny) for n in halo.names[:4]],
        [eps_table, material, pml_mask, start_block.reshape(rows, ny)],
        hbm=(0, 1, 2, 3),
        scratch=[
            pltpu.VMEM((rows + 3 * zs * xs, ny), jnp.float32),
            pltpu.VMEM((zs, xs, ny), jnp.int32),
            pltpu.VMEM((zs, xs, ny), jnp.int32),
            pltpu.SMEM((classes,), jnp.float32),
            pltpu.SemaphoreType.DMA((3 + width // 8,)),
        ],
    )
    messages = [moved(n, m, slabs, trans) for n, m in zip(halo.names, messages)]
    passed = call(
        functools.partial(relay_body, halo, width),
        [shape(halo.rows(n, width), ny) for n in halo.names[4:]],
        messages[:2],
    )
    messages += [moved(n, m, slabs, trans) for n, m in zip(halo.names[4:], passed)]
    (gram,) = call(functools.partial(start_gram_body, zs, xs), [shape(width, width)], [s0])
    outside = len(halo.first) - 3 * zs * xs
    basis, moments = call(
        functools.partial(apply_body, halo, width, ny, slabs, trans),
        [
            jax.ShapeDtypeStruct((len(cell_pairs(zs, xs)), 6 * width, 2 * ny), jnp.bfloat16),
            shape(40, 4 * width),
        ],
        [s0, diag, gram] + messages,
        scratch=[
            pltpu.VMEM(field.shape, jnp.float32),
            pltpu.VMEM(field.shape, jnp.float32),
            pltpu.VMEM((outside, 8, ny), jnp.float32),
        ],
    )
    moments = total_sum(moments, deep, trans, slabs * trans)
    blocks, couplings = call(
        functools.partial(last_body, zs, xs, width, ny, classes, entries),
        [shape(2, width, 3 * zs, xs, ny), shape(2, 2, width, width)],
        [eps_table, moments, basis],
        smem=(0,),
        hbm_out=(0,),
        scratch=[
            pltpu.VMEM((2, width + 1, 3 * zs, xs, ny), jnp.float32),
            pltpu.SemaphoreType.DMA((2, 3 * zs)),
        ],
    )
    return blocks.reshape(2, width, 3, zs, xs, ny), couplings


def solution(mesh):
    slabs, trans = mesh.devices.shape
    deep = 8 if slabs == 64 else 2
    sizes = (slabs // (2 * deep), deep, 2, trans)
    split = jax.sharding.Mesh(mesh.devices.reshape(sizes), AXES)
    slab = AXES[:3]
    return jax.shard_map(
        functools.partial(per_device, slabs, deep, trans),
        mesh=split,
        in_specs=(
            P(None, None, slab, "x", None),
            P(slab, "x", None),
            P(slab, "x", None),
            P(),
        ),
        out_specs=(P(None, None, None, slab, "x", None), P()),
        check_vma=False,
    )
```

```python
import functools

import jax
import jax.numpy as jnp
from jax import lax
from jax.experimental import pallas as pl
from jax.experimental.pallas import tpu as pltpu
from jax.sharding import PartitionSpec as P

AXES = ("y", "z", "core", "x")
ABSORB = 4.0
CURL_CENTRE = 5.0
VMEM_LIMIT = 40 * 1024 * 1024


def call(body, out_shape, operands, smem=(), hbm=(), hbm_out=(), scratch=()):
    special = {**{i: pltpu.SMEM for i in smem}, **{i: pltpu.HBM for i in hbm}}
    specs = [
        pl.BlockSpec(memory_space=special.get(i, pltpu.VMEM)) for i in range(len(operands))
    ]
    outs = [
        pl.BlockSpec(memory_space=pltpu.HBM if i in hbm_out else pltpu.VMEM)
        for i in range(len(out_shape))
    ]
    return pl.pallas_call(
        body,
        out_shape=out_shape,
        in_specs=specs,
        out_specs=outs,
        scratch_shapes=list(scratch),
        compiler_params=pltpu.CompilerParams(vmem_limit_bytes=VMEM_LIMIT),
    )(
        *(
            pltpu.with_memory_space_constraint(a, pltpu.HBM) if i in hbm else a
            for i, a in enumerate(operands)
        )
    )


def shape(*dims):
    return jax.ShapeDtypeStruct(dims, jnp.float32)


class Halo:
    def __init__(self, zs, xs):
        self.zs, self.xs = zs, xs
        self.first = set()
        for c in range(3):
            for z in range(zs):
                for x in range(xs):
                    self.first.add((c, z, x))
                    self.first |= reach(c, z, x)
        cells = set(self.first)
        for cell in self.first:
            cells |= reach(*cell)
        self.names = [(0, -1), (0, 1), (-1, 0), (1, 0), (-1, 2), (1, 2)]
        self.blocks, self.diagonal = {}, {}
        for name in self.names:
            self.blocks[name] = sorted(q for q in cells if self.name(q[1], q[2]) == name)
            near = {q[1:] for q in self.first if self.name(q[1], q[2]) == name}
            self.diagonal[name] = sorted(near)

    def name(self, z, x):
        side = self.side(z, x)
        return (side[0], 2) if side[0] and side[1] else side

    def side(self, z, x):
        return (
            -1 if z < 0 else int(z >= self.zs),
            -1 if x < 0 else int(x >= self.xs),
        )

    def own(self, name, z, x):
        return z - name[0] * self.zs, x - name[1] % 2 * name[1] * self.xs

    def rows(self, name, width):
        return len(self.blocks[name]) * width + 8

    def block_row(self, name, c, z, x, width):
        return self.blocks[name].index((c, z, x)) * width

    def diagonal_row(self, name, z, x, width):
        return len(self.blocks[name]) * width + self.diagonal[name].index((z, x))


CURL = (
    lambda z, x: {(2, z, x), (1, z + 1, x), (1, z, x)},
    lambda z, x: {(0, z + 1, x), (0, z, x), (2, z, x + 1), (2, z, x)},
    lambda z, x: {(1, z, x + 1), (1, z, x), (0, z, x)},
)
BACK = (
    lambda z, x: {(2, z, x), (1, z, x), (1, z - 1, x)},
    lambda z, x: {(0, z, x), (0, z - 1, x), (2, z, x), (2, z, x - 1)},
    lambda z, x: {(1, z, x), (1, z, x - 1), (0, z, x)},
)


def reach(c, z, x):
    cells = {(c, z, x)}
    for k, hz, hx in BACK[c](z, x):
        cells |= CURL[k](hz, hx)
    return cells


def stencil(e, lane, last):
    known = {}

    def step_y(value):
        return jnp.where(lane == last, 0.0, pltpu.roll(value, last, 1)) - value

    def h(k, z, x):
        if (k, z, x) not in known:
            if k == 0:
                value = step_y(e(2, z, x)) - (e(1, z + 1, x) - e(1, z, x))
            elif k == 1:
                value = (e(0, z + 1, x) - e(0, z, x)) - (e(2, z, x + 1) - e(2, z, x))
            else:
                value = (e(1, z, x + 1) - e(1, z, x)) - step_y(e(0, z, x))
            known[k, z, x] = value
        return known[k, z, x]

    def result(c, z, x):
        if c == 0:
            here = h(2, z, x)
            before = jnp.where(lane == 0, -e(0, z, x), pltpu.roll(here, 1, 1))
            return (here - before) - (h(1, z, x) - h(1, z - 1, x))
        if c == 1:
            return (h(0, z, x) - h(0, z - 1, x)) - (h(2, z, x) - h(2, z, x - 1))
        here = h(0, z, x)
        before = jnp.where(lane == 0, e(2, z, x), pltpu.roll(here, 1, 1))
        return (h(1, z, x) - h(1, z, x - 1)) - (here - before)

    return result


def split_body(halo, width, classes, eps, material, mask, start, field, diag, *refs):
    zs, xs = halo.zs, halo.xs
    rows = 3 * zs * xs
    messages, (start_in, material_in, mask_in, eps_in, sems) = refs[:4], refs[4:]
    pairs = [(eps, eps_in), (material, material_in), (mask, mask_in)]
    for g in range(0, width, 8):
        part = pl.ds(g * rows, 8 * rows)
        pairs.append((start.at[part], start_in.at[part]))
    copies = [
        pltpu.make_async_copy(source, target, sems.at[i])
        for i, (source, target) in enumerate(pairs)
    ]
    for copy in copies:
        copy.start()
    for copy in copies[:3]:
        copy.wait()
    eps = eps_in
    total = eps[0]
    for level in range(1, classes):
        total = total + eps[level]
    shift = total / classes + CURL_CENTRE
    value = jnp.zeros(material_in.shape, jnp.float32)
    for level in range(classes):
        value = value + jnp.where(material_in[...] == level, eps[level], 0.0)
    diag[...] = value + ABSORB * mask_in[...].astype(jnp.float32) - shift

    places = {}
    for name, message in zip(halo.names, messages):
        for c, z, x in halo.blocks[name]:
            row = halo.block_row(name, c, z, x, width)
            places.setdefault((c, *halo.own(name, z, x)), []).append((message, row))
        base = len(halo.blocks[name]) * width
        message[base : base + 8, :] = jnp.zeros((8, message.shape[1]), jnp.float32)
        for z, x in halo.diagonal[name]:
            row = halo.diagonal_row(name, z, x, width)
            oz, ox = halo.own(name, z, x)
            message[row : row + 1, :] = diag[oz, ox : ox + 1, :]
    for g in range(0, width, 8):
        copies[3 + g // 8].wait()
        for z in range(zs):
            for c in range(3):
                for x in range(xs):
                    at = g * rows + (c * zs + z) * xs + x
                    cell = start_in[pl.ds(at, 8, stride=rows), :]
                    field[z, c, x, g : g + 8] = cell
                    for message, row in places.get((c, z, x), ()):
                        message[row + g : row + g + 8, :] = cell


def relay_body(halo, width, before, after, *passed):
    received = {-1: ((0, -1), before), 1: ((0, 1), after)}
    for name, message in zip(halo.names[4:], passed):
        base = len(halo.blocks[name]) * width
        message[base : base + 8, :] = jnp.zeros((8, message.shape[1]), jnp.float32)
        for c, z, x in halo.blocks[name]:
            side, source = received[halo.side(z, x)[1]]
            at = halo.block_row(side, c, z - name[0] * halo.zs, x, width)
            row = halo.block_row(name, c, z, x, width)
            message[row : row + width, :] = source[at : at + width, :]
        for z, x in halo.diagonal[name]:
            side, source = received[halo.side(z, x)[1]]
            at = halo.diagonal_row(side, z - name[0] * halo.zs, x, width)
            row = halo.diagonal_row(name, z, x, width)
            message[row : row + 1, :] = source[at : at + 1, :]


def parts(value, count):
    found, rest = [], value
    for i in range(count):
        found.append(rest.astype(jnp.bfloat16))
        if i + 1 < count:
            rest = rest - found[-1].astype(jnp.float32)
    return found


def pair(ref, z, c, x):
    return jnp.concatenate([ref[z, c, x], ref[z, c, x + 1]], axis=1)


def product(left, right, contract):
    return lax.dot_general(
        left, right, (((1,), (contract,)), ((), ())), preferred_element_type=jnp.float32
    )


def fold(total, left, right):
    rows = total[:left] + total[left : 2 * left] + total[2 * left :]
    return rows[:, :right] + rows[:, right : 2 * right] + rows[:, 2 * right :]


def cell_pairs(zs, xs):
    return [(z, c, x) for z in range(zs) for c in range(3) for x in range(0, xs, 2)]


def start_gram_body(zs, xs, s0, out, split):
    total = None
    for i, (z, c, x) in enumerate(cell_pairs(zs, xs)):
        stack = jnp.concatenate(parts(pair(s0, z, c, x), 3), axis=0)
        split[i] = stack
        term = product(stack, stack, 1)
        total = term if total is None else total + term
    out[...] = fold(total, *out.shape)


def apply_body(halo, width, ny, slabs, trans, s0, diag, gram, split, *refs):
    zs, xs = halo.zs, halo.xs
    messages = dict(zip(halo.names, refs[:6]))
    basis, moments, s1, s2, outer = refs[6:]
    slab, across = lax.axis_index(AXES[:3]), lax.axis_index("x")
    held_z = {-1: slab > 0, 0: slab >= 0, 1: slab < slabs - 1}
    held_x = {-1: across > 0, 0: across >= 0, 1: across < trans - 1}
    inside = {
        (i, j): jnp.where(jnp.logical_and(held_z[i], held_x[j]), 1.0, 0.0)
        for i in (-1, 0, 1)
        for j in (-1, 0, 1)
    }
    extra = sorted(q for q in halo.first if halo.side(q[1], q[2]) != (0, 0))
    extra = {q: i for i, q in enumerate(extra)}
    lane = lax.broadcasted_iota(jnp.int32, (8, ny), 1)

    def diagonal(z, x):
        name = halo.name(z, x)
        if name == (0, 0):
            return diag[z, x : x + 1, :]
        row = halo.diagonal_row(name, z, x, width)
        return messages[name][row : row + 1, :]

    def group(at):
        def start(c, z, x):
            name = halo.name(z, x)
            if name == (0, 0):
                return s0[z, c, x, pl.ds(at, 8), :]
            row = halo.block_row(name, c, z, x, width)
            return messages[name][pl.ds(row + at, 8), :] * inside[halo.side(z, x)]

        def once(c, z, x):
            if halo.side(z, x) == (0, 0):
                return s1[z, c, x, pl.ds(at, 8), :]
            return outer[extra[c, z, x]]

        apply = stencil(start, lane, ny - 1)
        for x in range(-1, xs + 1):
            for z in range(-1, zs + 1):
                for c in range(3):
                    if (c, z, x) not in halo.first:
                        continue
                    value = apply(c, z, x) + diagonal(z, x) * start(c, z, x)
                    side = halo.side(z, x)
                    if side == (0, 0):
                        s1[z, c, x, pl.ds(at, 8), :] = value
                    else:
                        outer[extra[c, z, x]] = value * inside[side]
        apply = stencil(once, lane, ny - 1)
        for x in range(xs):
            for z in range(zs):
                for c in range(3):
                    value = apply(c, z, x) + diagonal(z, x) * once(c, z, x)
                    s2[z, c, x, pl.ds(at, 8), :] = value

    for at in range(0, width, 8):
        group(at)

    total = None
    for i, (z, c, x) in enumerate(cell_pairs(zs, xs)):
        k0 = [split[i, k * width : (k + 1) * width] for k in range(3)]
        k1, k2 = (parts(pair(s, z, c, x), 3) for s in (s1, s2))
        basis[i] = jnp.concatenate([k0[0], k1[0], k0[1], k1[1], k2[0], k2[1]], axis=0)
        left = jnp.concatenate([p for three in zip(k0, k1, k2) for p in three], axis=0)
        right = jnp.concatenate([p for two in zip(k1, k2) for p in two], axis=0)
        term = product(left, right, 1)
        total = term if total is None else total + term
    found = fold(total, 3 * width, 2 * width)
    w = width
    found = [
        gram[...],
        found[:w, :w],
        found[w : 2 * w, :w],
        found[w : 2 * w, w:],
        found[2 * w :, w:],
    ]
    for k, m in enumerate(found):
        for j in range(w // 8):
            moments[8 * k : 8 * k + 8, w * j : w * j + w] = m[8 * j : 8 * j + 8]


def precise(left, right, contract):
    return lax.dot_general(
        left,
        right,
        (((1,), (contract,)), ((), ())),
        precision=lax.Precision.HIGHEST,
        preferred_element_type=jnp.float32,
    )


def factor(gram, size, pauses):
    tiles = size // 8
    lane = lax.broadcasted_iota(jnp.int32, (8, size), 1)
    sub = lax.broadcasted_iota(jnp.int32, (8, size), 0)
    upper = [gram[8 * t : 8 * t + 8, :] for t in range(tiles)]
    inverse = [jnp.where(lane == sub + 8 * t, 1.0, 0.0) for t in range(tiles)]
    found_u, found_i = [], []

    def column(u, j):
        return jnp.broadcast_to(upper[u][:, j : j + 1], (8, size))

    ahead = [column(0, j) for j in range(8)]
    for t in range(tiles):
        cols = {u: [column(u, 8 * t + j) for j in range(8)] for u in range(t + 1, tiles)}
        cols[t] = ahead
        if t + 1 < tiles:
            ahead = [column(t + 1, 8 * t + 8 + j) for j in range(8)]
        pivots = jnp.zeros((8, size), jnp.float32)
        for s in range(8):
            pivot = jnp.broadcast_to(cols[t][s][s : s + 1, :], (8, size))
            pivots = jnp.where(sub == s, pivot, pivots)
            reciprocal = 1.0 / pivot
            heads = [cols[t][j][s : s + 1, :] for j in range(8)]
            row_u, row_i = upper[t][s : s + 1, :], inverse[t][s : s + 1, :]
            for u in range(t, tiles):
                f = cols[u][s] * reciprocal
                if u == t:
                    f = jnp.where(sub > s, f, 0.0)
                if u == t + 1:
                    for j in range(8):
                        ahead[j] = ahead[j] - f * cols[u][s][j : j + 1, :]
                for j in range(s + 1, 8):
                    cols[u][j] = cols[u][j] - f * heads[j]
                upper[u] = upper[u] - f * row_u
                inverse[u] = inverse[u] - f * row_i
        scale = lax.rsqrt(pivots)
        found_u.append(upper[t] * scale)
        found_i.append(inverse[t] * scale)
        if t + 1 in pauses:
            yield jnp.concatenate(found_u, axis=0), jnp.concatenate(found_i, axis=0)


def last_body(zs, xs, width, ny, classes, entries, eps, moments, basis, out, couplings, *scratch):
    w = width
    staged, sems = scratch
    total = eps[0]
    for level in range(1, classes):
        total = total + eps[level]
    shift = total / classes + CURL_CENTRE
    m = []
    for k in range(5):
        rows = moments[8 * k : 8 * k + 8, :] * (1.0 / entries)
        m.append(jnp.concatenate([rows[:, w * j : w * j + w] for j in range(w // 8)], axis=0))
    gram = jnp.concatenate(
        [jnp.concatenate([m[i + j] for j in range(3)], axis=1) for i in range(3)], axis=0
    )
    rows = 3 * zs * xs

    flat = staged.reshape(2, (w + 1) * rows, ny)

    def combine(block, mix, depth):
        found = []
        for i, (z, c, x) in enumerate(cell_pairs(zs, xs)):
            terms = product(mix, basis[i, :depth], 0)
            value = terms[:w] + terms[w : 2 * w] + terms[2 * w :]
            for k in range(2):
                at = (c * zs + z) * xs + x + k
                flat[block, pl.ds(at, w, stride=rows), :] = value[:, k * ny : (k + 1) * ny]
            if x == xs - 2:
                plane = c * zs + z
                source = staged.at[block, pl.ds(0, w), plane]
                target = out.at[block, :, plane]
                found.append(pltpu.make_async_copy(source, target, sems.at[block, plane]))
                found[-1].start()
        return found

    steps = factor(gram, 3 * w, (w // 4, 3 * w // 8))
    upper, inverse = next(steps)
    mix = [jnp.concatenate([p, p], axis=1) for p in parts(inverse[w:, : 2 * w], 3)]
    copies = combine(0, jnp.concatenate(mix, axis=0), 4 * w)
    upper, inverse = next(steps)
    mix = [
        jnp.concatenate([p[:, : 2 * w], p[:, : 2 * w], p[:, 2 * w :], p[:, 2 * w :]], axis=1)
        for p in parts(inverse[2 * w :], 3)
    ]
    copies += combine(1, jnp.concatenate(mix, axis=0), 6 * w)
    identity = jnp.where(
        lax.broadcasted_iota(jnp.int32, (w, w), 0) == lax.broadcasted_iota(jnp.int32, (w, w), 1),
        shift,
        0.0,
    )
    x0, x1 = inverse[:w, :w], inverse[w : 2 * w, w : 2 * w]
    u01, u11 = upper[:w, w : 2 * w], upper[w : 2 * w, w : 2 * w]
    u12, u22 = upper[w : 2 * w, 2 * w :], upper[2 * w :, 2 * w :]
    factor_one = precise(u11, x0, 1)
    couplings[0, 0] = precise(u01, x0, 1) + identity
    couplings[0, 1] = factor_one
    couplings[1, 0] = precise(u12 - precise(factor_one, u01, 0), x1, 1) + identity
    couplings[1, 1] = precise(u22, x1, 1)
    for copy in copies:
        copy.wait()


def moved(name, value, slabs, trans):
    dz, dx = name[0], name[1] % 2 * name[1]
    pairs = [
        (i * trans + j, (i - dz) % slabs * trans + (j - dx) % trans)
        for i in range(slabs)
        for j in range(trans)
    ]
    return lax.ppermute(value, AXES, pairs)


def total_sum(value, deep, trans, devices):
    count = devices // (2 * deep)
    copies = jnp.broadcast_to(value[None], (count, *value.shape))
    value = lax.all_to_all(copies, ("x", "y"), 0, 0, tiled=True).sum(0)
    core, near, middle, far = trans, 2 * trans, 4 * trans, 8 * trans
    rounds = [(middle, far ^ near, far ^ middle)] if deep == 8 else []
    rounds.append((core, near, core ^ near))
    for masks in rounds:
        one, two, three = (
            lax.ppermute(value, AXES, [(i, i ^ m) for i in range(devices)]) for m in masks
        )
        value = (value + one) + (two + three)
    return value


def per_device(slabs, deep, trans, start_block, material, pml_mask, eps_table):
    width, _, zs, xs, ny = start_block.shape
    classes = eps_table.shape[0]
    entries = float(3 * zs * xs * ny * slabs * trans)
    field = shape(zs, 3, xs, width, ny)
    rows = width * 3 * zs * xs
    halo = Halo(zs, xs)

    s0, diag, *messages = call(
        functools.partial(split_body, halo, width, classes),
        [field, shape(zs, xs, ny)] + [shape(halo.rows(n, width), ny) for n in halo.names[:4]],
        [eps_table, material, pml_mask, start_block.reshape(rows, ny)],
        hbm=(0, 1, 2, 3),
        scratch=[
            pltpu.VMEM((rows + 3 * zs * xs, ny), jnp.float32),
            pltpu.VMEM((zs, xs, ny), jnp.int32),
            pltpu.VMEM((zs, xs, ny), jnp.int32),
            pltpu.SMEM((classes,), jnp.float32),
            pltpu.SemaphoreType.DMA((3 + width // 8,)),
        ],
    )
    messages = [moved(n, m, slabs, trans) for n, m in zip(halo.names, messages)]
    passed = call(
        functools.partial(relay_body, halo, width),
        [shape(halo.rows(n, width), ny) for n in halo.names[4:]],
        messages[:2],
    )
    messages += [moved(n, m, slabs, trans) for n, m in zip(halo.names[4:], passed)]
    pairs = len(cell_pairs(zs, xs))
    gram, split = call(
        functools.partial(start_gram_body, zs, xs),
        [shape(width, width), jax.ShapeDtypeStruct((pairs, 3 * width, 2 * ny), jnp.bfloat16)],
        [s0],
    )
    outside = len(halo.first) - 3 * zs * xs
    basis, moments = call(
        functools.partial(apply_body, halo, width, ny, slabs, trans),
        [
            jax.ShapeDtypeStruct((len(cell_pairs(zs, xs)), 6 * width, 2 * ny), jnp.bfloat16),
            shape(40, 4 * width),
        ],
        [s0, diag, gram, split] + messages,
        scratch=[
            pltpu.VMEM(field.shape, jnp.float32),
            pltpu.VMEM(field.shape, jnp.float32),
            pltpu.VMEM((outside, 8, ny), jnp.float32),
        ],
    )
    moments = total_sum(moments, deep, trans, slabs * trans)
    blocks, couplings = call(
        functools.partial(last_body, zs, xs, width, ny, classes, entries),
        [shape(2, width, 3 * zs, xs, ny), shape(2, 2, width, width)],
        [eps_table, moments, basis],
        smem=(0,),
        hbm_out=(0,),
        scratch=[
            pltpu.VMEM((2, width + 1, 3 * zs, xs, ny), jnp.float32),
            pltpu.SemaphoreType.DMA((2, 3 * zs)),
        ],
    )
    return blocks.reshape(2, width, 3, zs, xs, ny), couplings


def solution(mesh):
    slabs, trans = mesh.devices.shape
    deep = 8 if slabs == 64 else 2
    sizes = (slabs // (2 * deep), deep, 2, trans)
    split = jax.sharding.Mesh(mesh.devices.reshape(sizes), AXES)
    slab = AXES[:3]
    return jax.shard_map(
        functools.partial(per_device, slabs, deep, trans),
        mesh=split,
        in_specs=(
            P(None, None, slab, "x", None),
            P(slab, "x", None),
            P(slab, "x", None),
            P(),
        ),
        out_specs=(P(None, None, None, slab, "x", None), P()),
        check_vma=False,
    )
```
